128 devices in a mesh: dp: 4 (over x), ex: 8 (over z, core), ey: 4 (over y).
Axes of the slice: x: 4, y: 4, z: 4, core: 2. Of those that a mesh axis runs over, the one named last changes fastest.
Arguments:
- tokens: bfloat16 [16384, 2048], P(('dp', 'ex', 'ey')), may hold values from -6 to 6
- out_grad: bfloat16 [16384, 2048], P(('dp', 'ex', 'ey')), may hold values from -0.59765625 to 0.59765625
- router_logits: float32 [16384, 128], P(('dp', 'ex', 'ey')), may hold values from -16 to 306
- expert_picks: int32 [16384, 8], P(('dp', 'ex', 'ey')), may hold values from 0 to 127, all different within a row; in each aligned block of 128 rows (0 to 127, 128 to 255, ...) at most 9 rows name the same one
- micro_batch: int32 [16384], P(('dp', 'ex', 'ey')), may hold values from 0 to 1
- w_gate: bfloat16 [128, 2048, 768], P(('dp', 'ex', 'ey'))
- w_up: bfloat16 [128, 2048, 768], P(('dp', 'ex', 'ey'))
- w_down: bfloat16 [128, 768, 2048], P(('dp', 'ex', 'ey'))
Outputs:
- grad_tokens: bfloat16 [16384, 2048], P(('dp', 'ex', 'ey'))
- grad_logits: float32 [16384, 128], P(('dp', 'ex', 'ey'))
- balance_grad: float32 [16384, 128], P(('dp', 'ex', 'ey'))
- grad_gate: bfloat16 [128, 2048, 768], P(('dp', 'ex', 'ey'))
- grad_up: bfloat16 [128, 2048, 768], P(('dp', 'ex', 'ey'))
- grad_down: bfloat16 [128, 768, 2048], P(('dp', 'ex', 'ey'))
The draws below stay inside these ranges and needn't reach their ends.
Inputs may be any that keep to these rules, and one draw needn't show every extreme that they name: `expert_picks`: each token names 8 different experts; among the tokens of one device no expert is named more than 9 times, and some expert of some device is named exactly 9 times.
All inputs are finite; a program needn't handle non-finite values.
Results may differ from the reference program's by a relative error of at most 0.02.
Values may be sent and summed in bfloat16 or wider, within the bound.
A program may use at most 128 MiB of HBM per device.

```python
import math
import jax
import jax.numpy as jnp
import numpy as np
from jax import lax

D = 2048
H = 768
K = 8
MICRO = 2
TOK_DEV = 128
EXPERTS = 128
TOKENS = 16384
CAP = 9
N_DP = 4
N_EX = 8
N_EY = 4


def draw_router_logits(key, part):
    key = jax.random.fold_in(key, 5)
    normal_key = jax.random.fold_in(key, 0)
    return 0.7 * jax.random.normal(normal_key, (TOKENS, EXPERTS), jnp.float32)


def draw_micro_batch(key, part):
    key = jax.random.fold_in(key, 11)
    position = jnp.arange(TOKENS, dtype=jnp.int32)
    threshold = TOKENS // 5 + 3 * position // 5
    uniform_draw = jax.random.randint(key, (TOKENS,), 0, TOKENS)
    return (uniform_draw < threshold).astype(jnp.int32)


def draw_w_gate(key, part):
    key = jax.random.fold_in(key, 21)
    values = jnp.clip(jax.random.normal(key, (EXPERTS, D, H), jnp.float32), -6.0, 6.0)
    return (values * D ** (-0.5)).astype(jnp.bfloat16)


def draw_w_up(key, part):
    key = jax.random.fold_in(key, 23)
    values = jnp.clip(jax.random.normal(key, (EXPERTS, D, H), jnp.float32), -6.0, 6.0)
    return (values * D ** (-0.5)).astype(jnp.bfloat16)


def draw_w_down(key, part):
    key = jax.random.fold_in(key, 29)
    values = jnp.clip(jax.random.normal(key, (EXPERTS, H, D), jnp.float32), -6.0, 6.0)
    return (values * H ** (-0.5)).astype(jnp.bfloat16)


def levels(rng, extent, cuts, low, largest):
    factor_of, own = 1.0, jax.random.fold_in(rng, 6)
    for dim, parts in cuts:
        heights = jnp.exp(jax.random.uniform(jax.random.fold_in(own, dim), (parts,), jnp.float32, low / len(cuts), largest / len(cuts)))
        factor_of = factor_of * jnp.repeat(heights, extent[dim] // parts).reshape([-1 if axis == dim else 1 for axis in range(len(extent))])
    return factor_of


def deal_out(stream_key, own, number, rows, count, top, limit, lean):
    order = jax.random.permutation(stream_key, count)
    packed, usual = portions_of(count, rows * top, limit, lean, True), portions_of(count, rows * top, limit, lean, False)
    places = jnp.arange(count)

    def named(tallies, offset_by):
        used = int((tallies > 0).sum())
        fixed = max(1, used // 4)
        shifted = fixed + (places - fixed + offset_by * (used - fixed)) % max(1, count - fixed)
        return jnp.zeros((count,), jnp.int32).at[order[jnp.where(places < fixed, places, shifted)]].set(jnp.asarray(tallies, jnp.int32))

    tallies = jnp.where(number % 4 == 0, named(packed, number // 4), named(usual, number - number // 4 - 1))
    mixed = jax.random.permutation(jax.random.fold_in(own, 3), count)
    source_of, taker = mixed[0:count // 2 * 2:2], mixed[1:count // 2 * 2:2]
    slack = jnp.minimum(tallies[source_of] - 1, limit - tallies[taker]) // 2
    slack = jnp.where((source_of == order[0]) | (taker == order[0]) | (tallies[taker] == 0), 0, jnp.maximum(slack, 0))
    shifted = jax.random.randint(jax.random.fold_in(own, 4), (count // 2,), 0, 1 << 20) % (slack + 1)
    tallies = tallies.at[source_of].add(-shifted).at[taker].add(shifted)
    labels = jnp.searchsorted(jnp.cumsum(tallies), jnp.arange(rows * top), side="right").astype(jnp.int32)
    grid = labels.reshape(top, rows).T
    grid = grid[jax.random.permutation(jax.random.fold_in(own, 1), rows)]
    offset_by = jax.random.randint(jax.random.fold_in(own, 2), (rows, 1), 0, top)
    return jnp.take_along_axis(grid, (jnp.arange(top)[None, :] + offset_by) % top, axis=1)


def portions_of(amount, total, limit, lean, full):
    portions = [(1 << 20) // math.isqrt(grade ** lean) + 1 for grade in range(1, amount + 1)]
    largest = limit if full else min(limit, max(-(-total // amount), total * portions[0] // sum(portions)))
    least = 1 if total - largest >= amount - 1 else 0
    given, surplus = [largest] + [least] * (amount - 1), total - largest - least * (amount - 1)
    while surplus > 0:
        movable = [i for i in range(1, amount) if given[i] < largest] or [i for i in range(1, amount) if given[i] < limit]
        pool, budget = sum([portions[i] for i in movable]), surplus
        for i in movable:
            extra = min(limit - given[i], max(1, budget * portions[i] // pool), surplus)
            given[i] = given[i] + extra
            surplus = surplus - extra
    return np.array(given)


def gaussian(stream_key, dims, width, reach, cuts=(), kind=jnp.bfloat16):
    loudness = levels(stream_key, dims, cuts, -0.22, 0.18) if cuts else 1.0
    values = jax.random.normal(stream_key, dims, jnp.float32) * width * loudness
    return jnp.minimum(jnp.maximum(values, -reach), reach).astype(kind)


def setup_inputs(seed: int = 0) -> dict:
    keys = jax.random.split(jax.random.key(seed), 9)
    tokens = gaussian(keys[0], (TOKENS, D), 1.0, 6.0, ((0, 128),))
    out_grad = gaussian(keys[1], (TOKENS, D), 0.1, 0.59765625, ((0, 128),))
    router_logits = draw_router_logits(jax.random.fold_in(keys[8], 71), 0)
    expert_picks_keys = jax.random.split(jax.random.fold_in(keys[3], 1), TOKENS // TOK_DEV)
    expert_picks_turns = jax.random.permutation(jax.random.fold_in(keys[3], 3), TOKENS // TOK_DEV)
    expert_picks = jax.vmap(lambda own, number: deal_out(jax.random.fold_in(keys[3], 2), own, number, TOK_DEV, EXPERTS, K, CAP, 4))(expert_picks_keys, expert_picks_turns).reshape((TOKENS, K))
    micro_batch = draw_micro_batch(jax.random.fold_in(keys[8], 71), 0)
    w_gate = draw_w_gate(jax.random.fold_in(keys[8], 71), 0)
    w_up = draw_w_up(jax.random.fold_in(keys[8], 71), 0)
    w_down = draw_w_down(jax.random.fold_in(keys[8], 71), 0)
    return {"tokens": tokens, "out_grad": out_grad, "router_logits": router_logits, "expert_picks": expert_picks, "micro_batch": micro_batch, "w_gate": w_gate, "w_up": w_up, "w_down": w_down}


contract_rows = (((0,), (0,)), ((), ()))
contract_cols = (((1,), (1,)), ((), ()))


def silu_parts(pre_gate):
    logistic = jax.nn.sigmoid(pre_gate)
    return pre_gate * logistic, logistic * (1.0 + pre_gate * (1.0 - logistic))


def expert_backward(token_rows, cotangent_rows, weight_rows, gate_matrix, up_matrix, down_matrix):
    pre_gate = jnp.dot(token_rows, gate_matrix, preferred_element_type=jnp.float32)
    pre_up = jnp.dot(token_rows, up_matrix, preferred_element_type=jnp.float32)
    activation, derivative = silu_parts(pre_gate)
    hidden = (activation * pre_up).astype(jnp.bfloat16)
    back_hidden = lax.dot_general(cotangent_rows, down_matrix, contract_cols, preferred_element_type=jnp.float32)
    scores = jnp.sum(hidden.astype(jnp.float32) * back_hidden, axis=1).astype(jnp.bfloat16)
    scaled_out = (weight_rows[:, None] * cotangent_rows.astype(jnp.float32)).astype(jnp.bfloat16)
    grad_down = lax.dot_general(hidden, scaled_out, contract_rows, preferred_element_type=jnp.float32).astype(jnp.bfloat16)
    hidden_grad = weight_rows[:, None] * back_hidden
    gate_grad = (hidden_grad * pre_up * derivative).astype(jnp.bfloat16)
    up_grad = (hidden_grad * activation).astype(jnp.bfloat16)
    grad_gate = lax.dot_general(token_rows, gate_grad, contract_rows, preferred_element_type=jnp.float32).astype(jnp.bfloat16)
    grad_up = lax.dot_general(token_rows, up_grad, contract_rows, preferred_element_type=jnp.float32).astype(jnp.bfloat16)
    pair_grad = lax.dot_general(gate_grad, gate_matrix, contract_cols, preferred_element_type=jnp.float32)
    pair_grad = pair_grad + lax.dot_general(up_grad, up_matrix, contract_cols, preferred_element_type=jnp.float32)
    return pair_grad.astype(jnp.bfloat16), scores, grad_gate, grad_up, grad_down


def reference(tokens, out_grad, router_logits, expert_picks, micro_batch, w_gate, w_up, w_down):
    device_count = N_DP * N_EX * N_EY
    pair_rows = TOK_DEV * K
    expert_ids = jnp.arange(EXPERTS, dtype=jnp.int32)
    row_top = jnp.max(router_logits, axis=1, keepdims=True)
    exponent = jnp.exp(router_logits - row_top)
    probabilities = exponent / jnp.sum(exponent, axis=1, keepdims=True)
    picked = jnp.take_along_axis(router_logits, expert_picks, axis=1)
    picked_exp = jnp.exp(picked - jnp.max(picked, axis=1, keepdims=True))
    route_weight = picked_exp / jnp.sum(picked_exp, axis=1, keepdims=True)
    sent_weight = route_weight.astype(jnp.bfloat16).reshape(TOKENS * K)
    flat_picks = expert_picks.reshape(device_count, pair_rows)
    flat_hot = (flat_picks[:, :, None] == expert_ids).astype(jnp.int32)
    slot_rank = jnp.sum((jnp.cumsum(flat_hot, axis=1) - 1) * flat_hot, axis=2).astype(jnp.int32)
    source_ids = jnp.broadcast_to(jnp.arange(device_count, dtype=jnp.int32)[:, None], flat_picks.shape)
    pair_index = jnp.arange(TOKENS * K, dtype=jnp.int32).reshape(device_count, pair_rows)
    slot_table = jnp.full((EXPERTS, device_count, CAP), -1, jnp.int32)
    slot_table = slot_table.at[flat_picks, source_ids, slot_rank].set(pair_index)
    slot_table = slot_table.reshape(EXPERTS, device_count * CAP)

    def one_expert(operands):
        slot_pairs, gate_matrix, up_matrix, down_matrix = operands
        occupied = slot_pairs >= 0
        safe_pair = jnp.where(occupied, slot_pairs, 0).astype(jnp.int32)
        token_index = (safe_pair // K).astype(jnp.int32)
        token_rows = jnp.where(occupied[:, None], tokens[token_index], 0).astype(jnp.bfloat16)
        cotangent_rows = jnp.where(occupied[:, None], out_grad[token_index], 0).astype(jnp.bfloat16)
        weight_rows = jnp.where(occupied, sent_weight[safe_pair], 0).astype(jnp.bfloat16).astype(jnp.float32)
        return expert_backward(token_rows, cotangent_rows, weight_rows, gate_matrix, up_matrix, down_matrix)

    pair_grads, scores, grad_gate, grad_up, grad_down = lax.map(one_expert, (slot_table, w_gate, w_up, w_down))
    position = (source_ids * CAP + slot_rank).astype(jnp.int32)
    gathered = pair_grads[flat_picks, position]
    grad_tokens = jnp.sum(gathered.reshape(TOKENS, K, D).astype(jnp.float32), axis=1).astype(jnp.bfloat16)
    pair_scores = scores[flat_picks, position].reshape(TOKENS, K).astype(jnp.float32)
    mean_score = jnp.sum(route_weight * pair_scores, axis=1, keepdims=True)
    route_grad = route_weight * (pair_scores - mean_score)
    pick_match = expert_picks[:, :, None] == expert_ids
    grad_logits = jnp.sum(jnp.where(pick_match, route_grad[:, :, None], 0.0), axis=1)
    pick_hot = jnp.sum(pick_match.astype(jnp.float32), axis=1)
    batch_hot = (micro_batch[:, None] == jnp.arange(MICRO, dtype=jnp.int32)).astype(jnp.float32)
    occupancy = jnp.dot(batch_hot.T, pick_hot, precision=lax.Precision.HIGHEST)
    load = occupancy * (EXPERTS * MICRO / (K * TOKENS))
    token_load = jnp.sum(batch_hot[:, :, None] * load[None, :, :], axis=1)
    mean_load = jnp.sum(probabilities * token_load, axis=1, keepdims=True)
    balance_grad = probabilities * (token_load - mean_load)
    return grad_tokens, grad_logits, balance_grad, grad_gate, grad_up, grad_down
```

```python
import functools

import jax
import jax.numpy as jnp
from jax import lax
from jax.experimental import pallas as pl
from jax.experimental.pallas import tpu as pltpu
from jax.sharding import PartitionSpec as P

MESH = pl.DeviceIdType.MESH
F32, BF16, I32 = jnp.float32, jnp.bfloat16, jnp.int32
NN = (((1,), (0,)), ((), ()))
NT = (((1,), (1,)), ((), ()))
TN = (((0,), (0,)), ((), ()))

D, H, K, T, E, CAP, MICRO = 2048, 768, 8, 128, 128, 9, 2
CH = D // 128
MSG = CAP * CH
GROUPS = 4
PER = E // GROUPS
ROWS = PER * CAP
PAIRS = E * CAP
BLK = 32


def mm(a, b, dims):
    return lax.dot_general(a, b, dims, preferred_element_type=F32)


def offset(i):
    a, b, c, d = i % 4, (i // 4) % 4, (i // 16) % 4, i // 64
    dx, dy, dz = a, (a + b) % 4, (a + b + c) % 4
    return dx, dz, (a + b + c + d) % 2, dy


def shifted(i, sign):
    x, ex, y = lax.axis_index("dp"), lax.axis_index("ex"), lax.axis_index("ey")
    dx, dz, dc, dy = offset(i)
    return (
        (x + sign * dx + 4) % 4,
        (ex // 2 + sign * dz + 4) % 4 * 2 + (ex % 2 + dc) % 2,
        (y + sign * dy + 4) % 4,
    )


def rows_of(g, size):
    return pl.ds(pl.multiple_of(g * size, size), size)


def iota(shape, dim):
    return lax.broadcasted_iota(I32, shape, dim)


def kernel(
    tok_ref, cot_ref, logit_ref, pick_ref, mb_ref, wg_hbm, wu_hbm, wd_hbm,
    gt_ref, gl_ref, gb_ref, gg_hbm, gu_hbm, gd_hbm,
    sx, sc, rx, rc, ps, pr, xs, cs, hid, gu, wg, wu, wd, pg, hot, whot, code_rel, perm_ref, rwm_ref, prob_ref,
    qs, qr, acc, cnt, cnt_in, out_a, out_d,
    w_sem, sx_sem, sc_sem, rx_sem, rc_sem, ps_sem, pr_sem, qs_sem, qr_sem, cs_sem, cr_sem, oa_sem, od_sem,
):
    x, ex, y = lax.axis_index("dp"), lax.axis_index("ex"), lax.axis_index("ey")
    barrier = pltpu.get_barrier_semaphore()

    def greet(i, carry):
        pl.semaphore_signal(barrier, inc=1, device_id=shifted(i, 1), device_id_type=MESH)
        return carry

    lax.fori_loop(1, E, greet, 0)
    loads = [
        pltpu.make_async_copy(src, dst, w_sem.at[n])
        for n, (src, dst) in enumerate(((wg_hbm, wg), (wu_hbm, wu), (wd_hbm, wd)))
    ]
    for load in loads:
        load.start()

    expert_lane = iota((T, E), 1)
    picked = jnp.zeros((T, E), F32)
    for k in range(K):
        picked = jnp.where(pick_ref[:, k : k + 1] == expert_lane, 1.0, picked)
    logits = logit_ref[...]
    prob = jnp.exp(logits - jnp.max(logits, axis=1, keepdims=True))
    prob_ref[...] = prob / jnp.sum(prob, axis=1, keepdims=True)
    top = jnp.max(jnp.where(picked > 0.0, logits, -jnp.inf), axis=1, keepdims=True)
    rwm = jnp.where(picked > 0.0, jnp.exp(jnp.minimum(logits - top, 0.0)), 0.0)
    rwm = rwm / jnp.sum(rwm, axis=1, keepdims=True)
    rwm_ref[...] = rwm
    earlier = (iota((T, T), 1) < iota((T, T), 0)).astype(BF16)
    slot = mm(earlier, picked.astype(BF16), NN)
    code = jnp.where(picked > 0.0, slot, -1.0).astype(BF16)
    i_row = iota((E, E), 0)
    a, b, c, d = i_row & 3, (i_row >> 2) & 3, (i_row >> 4) & 3, i_row >> 6
    target = (
        ((x + a) & 3) * 32
        + (((ex // 2 + a + b + c) & 3) * 2 + ((ex % 2 + a + b + c + d) & 1)) * 4
        + ((y + a + b) & 3)
    )
    perm = (target == expert_lane).astype(BF16)
    perm_ref[...] = perm
    code_rel[...] = mm(perm, code, NT)
    w_rel = mm(perm, rwm.astype(BF16), NT).astype(BF16)
    mb_hot = (mb_ref[...] == iota((8, T), 0)).astype(BF16)
    cnt[0:8, :] = mm(mb_hot, picked.astype(BF16), NN)

    spread = (iota((ROWS, PER), 0) // CAP == iota((ROWS, PER), 1)).astype(BF16)
    slot_row = (iota((ROWS, T), 0) % CAP).astype(F32)
    for g in range(GROUPS):
        is_it = mm(spread, code_rel[g * PER : (g + 1) * PER, :].astype(BF16), NN) == slot_row
        weight = mm(spread, w_rel[g * PER : (g + 1) * PER, :], NN)
        hot[g * ROWS : (g + 1) * ROWS, :] = jnp.where(is_it, 1.0, 0.0).astype(BF16)
        whot[g * ROWS : (g + 1) * ROWS, :] = jnp.where(is_it, weight, 0.0).astype(BF16)

    def gather_rows(one_hot, table, out, g):
        pg[...] = mm(one_hot[rows_of(g, ROWS), :], table[...], NN).astype(BF16)
        pack(out, g)

    def pack(out, g):
        def block(n, carry):
            tile = pg[rows_of(n, BLK), :].reshape(BLK, CH, 128)
            out[rows_of(g * (ROWS // BLK) + n, BLK * CH), :] = tile.reshape(BLK * CH, 128)
            return carry

        lax.fori_loop(0, ROWS // BLK, block, 0)

    def unpack(src, g, out, out_g):
        def block(n, carry):
            tile = src[rows_of(g * (ROWS // BLK) + n, BLK * CH), :].reshape(BLK, CH, 128)
            out[rows_of(out_g * (ROWS // BLK) + n, BLK), :] = tile.reshape(BLK, D)
            return carry

        lax.fori_loop(0, ROWS // BLK, block, 0)

    def dispatch(g, carry):
        gather_rows(hot, tok_ref, sx, g)
        gather_rows(whot, cot_ref, sc, g)

        @pl.when(g == 0)
        def _():
            pl.semaphore_wait(barrier, E - 1)
            rx[0:MSG, :] = sx[0:MSG, :]
            rc[0:MSG, :] = sc[0:MSG, :]

        def send(i, carry):
            for src, dst, s_sem, r_sem in ((sx, rx, sx_sem, rx_sem), (sc, rc, sc_sem, rc_sem)):
                pltpu.make_async_remote_copy(
                    src_ref=src.at[rows_of(i, MSG)],
                    dst_ref=dst.at[rows_of(i, MSG)],
                    send_sem=s_sem,
                    recv_sem=r_sem.at[g],
                    device_id=shifted(i, 1),
                    device_id_type=MESH,
                ).start()
            return carry

        lax.fori_loop(jnp.where(g == 0, 1, g * PER), (g + 1) * PER, send, 0)
        return carry

    lax.fori_loop(0, GROUPS, dispatch, 0)

    def count_round(base, others, stage):
        copies = []
        for n in range(others):
            step = n + 1
            if stage == 0:
                to = ((x + step) % 4, ex, y)
            elif stage == 1:
                to = (x, ex, (y + step) % 4)
            else:
                to = (x, (ex + step) % 8, y)
            copies.append(
                pltpu.make_async_remote_copy(
                    src_ref=cnt.at[pl.ds(stage * 8, 8)],
                    dst_ref=cnt_in.at[pl.ds((base + n) * 8, 8)],
                    send_sem=cs_sem.at[base + n],
                    recv_sem=cr_sem.at[base + n],
                    device_id=to,
                    device_id_type=MESH,
                )
            )
        for copy in copies:
            copy.start()
        return copies

    def count_sum(copies, base, stage):
        total = cnt[stage * 8 : stage * 8 + 8, :]
        for n, copy in enumerate(copies):
            copy.wait()
            total = total + cnt_in[(base + n) * 8 : (base + n) * 8 + 8, :]
        cnt[stage * 8 + 8 : stage * 8 + 16, :] = total

    copies = count_round(0, 3, 0)
    count_sum(copies, 0, 0)
    copies = count_round(3, 3, 1)
    count_sum(copies, 3, 1)
    copies = count_round(6, 7, 2)
    for load in loads:
        load.wait()

    collect = (iota((PER, ROWS), 1) // CAP == iota((PER, ROWS), 0)).astype(BF16)
    slot_lane = (iota((ROWS, 128), 0) % CAP == iota((ROWS, 128), 1)).astype(F32)

    def expert(g, carry):
        part = rows_of(g, ROWS)

        def arrived(buf, sem):
            @pl.when(g == 0)
            def _():
                piece = buf.at[pl.ds(MSG, (PER - 1) * MSG)]
                pltpu.make_async_copy(piece, piece, sem.at[0]).wait()

            @pl.when(g > 0)
            def _():
                piece = buf.at[rows_of(g, PER * MSG)]
                pltpu.make_async_copy(piece, piece, sem.at[g]).wait()

        arrived(rx, rx_sem)
        unpack(rx, g, xs, g)
        arrived(rc, rc_sem)
        unpack(rc, g, cs, g)
        score = jnp.zeros((ROWS, 1), F32)
        for h in range(H // 256):
            cols = slice(h * 256, (h + 1) * 256)
            pre_gate = mm(xs[part, :], wg[:, cols], NN)
            pre_up = mm(xs[part, :], wu[:, cols], NN)
            back = mm(cs[part, :], wd[cols, :], NT)
            logistic = jax.nn.sigmoid(pre_gate)
            act = pre_gate * logistic
            deriv = logistic * (1.0 + pre_gate * (1.0 - logistic))
            hidden = (act * pre_up).astype(BF16)
            hid[part, cols] = hidden
            score = score + jnp.sum(hidden.astype(F32) * back, axis=1, keepdims=True)
            gu[part, cols] = (back * pre_up * deriv).astype(BF16)
            gu[part, h * 256 + H : (h + 1) * 256 + H] = (back * act).astype(BF16)
        score_rows = mm(collect, (score * slot_lane).astype(BF16), NN)
        for i in range(PER):
            qs[g * PER + i] = score_rows[i : i + 1, :]
        for n in range(4):
            cols = slice(n * 512, (n + 1) * 512)
            pair = mm(gu[part, 0:H], wg[cols, :], NT) + mm(gu[part, H : 2 * H], wu[cols, :], NT)
            pg[:, cols] = pair.astype(BF16)
        pack(ps, g)

        @pl.when(g == 0)
        def _():
            pr[0:MSG, :] = ps[0:MSG, :]
            qr[0] = qs[0]

        def send(i, carry):
            to = shifted(i, -1)
            pltpu.make_async_remote_copy(
                src_ref=ps.at[rows_of(i, MSG)],
                dst_ref=pr.at[rows_of(i, MSG)],
                send_sem=ps_sem,
                recv_sem=pr_sem.at[g],
                device_id=to,
                device_id_type=MESH,
            ).start()
            pltpu.make_async_remote_copy(
                src_ref=qs.at[pl.ds(i, 1)],
                dst_ref=qr.at[pl.ds(i, 1)],
                send_sem=qs_sem,
                recv_sem=qr_sem,
                device_id=to,
                device_id_type=MESH,
            ).start()
            return carry

        lax.fori_loop(jnp.where(g == 0, 1, g * PER), (g + 1) * PER, send, 0)
        return carry

    lax.fori_loop(0, GROUPS, expert, 0)

    def out_copies(n, slot):
        rows = rows_of(n, 256)
        return (
            pltpu.make_async_copy(out_a.at[slot, :, pl.ds(0, H)], gg_hbm.at[rows], oa_sem.at[slot, 0]),
            pltpu.make_async_copy(out_a.at[slot, :, pl.ds(H, H)], gu_hbm.at[rows], oa_sem.at[slot, 1]),
        )

    def grad_in(n, carry):
        slot = n % 2

        @pl.when(n >= 2)
        def _():
            for copy in out_copies(n - 2, slot):
                copy.wait()

        out_a[slot] = mm(xs[:, rows_of(n, 256)], gu[...], TN).astype(BF16)
        for copy in out_copies(n, slot):
            copy.start()
        return carry

    lax.fori_loop(0, D // 256, grad_in, 0)

    def down_copy(n, slot):
        return pltpu.make_async_copy(out_d.at[slot], gd_hbm.at[rows_of(n, 256)], od_sem.at[slot])

    def grad_out(n, carry):
        slot = n % 2

        @pl.when(n >= 2)
        def _():
            down_copy(n - 2, slot).wait()

        out_d[slot] = mm(hid[:, rows_of(n, 256)], cs[...], TN).astype(BF16)
        down_copy(n, slot).start()
        return carry

    lax.fori_loop(0, H // 256, grad_out, 0)

    count_sum(copies, 6, 2)
    load = cnt[24:32, :] * (E * MICRO / (K * T * E))
    batch_col = jnp.transpose((mb_ref[...] == iota((T, T), 0)).astype(F32))[:, 1:2]
    token_load = jnp.where(batch_col > 0.0, load[1:2, :], load[0:1, :])
    prob = prob_ref[...]
    gb_ref[...] = prob * (token_load - jnp.sum(prob * token_load, axis=1, keepdims=True))

    acc[...] = jnp.zeros_like(acc)

    def combine(g, carry):
        @pl.when(g == 0)
        def _():
            piece = pr.at[pl.ds(MSG, (PER - 1) * MSG)]
            pltpu.make_async_copy(piece, piece, pr_sem.at[0]).wait()

        @pl.when(g > 0)
        def _():
            piece = pr.at[rows_of(g, PER * MSG)]
            pltpu.make_async_copy(piece, piece, pr_sem.at[g]).wait()

        unpack(pr, g, pg, 0)
        acc[...] += mm(hot[rows_of(g, ROWS), :], pg[...], TN)
        return carry

    lax.fori_loop(0, GROUPS, combine, 0)
    gt_ref[...] = acc[...].astype(BF16)

    pltpu.make_async_copy(qr.at[pl.ds(1, E - 1)], qr.at[pl.ds(1, E - 1)], qr_sem).wait()
    q_all = jnp.concatenate([qr[i] for i in range(E)], axis=0)
    q_rel = jnp.zeros((E, T), F32)
    for s in range(CAP):
        q_rel = jnp.where(code_rel[...] == float(s), q_all[:, s : s + 1], q_rel)
    q = mm(q_rel.astype(BF16), perm_ref[...], TN)
    gl_ref[...] = q - rwm_ref[...] * jnp.sum(q, axis=1, keepdims=True)

    for n in (D // 256 - 2, D // 256 - 1):
        for copy in out_copies(n, n % 2):
            copy.wait()
    for n in (H // 256 - 2, H // 256 - 1):
        down_copy(n, n % 2).wait()
    for buf, sem in ((sx, sx_sem), (sc, sc_sem), (ps, ps_sem)):
        piece = buf.at[pl.ds(MSG, (E - 1) * MSG)]
        pltpu.make_async_copy(piece, piece, sem).wait()
    pltpu.make_async_copy(qs.at[pl.ds(1, E - 1)], qs.at[pl.ds(1, E - 1)], qs_sem).wait()


def per_device(tokens, out_grad, router_logits, expert_picks, micro_batch, w_gate, w_up, w_down):
    vmem, hbm = pl.BlockSpec(memory_space=pltpu.VMEM), pl.BlockSpec(memory_space=pl.ANY)
    dma = pltpu.SemaphoreType.DMA
    outs = pl.pallas_call(
        kernel,
        out_shape=(
            jax.ShapeDtypeStruct((T, D), BF16),
            jax.ShapeDtypeStruct((T, E), F32),
            jax.ShapeDtypeStruct((T, E), F32),
            jax.ShapeDtypeStruct((D, H), BF16),
            jax.ShapeDtypeStruct((D, H), BF16),
            jax.ShapeDtypeStruct((H, D), BF16),
        ),
        in_specs=[vmem] * 5 + [hbm] * 3,
        out_specs=(vmem,) * 3 + (hbm,) * 3,
        scratch_shapes=[
            *[pltpu.VMEM((E * MSG, 128), BF16)] * 6,
            *[pltpu.VMEM((PAIRS, D), BF16)] * 2,
            pltpu.VMEM((PAIRS, H), BF16),
            pltpu.VMEM((PAIRS, 2 * H), BF16),
            pltpu.VMEM((D, H), BF16),
            pltpu.VMEM((D, H), BF16),
            pltpu.VMEM((H, D), BF16),
            pltpu.VMEM((ROWS, D), BF16),
            pltpu.VMEM((PAIRS, T), BF16),
            pltpu.VMEM((PAIRS, T), BF16),
            pltpu.VMEM((E, T), F32),
            pltpu.VMEM((E, E), BF16),
            pltpu.VMEM((T, E), F32),
            pltpu.VMEM((T, E), F32),
            pltpu.VMEM((E, 1, 128), F32),
            pltpu.VMEM((E, 1, 128), F32),
            pltpu.VMEM((T, D), F32),
            pltpu.VMEM((32, E), F32),
            pltpu.VMEM((13 * 8, E), F32),
            pltpu.VMEM((2, 256, 2 * H), BF16),
            pltpu.VMEM((2, 256, D), BF16),
            dma((3,)), dma, dma, dma((GROUPS,)), dma((GROUPS,)), dma, dma((GROUPS,)), dma, dma,
            dma((13,)), dma((13,)), dma((2, 2)), dma((2,)),
        ],
        compiler_params=pltpu.CompilerParams(
            collective_id=0, has_side_effects=True, vmem_limit_bytes=64 * 2**20
        ),
        name="expert_backward",
    )(tokens, out_grad, router_logits, expert_picks, micro_batch.reshape(1, T), w_gate[0], w_up[0], w_down[0])
    grad_tokens, grad_logits, balance_grad, grad_gate, grad_up, grad_down = outs
    return grad_tokens, grad_logits, balance_grad, grad_gate[None], grad_up[None], grad_down[None]


def solution(mesh):
    rows, cube = P(("dp", "ex", "ey"), None), P(("dp", "ex", "ey"), None, None)
    return jax.shard_map(
        per_device,
        mesh=mesh,
        in_specs=(rows, rows, rows, rows, P(("dp", "ex", "ey")), cube, cube, cube),
        out_specs=(rows, rows, rows, cube, cube, cube),
        check_vma=False,
    )
```

```python
import jax
import jax.numpy as jnp
from jax import lax
from jax.experimental import pallas as pl
from jax.experimental.pallas import tpu as pltpu
from jax.sharding import PartitionSpec as P

MESH = pl.DeviceIdType.MESH
F32, BF16, I32 = jnp.float32, jnp.bfloat16, jnp.int32
NN = (((1,), (0,)), ((), ()))
NT = (((1,), (1,)), ((), ()))
TN = (((0,), (0,)), ((), ()))

D, H, K, T, E, CAP, MICRO = 2048, 768, 8, 128, 128, 9, 2
AXES = 3
LINE = 4
PLANE = E // LINE
GROUPS = 2
PER = PLANE // GROUPS
MSG = LINE * CAP
ROWS = PER * MSG
PAIRS = E * CAP
HALF = ROWS // 2
SHEET = LINE * MSG
BLK = 32
Q_TOK, Q_COT, Q_PAIR = (4, 4, 8), (4, 8, 4), (8, 4, 4)


def slices(chunks):
    starts = [sum(chunks[:a]) * 128 for a in range(AXES)]
    return [slice(s, s + q * 128) for s, q in zip(starts, chunks)]


COLS_TOK, COLS_COT, COLS_PAIR = slices(Q_TOK), slices(Q_COT), slices(Q_PAIR)
PAIR_HOME = (2, 1, 0)


def mm(a, b, dims):
    return lax.dot_general(a, b, dims, preferred_element_type=F32)


def rows_of(g, size):
    return pl.ds(pl.multiple_of(g * size, size), size)


def iota(shape, dim):
    return lax.broadcasted_iota(I32, shape, dim)


def moved(dx, dy, dz, dc, sign=1):
    x, ex, y = lax.axis_index("dp"), lax.axis_index("ex"), lax.axis_index("ey")
    return (
        (x + sign * dx + 4) % 4,
        (ex // 2 + sign * dz + 4) % 4 * 2 + (ex % 2 + dc) % 2,
        (y + sign * dy + 4) % 4,
    )


def along(axis, step, sign=1):
    return moved(*(step if axis == n else 0 for n in range(AXES)), 0, sign)


def in_plane(axis, j, sign=1):
    core, high, low = j // 16, (j // 4) % 4, j % 4
    place = ((0, low, high), (low, 0, high), (low, high, 0))[axis]
    return moved(*place, core, sign)


def any_offset(i, sign=1):
    return moved(i % 4, (i // 4) % 4, (i // 16) % 4, i // 64, sign)


def turn(n):
    return (n % 4 + n // 4) % 4 * 4 + n % 4


def expert_at(dx, dy, dz, dc):
    x, ex, y = lax.axis_index("dp"), lax.axis_index("ex"), lax.axis_index("ey")
    return ((x + dx) & 3) * 32 + ((((ex // 2) + dz) & 3) * 2 + (((ex % 2) + dc) & 1)) * 4 + ((y + dy) & 3)


def kernel(
    tok_hbm, cot_hbm, logit_ref, pick_ref, mb_ref, wg_hbm, wu_hbm, wd_hbm,
    gt_ref, gl_ref, gb_ref, gg_hbm, gu_hbm, gd_hbm,
    st0, st1, st2, sc0, sc1, sc2, rt0, rt1, rt2, rc0, rc1, rc2, pr0, pr1, pr2,
    tt0, tt1, tt2, tc0, tc1, tc2, hot0, hot1, hot2, fr0, fr1, fr2, perm_y, perm_z,
    xs, cs, hid, gu, wg, wu, wd, pg, out_buf, cw, cwg, code_rel, perm_ref, rwm_ref, qs, qr, cnt, cnt_in,
    w_sem, own_sem, gt_s, gt_r, gc_s, gc_r, gw_s, gw_r, st_sem, sc_sem, rt_sem, rc_sem, ps_sem, pr_sem, fs_sem, fr_sem,
    qs_sem, qr_sem, cs_sem, cr_sem, oa_sem, od_sem,
):
    x, ex, y = lax.axis_index("dp"), lax.axis_index("ex"), lax.axis_index("ey")
    st, sc, rt, rc, pr = (st0, st1, st2), (sc0, sc1, sc2), (rt0, rt1, rt2), (rc0, rc1, rc2), (pr0, pr1, pr2)
    tt, tc, hot, fr = (tt0, tt1, tt2), (tc0, tc1, tc2), (hot0, hot1, hot2), (fr0, fr1, fr2)
    ps = tuple(st[n] for n in PAIR_HOME)
    fs = tuple(tt[n] for n in PAIR_HOME)
    barrier = pltpu.get_barrier_semaphore()

    def greet(i, carry):
        pl.semaphore_signal(barrier, inc=1, device_id=any_offset(i), device_id_type=MESH)
        return carry

    lax.fori_loop(1, E, greet, 0)
    loads = [
        pltpu.make_async_copy(src, dst, w_sem.at[n])
        for n, (src, dst) in enumerate(((wg_hbm, wg), (wu_hbm, wu), (wd_hbm, wd)))
    ]
    own = []
    for a in range(AXES):
        own.append(pltpu.make_async_copy(tok_hbm.at[:, COLS_TOK[a]], tt[a].at[pl.ds(0, T)], own_sem.at[0, a]))
        own.append(pltpu.make_async_copy(cot_hbm.at[:, COLS_COT[a]], tc[a].at[pl.ds(0, T)], own_sem.at[1, a]))
    for load in own + loads:
        load.start()

    def remote(src, dst, send_sem, recv_sem, to):
        pltpu.make_async_remote_copy(
            src_ref=src, dst_ref=dst, send_sem=send_sem, recv_sem=recv_sem, device_id=to, device_id_type=MESH
        ).start()

    def await_bytes(piece, sem):
        pltpu.make_async_copy(piece, piece, sem).wait()

    expert_row = iota((E, T), 0)
    picked_t = jnp.zeros((E, T), F32)
    for k in range(K):
        picked_t = jnp.where(pick_ref[k : k + 1, :] == expert_row, 1.0, picked_t)
    picked = jnp.transpose(picked_t)
    logits = logit_ref[...]
    top = jnp.max(jnp.where(picked > 0.0, logits, -jnp.inf), axis=1, keepdims=True)
    rwm = jnp.where(picked > 0.0, jnp.exp(jnp.minimum(logits - top, 0.0)), 0.0)
    rwm = rwm / jnp.sum(rwm, axis=1, keepdims=True)
    rwm_ref[...] = rwm
    weight = rwm.astype(BF16)
    earlier = (iota((T, T), 1) < iota((T, T), 0)).astype(BF16)
    code = jnp.where(picked > 0.0, mm(earlier, picked.astype(BF16), NN) + 1.0, 0.0).astype(BF16)
    row, lane = iota((E, E), 0), iota((E, E), 1)
    perm = (expert_at(row & 3, (row >> 2) & 3, (row >> 4) & 3, row >> 6) == lane).astype(BF16)
    perm_ref[...] = perm
    code_rel[...] = mm(perm, code, NT)
    step, core, high, low = row >> 5, (row >> 4) & 1, (row >> 2) & 3, row & 3
    for a in range(AXES):
        place = ((step, low, high), (low, step, high), (low, high, step))[a]
        perm = (expert_at(*place, core) == lane).astype(BF16)
        code_a, weight_a = mm(perm, code, NT).astype(BF16), mm(perm, weight, NT).astype(BF16)
        for s in range(LINE):
            home = cw if s else cwg
            home[a, s * 64 : s * 64 + 32, :] = code_a[s * 32 : s * 32 + 32, :]
            home[a, s * 64 + 32 : s * 64 + 64, :] = weight_a[s * 32 : s * 32 + 32, :]
    mb_hot = (mb_ref[...] == iota((8, T), 0)).astype(BF16)
    cnt[0:8, :] = mm(mb_hot, picked.astype(BF16), NN)
    pl.semaphore_wait(barrier, E - 1)

    for s in (1, 3, 2):
        for a in range(AXES):
            home = tt[a].at[pl.ds(s * T, T)]
            remote(tok_hbm.at[:, COLS_TOK[a]], home, gt_s.at[a], gt_r.at[a], along(a, s))
    for s in (1, 3, 2):
        for a in range(AXES):
            piece = pl.ds(s * 64, 64)
            remote(cw.at[a, piece], cwg.at[a, piece], gw_s.at[a], gw_r.at[a], along(a, s))
    for s in (1, 3, 2):
        for a in range(AXES):
            home = tc[a].at[pl.ds(s * T, T)]
            remote(cot_hbm.at[:, COLS_COT[a]], home, gc_s.at[a], gc_r.at[a], along(a, s))

    def count_round(base, others, stage):
        copies = []
        for n in range(others):
            to = (
                ((x + n + 1) % 4, ex, y),
                (x, ex, (y + n + 1) % 4),
                (x, (ex + n + 1) % 8, y),
            )[stage]
            copies.append(
                pltpu.make_async_remote_copy(
                    src_ref=cnt.at[pl.ds(stage * 8, 8)],
                    dst_ref=cnt_in.at[pl.ds((base + n) * 8, 8)],
                    send_sem=cs_sem.at[base + n],
                    recv_sem=cr_sem.at[base + n],
                    device_id=to,
                    device_id_type=MESH,
                )
            )
        for copy in copies:
            copy.start()
        return copies

    def count_sum(copies, base, stage):
        total = cnt[stage * 8 : stage * 8 + 8, :]
        for n, copy in enumerate(copies):
            copy.wait()
            total = total + cnt_in[(base + n) * 8 : (base + n) * 8 + 8, :]
        cnt[stage * 8 + 8 : stage * 8 + 16, :] = total

    copies = count_round(0, 3, 0)


    def order_block(n, carry):
        pair = iota((64, 1), 0) + n * 64
        s_, x_, y_, z_ = pair % CAP, pair // 9 % 4, pair // 36 % 4, pair // 144
        perm_z[rows_of(n, 64), :] = (((y_ * 4 + x_) * 4 + z_) * CAP + s_ == iota((64, ROWS), 1)).astype(BF16)
        return carry

    lax.fori_loop(0, ROWS // 64, order_block, 0)
    pair = iota((SHEET, 1), 0)
    perm_y[...] = ((pair // 9 % 4 * 4 + pair // 36) * CAP + pair % CAP == iota((SHEET, SHEET), 1)).astype(BF16)
    for load in own:
        load.wait()

    def pack(out, g, q):
        def block(n, carry):
            tile = pg[rows_of(n, BLK), 0 : q * 128].reshape(BLK, q, 128)
            out[rows_of(g * (ROWS // BLK) + n, BLK * q), :] = tile.reshape(BLK * q, 128)
            return carry

        lax.fori_loop(0, ROWS // BLK, block, 0)

    def unpack(src, g, q, out, out_g):
        def block(n, carry):
            tile = src[rows_of(g * (ROWS // BLK) + n, BLK * q), :].reshape(BLK, q, 128)
            out[rows_of(out_g * (ROWS // BLK) + n, BLK), 0 : q * 128] = tile.reshape(BLK, q * 128)
            return carry

        lax.fori_loop(0, ROWS // BLK, block, 0)

    def own_message(g, src, dst, q):
        @pl.when(g == 0)
        def _():
            dst[0 : MSG * q, :] = src[0 : MSG * q, :]

    def send_group(g, parts, sign):
        def send(n, carry):
            j = g * PER + turn(n)
            for a, (src, dst, s_sem, r_sem, q) in enumerate(parts):
                piece = rows_of(j, MSG * q)
                remote(src.at[piece], dst.at[piece], s_sem.at[g, a], r_sem.at[g, a], in_plane(a, j, sign))
            return carry

        lax.fori_loop(jnp.where(g == 0, 1, 0), PER, send, 0)

    def await_group(g, buf, sem, a, q):
        @pl.when(g == 0)
        def _():
            await_bytes(buf.at[pl.ds(MSG * q, (PER - 1) * MSG * q)], sem.at[0, a])

        @pl.when(g > 0)
        def _():
            await_bytes(buf.at[rows_of(g, ROWS * q)], sem.at[g, a])

    slot = (iota((ROWS, T), 0) % CAP + 1).astype(F32)

    def pick_rows(a, g, s):
        pair, j = iota((ROWS, PER), 0), iota((ROWS, PER), 1)
        return jnp.logical_and(pair // MSG == j, pair // CAP % LINE == s).astype(BF16)

    def fill(one_hot, table, q):
        def half(n, carry):
            for c in range(0, q, 4):
                lanes = slice(c * 128, (c + 4) * 128)
                pg[rows_of(n, HALF), lanes] = mm(one_hot(n), table[:, lanes], NN).astype(BF16)
            return carry

        lax.fori_loop(0, 2, half, 0)

    def dispatch(g, carry):
        part = rows_of(g, ROWS)
        for a in range(AXES):

            @pl.when(g == 0)
            def _():
                await_bytes(cwg.at[a, pl.ds(64, 192)], gw_r.at[a])

            for s in range(LINE):
                found = mm(pick_rows(a, g, s), cwg[a, pl.ds(s * 64 + g * PER, PER), :], NN)
                hot[a][part, s * T : (s + 1) * T] = (found == slot).astype(BF16)
        for a in range(AXES):

            @pl.when(g == 0)
            def _():
                await_bytes(tt[a].at[pl.ds(T, 3 * T)], gt_r.at[a])

            fill(lambda rows: hot[a][rows_of(2 * g + rows, HALF), :], tt[a], Q_TOK[a])
            pack(st[a], g, Q_TOK[a])
            own_message(g, st[a], rt[a], Q_TOK[a])
        send_group(g, [(st[a], rt[a], st_sem, rt_sem, Q_TOK[a]) for a in range(AXES)], 1)
        for a in range(AXES):
            for s in range(LINE):
                lanes = slice(s * T, (s + 1) * T)
                scale = mm(pick_rows(a, g, s), cwg[a, pl.ds(s * 64 + 32 + g * PER, PER), :], NN)
                xs[0:ROWS, lanes] = (hot[a][part, lanes].astype(F32) * scale).astype(BF16)

            @pl.when(g == 0)
            def _():
                await_bytes(tc[a].at[pl.ds(T, 3 * T)], gc_r.at[a])

            fill(lambda rows: xs[rows_of(rows, HALF), 0 : LINE * T], tc[a], Q_COT[a])
            pack(sc[a], g, Q_COT[a])
            own_message(g, sc[a], rc[a], Q_COT[a])
        send_group(g, [(sc[a], rc[a], sc_sem, rc_sem, Q_COT[a]) for a in range(AXES)], 1)
        return carry

    lax.fori_loop(0, GROUPS, dispatch, 0)
    count_sum(copies, 0, 0)
    copies = count_round(3, 3, 1)
    for load in loads:
        load.wait()

    def reorder(a, src, src_col, dst, dst_rows, dst_col, q, dims):
        for c in range(0, q * 128, 256):
            rows, lanes = src(slice(src_col + c, src_col + c + 256)), slice(dst_col + c, dst_col + c + 256)
            if a == 1:
                sheets = [rows[n * SHEET : (n + 1) * SHEET, :] for n in range(ROWS // SHEET)]
                rows = jnp.concatenate([mm(perm_y[...], sheet, dims).astype(BF16) for sheet in sheets], axis=0)
            elif a == 2:
                rows = mm(perm_z[...], rows, dims).astype(BF16)
            dst[dst_rows, lanes] = rows

    collect = (iota((2 * PER, HALF), 1) // CAP == iota((2 * PER, HALF), 0)).astype(BF16)
    slot_lane = (iota((HALF, 128), 0) % CAP == iota((HALF, 128), 1)).astype(F32)

    def expert(g, carry):
        part = rows_of(g, ROWS)
        for out, src, sem, chunks, cols in ((xs, rt, rt_sem, Q_TOK, COLS_TOK), (cs, rc, rc_sem, Q_COT, COLS_COT)):
            for a in range(AXES):
                await_group(g, src[a], sem, a, chunks[a])
                unpack(src[a], g, chunks[a], pg, 0)
                reorder(a, lambda lanes: pg[:, lanes], 0, out, part, cols[a].start, chunks[a], NN)

        def hidden_rows(n, carry):
            part = rows_of(2 * g + n, HALF)
            score = jnp.zeros((HALF, 1), F32)
            for h in range(H // 256):
                cols = slice(h * 256, (h + 1) * 256)
                pre_gate = mm(xs[part, :], wg[:, cols], NN)
                pre_up = mm(xs[part, :], wu[:, cols], NN)
                back = mm(cs[part, :], wd[cols, :], NT)
                logistic = jax.nn.sigmoid(pre_gate)
                act = pre_gate * logistic
                deriv = logistic * (1.0 + pre_gate * (1.0 - logistic))
                hidden = (act * pre_up).astype(BF16)
                hid[part, cols] = hidden
                score = score + jnp.sum(hidden.astype(F32) * back, axis=1, keepdims=True)
                gu[part, cols] = (back * pre_up * deriv).astype(BF16)
                gu[part, h * 256 + H : (h + 1) * 256 + H] = (back * act).astype(BF16)
            score_rows = mm(collect, (score * slot_lane).astype(BF16), NN)
            for i in range(2 * PER):
                qs[(2 * g + n) * 2 * PER + i] = score_rows[i : i + 1, :]
            return carry

        lax.fori_loop(0, 2, hidden_rows, 0)
        for a in range(AXES):
            q, first = Q_PAIR[a], COLS_PAIR[a].start

            def pair_cols(lanes):
                rows = mm(gu[part, 0:H], wg[lanes, :], NT) + mm(gu[part, H : 2 * H], wu[lanes, :], NT)
                return rows.astype(BF16)

            reorder(a, pair_cols, first, pg, slice(0, ROWS), 0, q, TN)
            await_group(g, st[PAIR_HOME[a]], st_sem, PAIR_HOME[a], q)
            pack(ps[a], g, q)
            own_message(g, ps[a], pr[a], q)
        send_group(g, [(ps[a], pr[a], ps_sem, pr_sem, Q_PAIR[a]) for a in range(AXES)], -1)
        @pl.when(g == 0)
        def _():
            qr[0] = qs[0]

        def send_score(i, carry):
            remote(qs.at[pl.ds(i, 1)], qr.at[pl.ds(i, 1)], qs_sem, qr_sem, any_offset(i, -1))
            return carry

        lax.fori_loop(jnp.where(g == 0, 1, g * 4 * PER), (g + 1) * 4 * PER, send_score, 0)
        return carry

    lax.fori_loop(0, GROUPS, expert, 0)
    count_sum(copies, 3, 1)
    copies = count_round(6, 7, 2)

    def in_copies(n, buf):
        rows = rows_of(n, 256)
        return (
            pltpu.make_async_copy(out_buf.at[buf, :, pl.ds(0, H)], gg_hbm.at[rows], oa_sem.at[buf, 0]),
            pltpu.make_async_copy(out_buf.at[buf, :, pl.ds(H, H)], gu_hbm.at[rows], oa_sem.at[buf, 1]),
        )

    def grad_in(n, carry):
        buf = n % 2

        @pl.when(n >= 2)
        def _():
            for copy in in_copies(n - 2, buf):
                copy.wait()

        turned = jnp.transpose(xs[:, rows_of(n, 256)])
        for part in (slice(0, H), slice(H, 2 * H)):
            out_buf[buf, :, part] = mm(turned, gu[:, part], NN).astype(BF16)
        for copy in in_copies(n, buf):
            copy.start()
        return carry

    lax.fori_loop(0, D // 256, grad_in, 0)
    for n in (D // 256 - 2, D // 256 - 1):
        for copy in in_copies(n, n % 2):
            copy.wait()

    for a in range(AXES):
        q = Q_PAIR[a]
        for g in range(GROUPS):
            await_group(g, pr[a], pr_sem, a, q)
            unpack(pr[a], g, q, xs, g)
        for c in range(0, q, 4):
            lanes = slice(c * 128, (c + 4) * 128)
            fs[a][:, lanes] = mm(hot[a][...], xs[:, lanes], TN).astype(BF16)
        for s in (1, 3, 2):
            piece = fr[a].at[pl.ds((s - 1) * T, T)]
            remote(fs[a].at[pl.ds(s * T, T)], piece, fs_sem.at[a], fr_sem.at[a], along(a, s, -1))

    def down_copy(n, buf):
        place = gd_hbm.at[rows_of(n // 2, 256), rows_of(n % 2, D // 2)]
        return pltpu.make_async_copy(out_buf.at[buf, :, pl.ds(0, D // 2)], place, od_sem.at[buf])

    def grad_out(n, carry):
        buf = n % 2

        @pl.when(n >= 2)
        def _():
            down_copy(n - 2, buf).wait()

        rows = mm(hid[:, rows_of(n // 2, 256)], cs[:, rows_of(n % 2, D // 2)], TN)
        out_buf[buf, :, 0 : D // 2] = rows.astype(BF16)
        down_copy(n, buf).start()
        return carry

    lax.fori_loop(0, H // 128, grad_out, 0)

    prob = jnp.exp(logit_ref[...] - jnp.max(logit_ref[...], axis=1, keepdims=True))
    prob = prob / jnp.sum(prob, axis=1, keepdims=True)
    count_sum(copies, 6, 2)
    load = cnt[24:32, :] * (E * MICRO / (K * T * E))
    batch_col = jnp.transpose((mb_ref[...] == iota((T, T), 0)).astype(F32))[:, 1:2]
    token_load = jnp.where(batch_col > 0.0, load[1:2, :], load[0:1, :])
    gb_ref[...] = prob * (token_load - jnp.sum(prob * token_load, axis=1, keepdims=True))

    await_bytes(qr.at[pl.ds(1, E - 1)], qr_sem)
    q_all = jnp.concatenate([qr[i] for i in range(E)], axis=0)
    q_rel = jnp.zeros((E, T), F32)
    for s in range(CAP):
        q_rel = jnp.where(code_rel[...] == float(s + 1), q_all[:, s : s + 1], q_rel)
    q_own = mm(q_rel.astype(BF16), perm_ref[...], TN)
    gl_ref[...] = q_own - rwm_ref[...] * jnp.sum(q_own, axis=1, keepdims=True)

    for a in range(AXES):
        await_bytes(fr[a], fr_sem.at[a])
        total = fs[a][0:T, :].astype(F32)
        for s in range(LINE - 1):
            total = total + fr[a][s * T : (s + 1) * T, :].astype(F32)
        gt_ref[:, COLS_PAIR[a]] = total.astype(BF16)

    for n in (H // 128 - 2, H // 128 - 1):
        down_copy(n, n % 2).wait()
    for a in range(AXES):
        await_bytes(tt[a].at[pl.ds(T, 3 * T)], gt_s.at[a])
        await_bytes(tc[a].at[pl.ds(T, 3 * T)], gc_s.at[a])
        await_bytes(cw.at[a, pl.ds(64, 192)], gw_s.at[a])
        await_bytes(fr[a], fs_sem.at[a])
        for g in range(GROUPS):
            await_group(g, sc[a], sc_sem, a, Q_COT[a])
            await_group(g, ps[a], ps_sem, a, Q_PAIR[a])
    await_bytes(qs.at[pl.ds(1, E - 1)], qs_sem)


def settle_kernel(*refs):
    sources, targets, sem, held = refs[:6], refs[6:12], refs[12], refs[13:]
    copies = []
    for src, dst, buf in zip(sources, targets, held):
        pieces = 8 if src.shape[0] > T else 1
        size = src.shape[0] // pieces
        for n in range(pieces):
            rows = pl.ds(n * size, size)
            m = len(copies)
            copies.append(
                (
                    pltpu.make_async_copy(src.at[rows], buf.at[rows], sem.at[0, m]),
                    pltpu.make_async_copy(buf.at[rows], dst.at[rows], sem.at[1, m]),
                )
            )
    for fetch, _ in copies:
        fetch.start()
    for fetch, store in copies:
        fetch.wait()
        store.start()
    for _, store in copies:
        store.wait()


def settle(outs):
    hbm = pl.BlockSpec(memory_space=pl.ANY)
    return pl.pallas_call(
        settle_kernel,
        out_shape=tuple(jax.ShapeDtypeStruct(o.shape, o.dtype) for o in outs),
        in_specs=[hbm] * 6,
        out_specs=(hbm,) * 6,
        scratch_shapes=[pltpu.SemaphoreType.DMA((2, 27))] + [pltpu.VMEM(o.shape, o.dtype) for o in outs],
        compiler_params=pltpu.CompilerParams(vmem_limit_bytes=60 * 2**20),
        name="settle",
    )(*outs)


def per_device(tokens, out_grad, router_logits, expert_picks, micro_batch, w_gate, w_up, w_down):
    vmem, hbm = pl.BlockSpec(memory_space=pltpu.VMEM), pl.BlockSpec(memory_space=pl.ANY)
    dma = pltpu.SemaphoreType.DMA

    def sliced(rows, chunks):
        return [pltpu.VMEM((rows * q, 128), BF16) for q in chunks]

    outs = pl.pallas_call(
        kernel,
        out_shape=(
            jax.ShapeDtypeStruct((T, D), BF16),
            jax.ShapeDtypeStruct((T, E), F32),
            jax.ShapeDtypeStruct((T, E), F32),
            jax.ShapeDtypeStruct((D, H), BF16),
            jax.ShapeDtypeStruct((D, H), BF16),
            jax.ShapeDtypeStruct((H, D), BF16),
        ),
        in_specs=[hbm] * 2 + [vmem] * 3 + [hbm] * 3,
        out_specs=(vmem,) * 3 + (hbm,) * 3,
        scratch_shapes=[
            *sliced(PAIRS, Q_TOK), *sliced(PAIRS, Q_COT),
            *sliced(PAIRS, Q_TOK), *sliced(PAIRS, Q_COT), *sliced(PAIRS, Q_PAIR),
            *[pltpu.VMEM((LINE * T, q * 128), BF16) for q in Q_TOK],
            *[pltpu.VMEM((LINE * T, q * 128), BF16) for q in Q_COT],
            *[pltpu.VMEM((PAIRS, LINE * T), BF16)] * AXES,
            *[pltpu.VMEM((3 * T, q * 128), BF16) for q in Q_PAIR],
            pltpu.VMEM((SHEET, SHEET), BF16), pltpu.VMEM((ROWS, ROWS), BF16),
            *[pltpu.VMEM((PAIRS, D), BF16)] * 2,
            pltpu.VMEM((PAIRS, H), BF16),
            pltpu.VMEM((PAIRS, 2 * H), BF16),
            pltpu.VMEM((D, H), BF16),
            pltpu.VMEM((D, H), BF16),
            pltpu.VMEM((H, D), BF16),
            pltpu.VMEM((ROWS, 1024), BF16),
            pltpu.VMEM((2, 256, 2 * H), BF16),
            pltpu.VMEM((AXES, 256, T), BF16),
            pltpu.VMEM((AXES, 256, T), BF16),
            pltpu.VMEM((E, T), F32),
            pltpu.VMEM((E, E), BF16),
            pltpu.VMEM((T, E), F32),
            pltpu.VMEM((E, 1, 128), F32),
            pltpu.VMEM((E, 1, 128), F32),
            pltpu.VMEM((32, E), F32),
            pltpu.VMEM((13 * 8, E), F32),
            dma((3,)),
            dma((2, AXES)),
            *[dma((AXES,))] * 6,
            *[dma((GROUPS, AXES))] * 6,
            *[dma((AXES,))] * 2,
            dma, dma, dma((13,)), dma((13,)), dma((2, 2)), dma((2,)),
        ],
        compiler_params=pltpu.CompilerParams(
            collective_id=0, has_side_effects=True, vmem_limit_bytes=64 * 2**20
        ),
        name="expert_backward",
    )(tokens, out_grad, router_logits, expert_picks.T, micro_batch.reshape(1, T), w_gate[0], w_up[0], w_down[0])
    grad_tokens, grad_logits, balance_grad, grad_gate, grad_up, grad_down = settle(outs)
    return grad_tokens, grad_logits, balance_grad, grad_gate[None], grad_up[None], grad_down[None]


def solution(mesh):
    rows, cube = P(("dp", "ex", "ey"), None), P(("dp", "ex", "ey"), None, None)
    return jax.shard_map(
        per_device,
        mesh=mesh,
        in_specs=(rows, rows, rows, rows, P(("dp", "ex", "ey")), cube, cube, cube),
        out_specs=(rows, rows, rows, cube, cube, cube),
        check_vma=False,
    )
```

```python
import jax
import jax.numpy as jnp
from jax import lax
from jax.experimental import pallas as pl
from jax.experimental.pallas import tpu as pltpu
from jax.sharding import PartitionSpec as P

MESH = pl.DeviceIdType.MESH
F32, BF16, I32 = jnp.float32, jnp.bfloat16, jnp.int32
NN = (((1,), (0,)), ((), ()))
NT = (((1,), (1,)), ((), ()))
TN = (((0,), (0,)), ((), ()))

D, H, K, T, E, CAP, MICRO = 2048, 768, 8, 128, 128, 9, 2
AXES = 3
LINE = 4
PLANE = E // LINE
GROUPS = 2
PER = PLANE // GROUPS
MSG = LINE * CAP
ROWS = PER * MSG
PAIRS = E * CAP
HALF = ROWS // 2
SHEET = LINE * MSG
BLK = 32
Q_TOK, Q_COT, Q_PAIR = (4, 4, 8), (4, 8, 4), (8, 4, 4)


def slices(chunks):
    starts = [sum(chunks[:a]) * 128 for a in range(AXES)]
    return [slice(s, s + q * 128) for s, q in zip(starts, chunks)]


COLS_TOK, COLS_COT, COLS_PAIR = slices(Q_TOK), slices(Q_COT), slices(Q_PAIR)
PAIR_HOME = (2, 1, 0)


def mm(a, b, dims):
    return lax.dot_general(a, b, dims, preferred_element_type=F32)


def rows_of(g, size):
    return pl.ds(pl.multiple_of(g * size, size), size)


def iota(shape, dim):
    return lax.broadcasted_iota(I32, shape, dim)


def moved(steps, dc, sign=1):
    x, ex, y = lax.axis_index("dp"), lax.axis_index("ex"), lax.axis_index("ey")
    side = ex % 2 if sign == 1 else (ex + dc) % 2
    dx, dy, dz = axes_of(steps, side)
    return (
        (x + sign * dx + 4) % 4,
        (ex // 2 + sign * dz + 4) % 4 * 2 + (ex % 2 + dc) % 2,
        (y + sign * dy + 4) % 4,
    )


def axes_of(steps, side):
    a, b, c = steps
    return a + side * (c - a), b + side * (a - b), c + side * (b - c)


def along(axis, step, sign=1):
    return moved([step if axis == n else 0 for n in range(AXES)], 0, sign)


def in_plane(axis, j, sign=1):
    core, high, low = j // 16, (j // 4) % 4, j % 4
    return moved(((0, low, high), (low, 0, high), (low, high, 0))[axis], core, sign)


def any_offset(i, sign=1):
    return moved((i % 4, (i // 4) % 4, (i // 16) % 4), i // 64, sign)


def turn(n):
    return (n % 4 + n // 4) % 4 * 4 + n % 4


def expert_at(steps, dc):
    x, ex, y = lax.axis_index("dp"), lax.axis_index("ex"), lax.axis_index("ey")
    dx, dy, dz = axes_of(steps, ex % 2)
    return ((x + dx) & 3) * 32 + ((((ex // 2) + dz) & 3) * 2 + (((ex % 2) + dc) & 1)) * 4 + ((y + dy) & 3)


def kernel(
    tok_hbm, cot_hbm, logit_ref, pick_ref, mb_ref, wg_hbm, wu_hbm, wd_hbm,
    gt_ref, gl_ref, gb_ref, gg_hbm, gu_hbm, gd_hbm,
    st0, st1, st2, sc0, sc1, sc2, rt0, rt1, rt2, rc0, rc1, rc2, pr0, pr1, pr2,
    tt0, tt1, tt2, tc0, tc1, tc2, hot0, hot1, hot2, fr0, fr1, fr2, perm_y, perm_z,
    xs, cs, hid, gu, wg, wu, wd, pg, out_buf, cw, cwg, code_rel, perm_ref, rwm_ref, qs, qr, cnt, cnt_in,
    w_sem, own_sem, gt_s, gt_r, gc_s, gc_r, gw_s, gw_r, st_sem, sc_sem, rt_sem, rc_sem, ps_sem, pr_sem, fs_sem, fr_sem,
    qs_sem, qr_sem, cs_sem, cr_sem, oa_sem, od_sem,
):
    x, ex, y = lax.axis_index("dp"), lax.axis_index("ex"), lax.axis_index("ey")
    st, sc, rt, rc, pr = (st0, st1, st2), (sc0, sc1, sc2), (rt0, rt1, rt2), (rc0, rc1, rc2), (pr0, pr1, pr2)
    tt, tc, hot, fr = (tt0, tt1, tt2), (tc0, tc1, tc2), (hot0, hot1, hot2), (fr0, fr1, fr2)
    ps = tuple(st[n] for n in PAIR_HOME)
    fs = tuple(tt[n] for n in PAIR_HOME)
    barrier = pltpu.get_barrier_semaphore()

    def greet(i, carry):
        pl.semaphore_signal(barrier, inc=1, device_id=any_offset(i), device_id_type=MESH)
        return carry

    lax.fori_loop(1, E, greet, 0)
    loads = [
        pltpu.make_async_copy(src, dst, w_sem.at[n])
        for n, (src, dst) in enumerate(((wg_hbm, wg), (wu_hbm, wu), (wd_hbm, wd)))
    ]
    own = []
    for a in range(AXES):
        own.append(pltpu.make_async_copy(tok_hbm.at[:, COLS_TOK[a]], tt[a].at[pl.ds(0, T)], own_sem.at[0, a]))
        own.append(pltpu.make_async_copy(cot_hbm.at[:, COLS_COT[a]], tc[a].at[pl.ds(0, T)], own_sem.at[1, a]))
    for load in own + loads:
        load.start()

    def remote(src, dst, send_sem, recv_sem, to):
        pltpu.make_async_remote_copy(
            src_ref=src, dst_ref=dst, send_sem=send_sem, recv_sem=recv_sem, device_id=to, device_id_type=MESH
        ).start()

    def await_bytes(piece, sem):
        pltpu.make_async_copy(piece, piece, sem).wait()

    pl.semaphore_wait(barrier, E - 1)
    for s in (1, 3, 2):
        for a in range(AXES):
            home = tt[a].at[pl.ds(s * T, T)]
            remote(tok_hbm.at[:, COLS_TOK[a]], home, gt_s.at[a], gt_r.at[a], along(a, s))

    expert_row = iota((E, T), 0)
    picked_t = jnp.zeros((E, T), F32)
    for k in range(K):
        picked_t = jnp.where(pick_ref[k : k + 1, :] == expert_row, 1.0, picked_t)
    picked = jnp.transpose(picked_t)
    logits = logit_ref[...]
    top = jnp.max(jnp.where(picked > 0.0, logits, -jnp.inf), axis=1, keepdims=True)
    rwm = jnp.where(picked > 0.0, jnp.exp(jnp.minimum(logits - top, 0.0)), 0.0)
    rwm = rwm / jnp.sum(rwm, axis=1, keepdims=True)
    rwm_ref[...] = rwm
    weight = rwm.astype(BF16)
    earlier = (iota((T, T), 1) < iota((T, T), 0)).astype(BF16)
    code = jnp.where(picked > 0.0, mm(earlier, picked.astype(BF16), NN) + 1.0, 0.0).astype(BF16)
    row, lane = iota((E, E), 0), iota((E, E), 1)
    perm = (expert_at((row & 3, (row >> 2) & 3, (row >> 4) & 3), row >> 6) == lane).astype(BF16)
    perm_ref[...] = perm
    code_rel[...] = mm(perm, code, NT)
    step, core, high, low = row >> 5, (row >> 4) & 1, (row >> 2) & 3, row & 3
    for a in range(AXES):
        place = ((step, low, high), (low, step, high), (low, high, step))[a]
        perm = (expert_at(place, core) == lane).astype(BF16)
        code_a, weight_a = mm(perm, code, NT).astype(BF16), mm(perm, weight, NT).astype(BF16)
        for s in range(LINE):
            home = cw if s else cwg
            home[a, s * 64 : s * 64 + 32, :] = code_a[s * 32 : s * 32 + 32, :]
            home[a, s * 64 + 32 : s * 64 + 64, :] = weight_a[s * 32 : s * 32 + 32, :]
    mb_hot = (mb_ref[...] == iota((8, T), 0)).astype(BF16)
    cnt[0:8, :] = mm(mb_hot, picked.astype(BF16), NN)
    for s in (1, 3, 2):
        for a in range(AXES):
            piece = pl.ds(s * 64, 64)
            remote(cw.at[a, piece], cwg.at[a, piece], gw_s.at[a], gw_r.at[a], along(a, s))
    for s in (1, 3, 2):
        for a in range(AXES):
            home = tc[a].at[pl.ds(s * T, T)]
            remote(cot_hbm.at[:, COLS_COT[a]], home, gc_s.at[a], gc_r.at[a], along(a, s))

    def count_round(base, others, stage):
        copies = []
        for n in range(others):
            to = (
                ((x + n + 1) % 4, ex, y),
                (x, ex, (y + n + 1) % 4),
                (x, (ex + n + 1) % 8, y),
            )[stage]
            copies.append(
                pltpu.make_async_remote_copy(
                    src_ref=cnt.at[pl.ds(stage * 8, 8)],
                    dst_ref=cnt_in.at[pl.ds((base + n) * 8, 8)],
                    send_sem=cs_sem.at[base + n],
                    recv_sem=cr_sem.at[base + n],
                    device_id=to,
                    device_id_type=MESH,
                )
            )
        for copy in copies:
            copy.start()
        return copies

    def count_sum(copies, base, stage):
        total = cnt[stage * 8 : stage * 8 + 8, :]
        for n, copy in enumerate(copies):
            copy.wait()
            total = total + cnt_in[(base + n) * 8 : (base + n) * 8 + 8, :]
        cnt[stage * 8 + 8 : stage * 8 + 16, :] = total

    copies = count_round(0, 3, 0)


    def order_block(n, carry):
        pair = iota((64, 1), 0) + n * 64
        s_, x_, y_, z_ = pair % CAP, pair // 9 % 4, pair // 36 % 4, pair // 144
        perm_z[rows_of(n, 64), :] = (((y_ * 4 + x_) * 4 + z_) * CAP + s_ == iota((64, ROWS), 1)).astype(BF16)
        return carry

    lax.fori_loop(0, ROWS // 64, order_block, 0)
    pair = iota((SHEET, 1), 0)
    perm_y[...] = ((pair // 9 % 4 * 4 + pair // 36) * CAP + pair % CAP == iota((SHEET, SHEET), 1)).astype(BF16)
    for load in own:
        load.wait()

    def pack(out, g, q):
        def block(n, carry):
            tile = pg[rows_of(n, BLK), 0 : q * 128].reshape(BLK, q, 128)
            out[rows_of(g * (ROWS // BLK) + n, BLK * q), :] = tile.reshape(BLK * q, 128)
            return carry

        lax.fori_loop(0, ROWS // BLK, block, 0)

    def unpack(src, g, q, out, out_g):
        def block(n, carry):
            tile = src[rows_of(g * (ROWS // BLK) + n, BLK * q), :].reshape(BLK, q, 128)
            out[rows_of(out_g * (ROWS // BLK) + n, BLK), 0 : q * 128] = tile.reshape(BLK, q * 128)
            return carry

        lax.fori_loop(0, ROWS // BLK, block, 0)

    def own_message(g, src, dst, q):
        @pl.when(g == 0)
        def _():
            dst[0 : MSG * q, :] = src[0 : MSG * q, :]

    def send_groups(parts, sign):
        def send(n, carry):
            for g, a, src, dst, s_sem, r_sem, q in parts:
                j = g * PER + turn(n)
                piece = rows_of(j, MSG * q)
                remote(src.at[piece], dst.at[piece], s_sem.at[g, a], r_sem.at[g, a], in_plane(a, j, sign))
            return carry

        lax.fori_loop(1, PER, send, 0)
        for g, a, src, dst, s_sem, r_sem, q in parts:
            if g:
                piece = pl.ds(g * ROWS * q, MSG * q)
                to = in_plane(a, g * PER, sign)
                remote(src.at[piece], dst.at[piece], s_sem.at[g, a], r_sem.at[g, a], to)

    def await_group(g, buf, sem, a, q):
        @pl.when(g == 0)
        def _():
            await_bytes(buf.at[pl.ds(MSG * q, (PER - 1) * MSG * q)], sem.at[0, a])

        @pl.when(g > 0)
        def _():
            await_bytes(buf.at[rows_of(g, ROWS * q)], sem.at[g, a])

    slot = (iota((ROWS, T), 0) % CAP + 1).astype(F32)

    def pick_rows(a, g, s):
        pair, j = iota((ROWS, PER), 0), iota((ROWS, PER), 1)
        return jnp.logical_and(pair // MSG == j, pair // CAP % LINE == s).astype(BF16)

    def fill(one_hot, table, q):
        def half(n, carry):
            for c in range(0, q, 4):
                lanes = slice(c * 128, (c + 4) * 128)
                pg[rows_of(n, HALF), lanes] = mm(one_hot(n), table[:, lanes], NN).astype(BF16)
            return carry

        lax.fori_loop(0, 2, half, 0)

    def find_rows(g):
        for a in range(AXES):
            if g == 0:
                await_bytes(cwg.at[a, pl.ds(64, 192)], gw_r.at[a])
            for s in range(LINE):
                found = mm(pick_rows(a, g, s), cwg[a, pl.ds(s * 64 + g * PER, PER), :], NN)
                hot[a][g * ROWS : (g + 1) * ROWS, s * T : (s + 1) * T] = (found == slot).astype(BF16)

    def token_rows(g):
        for a in range(AXES):
            if g == 0:
                await_bytes(tt[a].at[pl.ds(T, 3 * T)], gt_r.at[a])
            fill(lambda n: hot[a][rows_of(2 * g + n, HALF), :], tt[a], Q_TOK[a])
            pack(st[a], g, Q_TOK[a])
            own_message(g, st[a], rt[a], Q_TOK[a])
        return [(g, a, st[a], rt[a], st_sem, rt_sem, Q_TOK[a]) for a in range(AXES)]

    def cotangent_rows(g):
        for a in range(AXES):
            for s in range(LINE):
                lanes = slice(s * T, (s + 1) * T)
                scale = mm(pick_rows(a, g, s), cwg[a, pl.ds(s * 64 + 32 + g * PER, PER), :], NN)
                one_hot = hot[a][g * ROWS : (g + 1) * ROWS, lanes].astype(F32)
                xs[0:ROWS, lanes] = (one_hot * scale).astype(BF16)
            if g == 0:
                await_bytes(tc[a].at[pl.ds(T, 3 * T)], gc_r.at[a])
            fill(lambda n: xs[rows_of(n, HALF), 0 : LINE * T], tc[a], Q_COT[a])
            pack(sc[a], g, Q_COT[a])
            own_message(g, sc[a], rc[a], Q_COT[a])
        return [(g, a, sc[a], rc[a], sc_sem, rc_sem, Q_COT[a]) for a in range(AXES)]

    find_rows(0)
    send_groups(token_rows(0), 1)
    send_groups(cotangent_rows(0), 1)
    find_rows(1)
    send_groups(token_rows(1), 1)
    send_groups(cotangent_rows(1), 1)
    count_sum(copies, 0, 0)
    copies = count_round(3, 3, 1)
    for load in loads:
        load.wait()

    def reorder(a, src, src_col, dst, dst_rows, dst_col, q, dims):
        for c in range(0, q * 128, 256):
            rows, lanes = src(slice(src_col + c, src_col + c + 256)), slice(dst_col + c, dst_col + c + 256)
            if a == 1:
                sheets = [rows[n * SHEET : (n + 1) * SHEET, :] for n in range(ROWS // SHEET)]
                rows = jnp.concatenate([mm(perm_y[...], sheet, dims).astype(BF16) for sheet in sheets], axis=0)
            elif a == 2:
                rows = mm(perm_z[...], rows, dims).astype(BF16)
            dst[dst_rows, lanes] = rows

    collect = (iota((2 * PER, HALF), 1) // CAP == iota((2 * PER, HALF), 0)).astype(BF16)
    slot_lane = (iota((HALF, 128), 0) % CAP == iota((HALF, 128), 1)).astype(F32)

    def arrive(g, out, src, sem, chunks, cols):
        for a in range(AXES):
            await_group(g, src[a], sem, a, chunks[a])
            unpack(src[a], g, chunks[a], pg, 0)
            reorder(a, lambda lanes: pg[:, lanes], 0, out, rows_of(g, ROWS), cols[a].start, chunks[a], NN)

    def send_back(g):
        send_groups([(g, a, ps[a], pr[a], ps_sem, pr_sem, Q_PAIR[a]) for a in range(AXES)], -1)

        def send_score(i, carry):
            remote(qs.at[pl.ds(i, 1)], qr.at[pl.ds(i, 1)], qs_sem, qr_sem, any_offset(i, -1))
            return carry

        lax.fori_loop(jnp.where(g == 0, 1, g * 4 * PER), (g + 1) * 4 * PER, send_score, 0)

    def expert(g, carry):
        arrive(g, xs, rt, rt_sem, Q_TOK, COLS_TOK)

        def forward(n, carry):
            part = rows_of(2 * g + n, HALF)
            for h in range(H // 256):
                cols = slice(h * 256, (h + 1) * 256)
                pre_gate = mm(xs[part, :], wg[:, cols], NN)
                pre_up = mm(xs[part, :], wu[:, cols], NN)
                logistic = jax.nn.sigmoid(pre_gate)
                act = pre_gate * logistic
                deriv = logistic * (1.0 + pre_gate * (1.0 - logistic))
                hid[part, cols] = (act * pre_up).astype(BF16)
                gu[part, cols] = (pre_up * deriv).astype(BF16)
                gu[part, h * 256 + H : (h + 1) * 256 + H] = act.astype(BF16)
            return carry

        lax.fori_loop(0, 2, forward, 0)
        arrive(g, cs, rc, rc_sem, Q_COT, COLS_COT)
        def backward(n, carry):
            part = rows_of(2 * g + n, HALF)
            score = jnp.zeros((HALF, 1), F32)
            for h in range(H // 256):
                cols, more = slice(h * 256, (h + 1) * 256), slice(h * 256 + H, (h + 1) * 256 + H)
                back = mm(cs[part, :], wd[cols, :], NT)
                score = score + jnp.sum(hid[part, cols].astype(F32) * back, axis=1, keepdims=True)
                gu[part, cols] = (back * gu[part, cols].astype(F32)).astype(BF16)
                gu[part, more] = (back * gu[part, more].astype(F32)).astype(BF16)
            score_rows = mm(collect, (score * slot_lane).astype(BF16), NN)
            for i in range(2 * PER):
                qs[(2 * g + n) * 2 * PER + i] = score_rows[i : i + 1, :]
            return carry

        lax.fori_loop(0, 2, backward, 0)
        part = rows_of(g, ROWS)
        for a in range(AXES):
            q, first = Q_PAIR[a], COLS_PAIR[a].start

            def pair_cols(lanes):
                rows = mm(gu[part, 0:H], wg[lanes, :], NT) + mm(gu[part, H : 2 * H], wu[lanes, :], NT)
                return rows.astype(BF16)

            reorder(a, pair_cols, first, pg, slice(0, ROWS), 0, q, TN)
            await_group(g, st[PAIR_HOME[a]], st_sem, PAIR_HOME[a], q)
            pack(ps[a], g, q)
            own_message(g, ps[a], pr[a], q)

        @pl.when(g == 0)
        def _():
            qr[0] = qs[0]

        @pl.when(g == 0)
        def _():
            send_back(0)

        return carry

    lax.fori_loop(0, GROUPS, expert, 0)
    send_back(1)
    count_sum(copies, 3, 1)
    copies = count_round(6, 7, 2)

    def in_copies(n, buf):
        rows = rows_of(n, 256)
        return (
            pltpu.make_async_copy(out_buf.at[buf, :, pl.ds(0, H)], gg_hbm.at[rows], oa_sem.at[buf, 0]),
            pltpu.make_async_copy(out_buf.at[buf, :, pl.ds(H, H)], gu_hbm.at[rows], oa_sem.at[buf, 1]),
        )

    def grad_in(n, carry):
        buf = n % 2

        @pl.when(n >= 2)
        def _():
            for copy in in_copies(n - 2, buf):
                copy.wait()

        turned = jnp.transpose(xs[:, rows_of(n, 256)])
        for part in (slice(0, H), slice(H, 2 * H)):
            out_buf[buf, :, part] = mm(turned, gu[:, part], NN).astype(BF16)
        for copy in in_copies(n, buf):
            copy.start()
        return carry

    lax.fori_loop(0, D // 256, grad_in, 0)
    for n in (D // 256 - 2, D // 256 - 1):
        for copy in in_copies(n, n % 2):
            copy.wait()

    for a in range(AXES):
        q = Q_PAIR[a]
        for g in range(GROUPS):
            await_group(g, pr[a], pr_sem, a, q)
            unpack(pr[a], g, q, xs, g)
        for c in range(0, q, 4):
            lanes = slice(c * 128, (c + 4) * 128)
            fs[a][:, lanes] = mm(hot[a][...], xs[:, lanes], TN).astype(BF16)
        for s in (1, 3, 2):
            piece = fr[a].at[pl.ds((s - 1) * T, T)]
            remote(fs[a].at[pl.ds(s * T, T)], piece, fs_sem.at[a], fr_sem.at[a], along(a, s, -1))

    def down_copy(n, buf):
        place = gd_hbm.at[rows_of(n // 2, 256), rows_of(n % 2, D // 2)]
        return pltpu.make_async_copy(out_buf.at[buf, :, pl.ds(0, D // 2)], place, od_sem.at[buf])

    def grad_out(n, carry):
        buf = n % 2

        @pl.when(n >= 2)
        def _():
            down_copy(n - 2, buf).wait()

        rows = mm(hid[:, rows_of(n // 2, 256)], cs[:, rows_of(n % 2, D // 2)], TN)
        out_buf[buf, :, 0 : D // 2] = rows.astype(BF16)
        down_copy(n, buf).start()
        return carry

    lax.fori_loop(0, H // 128, grad_out, 0)

    prob = jnp.exp(logit_ref[...] - jnp.max(logit_ref[...], axis=1, keepdims=True))
    prob = prob / jnp.sum(prob, axis=1, keepdims=True)
    count_sum(copies, 6, 2)
    load = cnt[24:32, :] * (E * MICRO / (K * T * E))
    batch_col = jnp.transpose((mb_ref[...] == iota((T, T), 0)).astype(F32))[:, 1:2]
    token_load = jnp.where(batch_col > 0.0, load[1:2, :], load[0:1, :])
    gb_ref[...] = prob * (token_load - jnp.sum(prob * token_load, axis=1, keepdims=True))

    await_bytes(qr.at[pl.ds(1, E - 1)], qr_sem)
    q_all = jnp.concatenate([qr[i] for i in range(E)], axis=0)
    q_rel = jnp.zeros((E, T), F32)
    for s in range(CAP):
        q_rel = jnp.where(code_rel[...] == float(s + 1), q_all[:, s : s + 1], q_rel)
    q_own = mm(q_rel.astype(BF16), perm_ref[...], TN)
    gl_ref[...] = q_own - rwm_ref[...] * jnp.sum(q_own, axis=1, keepdims=True)

    for a in range(AXES):
        await_bytes(fr[a], fr_sem.at[a])
        total = fs[a][0:T, :].astype(F32)
        for s in range(LINE - 1):
            total = total + fr[a][s * T : (s + 1) * T, :].astype(F32)
        gt_ref[:, COLS_PAIR[a]] = total.astype(BF16)

    for n in (H // 128 - 2, H // 128 - 1):
        down_copy(n, n % 2).wait()
    for a in range(AXES):
        await_bytes(tt[a].at[pl.ds(T, 3 * T)], gt_s.at[a])
        await_bytes(tc[a].at[pl.ds(T, 3 * T)], gc_s.at[a])
        await_bytes(cw.at[a, pl.ds(64, 192)], gw_s.at[a])
        await_bytes(fr[a], fs_sem.at[a])
        for g in range(GROUPS):
            await_group(g, sc[a], sc_sem, a, Q_COT[a])
            await_group(g, ps[a], ps_sem, a, Q_PAIR[a])
    await_bytes(qs.at[pl.ds(1, E - 1)], qs_sem)


def settle_kernel(*refs):
    sources, targets, sem, held = refs[:6], refs[6:12], refs[12], refs[13:]
    copies = []
    for src, dst, buf in zip(sources, targets, held):
        pieces = 8 if src.shape[0] > T else 1
        size = src.shape[0] // pieces
        for n in range(pieces):
            rows = pl.ds(n * size, size)
            m = len(copies)
            copies.append(
                (
                    pltpu.make_async_copy(src.at[rows], buf.at[rows], sem.at[0, m]),
                    pltpu.make_async_copy(buf.at[rows], dst.at[rows], sem.at[1, m]),
                )
            )
    for fetch, _ in copies:
        fetch.start()
    for fetch, store in copies:
        fetch.wait()
        store.start()
    for _, store in copies:
        store.wait()


def settle(outs):
    hbm = pl.BlockSpec(memory_space=pl.ANY)
    return pl.pallas_call(
        settle_kernel,
        out_shape=tuple(jax.ShapeDtypeStruct(o.shape, o.dtype) for o in outs),
        in_specs=[hbm] * 6,
        out_specs=(hbm,) * 6,
        scratch_shapes=[pltpu.SemaphoreType.DMA((2, 27))] + [pltpu.VMEM(o.shape, o.dtype) for o in outs],
        compiler_params=pltpu.CompilerParams(vmem_limit_bytes=60 * 2**20),
        name="settle",
    )(*outs)


def per_device(tokens, out_grad, router_logits, expert_picks, micro_batch, w_gate, w_up, w_down):
    vmem, hbm = pl.BlockSpec(memory_space=pltpu.VMEM), pl.BlockSpec(memory_space=pl.ANY)
    dma = pltpu.SemaphoreType.DMA

    def sliced(rows, chunks):
        return [pltpu.VMEM((rows * q, 128), BF16) for q in chunks]

    outs = pl.pallas_call(
        kernel,
        out_shape=(
            jax.ShapeDtypeStruct((T, D), BF16),
            jax.ShapeDtypeStruct((T, E), F32),
            jax.ShapeDtypeStruct((T, E), F32),
            jax.ShapeDtypeStruct((D, H), BF16),
            jax.ShapeDtypeStruct((D, H), BF16),
            jax.ShapeDtypeStruct((H, D), BF16),
        ),
        in_specs=[hbm] * 2 + [vmem] * 3 + [hbm] * 3,
        out_specs=(vmem,) * 3 + (hbm,) * 3,
        scratch_shapes=[
            *sliced(PAIRS, Q_TOK), *sliced(PAIRS, Q_COT),
            *sliced(PAIRS, Q_TOK), *sliced(PAIRS, Q_COT), *sliced(PAIRS, Q_PAIR),
            *[pltpu.VMEM((LINE * T, q * 128), BF16) for q in Q_TOK],
            *[pltpu.VMEM((LINE * T, q * 128), BF16) for q in Q_COT],
            *[pltpu.VMEM((PAIRS, LINE * T), BF16)] * AXES,
            *[pltpu.VMEM((3 * T, q * 128), BF16) for q in Q_PAIR],
            pltpu.VMEM((SHEET, SHEET), BF16), pltpu.VMEM((ROWS, ROWS), BF16),
            *[pltpu.VMEM((PAIRS, D), BF16)] * 2,
            pltpu.VMEM((PAIRS, H), BF16),
            pltpu.VMEM((PAIRS, 2 * H), BF16),
            pltpu.VMEM((D, H), BF16),
            pltpu.VMEM((D, H), BF16),
            pltpu.VMEM((H, D), BF16),
            pltpu.VMEM((ROWS, 1024), BF16),
            pltpu.VMEM((2, 256, 2 * H), BF16),
            pltpu.VMEM((AXES, 256, T), BF16),
            pltpu.VMEM((AXES, 256, T), BF16),
            pltpu.VMEM((E, T), F32),
            pltpu.VMEM((E, E), BF16),
            pltpu.VMEM((T, E), F32),
            pltpu.VMEM((E, 1, 128), F32),
            pltpu.VMEM((E, 1, 128), F32),
            pltpu.VMEM((32, E), F32),
            pltpu.VMEM((13 * 8, E), F32),
            dma((3,)),
            dma((2, AXES)),
            *[dma((AXES,))] * 6,
            *[dma((GROUPS, AXES))] * 6,
            *[dma((AXES,))] * 2,
            dma, dma, dma((13,)), dma((13,)), dma((2, 2)), dma((2,)),
        ],
        compiler_params=pltpu.CompilerParams(
            collective_id=0, has_side_effects=True, vmem_limit_bytes=64 * 2**20
        ),
        name="expert_backward",
    )(tokens, out_grad, router_logits, expert_picks.T, micro_batch.reshape(1, T), w_gate[0], w_up[0], w_down[0])
    grad_tokens, grad_logits, balance_grad, grad_gate, grad_up, grad_down = settle(outs)
    return grad_tokens, grad_logits, balance_grad, grad_gate[None], grad_up[None], grad_down[None]


def solution(mesh):
    rows, cube = P(("dp", "ex", "ey"), None), P(("dp", "ex", "ey"), None, None)
    return jax.shard_map(
        per_device,
        mesh=mesh,
        in_specs=(rows, rows, rows, rows, P(("dp", "ex", "ey")), cube, cube, cube),
        out_specs=(rows, rows, rows, cube, cube, cube),
        check_vma=False,
    )
```

```python
import jax
import jax.numpy as jnp
from jax import lax
from jax.experimental import pallas as pl
from jax.experimental.pallas import tpu as pltpu
from jax.sharding import PartitionSpec as P

MESH = pl.DeviceIdType.MESH
F32, BF16, I32 = jnp.float32, jnp.bfloat16, jnp.int32
NN = (((1,), (0,)), ((), ()))
NT = (((1,), (1,)), ((), ()))
TN = (((0,), (0,)), ((), ()))

D, H, K, T, E, CAP, MICRO = 2048, 768, 8, 128, 128, 9, 2
AXES = 3
LINE = 4
PLANE = E // LINE
GROUPS = 2
PER = PLANE // GROUPS
MSG = LINE * CAP
ROWS = PER * MSG
PAIRS = E * CAP
HALF = ROWS // 2
SHEET = LINE * MSG
BLK = 32
Q_TOK, Q_COT, Q_PAIR = (4, 4, 8), (4, 8, 4), (8, 4, 4)


def slices(chunks):
    starts = [sum(chunks[:a]) * 128 for a in range(AXES)]
    return [slice(s, s + q * 128) for s, q in zip(starts, chunks)]


COLS_TOK, COLS_COT, COLS_PAIR = slices(Q_TOK), slices(Q_COT), slices(Q_PAIR)
PAIR_HOME = (2, 1, 0)


def mm(a, b, dims):
    return lax.dot_general(a, b, dims, preferred_element_type=F32)


def rows_of(g, size):
    return pl.ds(pl.multiple_of(g * size, size), size)


def iota(shape, dim):
    return lax.broadcasted_iota(I32, shape, dim)


def rem(value, size):
    return lax.rem(value, jnp.int32(size)) if isinstance(value, jax.Array) else value % size


def quot(value, size):
    return lax.div(value, jnp.int32(size)) if isinstance(value, jax.Array) else value // size


def moved(steps, dc, sign=1):
    x, ex, y = lax.axis_index("dp"), lax.axis_index("ex"), lax.axis_index("ey")
    z, core = quot(ex, 2), rem(ex, 2)
    side = core if sign == 1 else rem(core + dc, 2)
    dx, dy, dz = axes_of(steps, side)
    if sign == -1:
        dx, dy, dz = 4 - dx, 4 - dy, 4 - dz
    return rem(x + dx, 4), rem(z + dz, 4) * 2 + rem(core + dc, 2), rem(y + dy, 4)


def axes_of(steps, side):
    a, b, c = steps
    return a + side * (c - a), b + side * (a - b), c + side * (b - c)


def along(axis, step, sign=1):
    return moved([step if axis == n else 0 for n in range(AXES)], 0, sign)


def in_plane(axis, j, sign=1):
    core, high, low = quot(j, 16), rem(quot(j, 4), 4), rem(j, 4)
    return moved(((0, low, high), (low, 0, high), (low, high, 0))[axis], core, sign)


def any_offset(i, sign=1):
    return moved((rem(i, 4), rem(quot(i, 4), 4), rem(quot(i, 16), 4)), quot(i, 64), sign)


def turn(n):
    return rem(rem(n, 4) + quot(n, 4), 4) * 4 + rem(n, 4)


def expert_at(steps, dc):
    x, ex, y = lax.axis_index("dp"), lax.axis_index("ex"), lax.axis_index("ey")
    dx, dy, dz = axes_of(steps, ex % 2)
    return ((x + dx) & 3) * 32 + ((((ex // 2) + dz) & 3) * 2 + (((ex % 2) + dc) & 1)) * 4 + ((y + dy) & 3)


def kernel(
    tok_hbm, cot_hbm, logit_ref, pick_ref, mb_ref, wg_hbm, wu_hbm, wd_hbm,
    gt_ref, gl_ref, gb_ref, gg_hbm, gu_hbm, gd_hbm,
    st0, st1, st2, sc0, sc1, sc2, rt0, rt1, rt2, rc0, rc1, rc2, pr0, pr1, pr2,
    tt0, tt1, tt2, tc0, tc1, tc2, hot0, hot1, hot2, fr0, fr1, fr2, perm_y, perm_z,
    xs, cs, hid, gu, wg, wu, wd, pg, out_buf, cw, cwg, code_rel, perm_ref, rwm_ref, qs, qr, cnt, cnt_in,
    w_sem, own_sem, gt_s, gt_r, gc_s, gc_r, gw_s, gw_r, st_sem, sc_sem, rt_sem, rc_sem, ps_sem, pr_sem, fs_sem, fr_sem,
    qs_sem, qr_sem, cs_sem, cr_sem, oa_sem, od_sem,
):
    x, ex, y = lax.axis_index("dp"), lax.axis_index("ex"), lax.axis_index("ey")
    st, sc, rt, rc, pr = (st0, st1, st2), (sc0, sc1, sc2), (rt0, rt1, rt2), (rc0, rc1, rc2), (pr0, pr1, pr2)
    tt, tc, hot, fr = (tt0, tt1, tt2), (tc0, tc1, tc2), (hot0, hot1, hot2), (fr0, fr1, fr2)
    ps = tuple(st[n] for n in PAIR_HOME)
    fs = tuple(tt[n] for n in PAIR_HOME)
    barrier = pltpu.get_barrier_semaphore()

    ys = [rem(y + n, 4) for n in range(4)]
    exs = [rem(quot(ex, 2) + n, 4) * 2 + c for n in range(4) for c in (rem(ex, 2), rem(ex + 1, 2))]

    def greet(n, carry):
        to_x = rem(x + n, 4)
        for m in range(1, 32):
            to = (to_x, exs[m // 4], ys[m % 4])
            pl.semaphore_signal(barrier, inc=1, device_id=to, device_id_type=MESH)
        return carry

    lax.fori_loop(0, 4, greet, 0)
    for n in range(1, 4):
        pl.semaphore_signal(barrier, inc=1, device_id=(rem(x + n, 4), ex, y), device_id_type=MESH)
    loads = [
        pltpu.make_async_copy(src, dst, w_sem.at[n])
        for n, (src, dst) in enumerate(((wg_hbm, wg), (wu_hbm, wu), (wd_hbm, wd)))
    ]
    own = []
    for a in range(AXES):
        own.append(pltpu.make_async_copy(tok_hbm.at[:, COLS_TOK[a]], tt[a].at[pl.ds(0, T)], own_sem.at[0, a]))
        own.append(pltpu.make_async_copy(cot_hbm.at[:, COLS_COT[a]], tc[a].at[pl.ds(0, T)], own_sem.at[1, a]))
    for load in own:
        load.start()

    def remote(src, dst, send_sem, recv_sem, to):
        pltpu.make_async_remote_copy(
            src_ref=src, dst_ref=dst, send_sem=send_sem, recv_sem=recv_sem, device_id=to, device_id_type=MESH
        ).start()

    def await_bytes(piece, sem):
        pltpu.make_async_copy(piece, piece, sem).wait()

    pl.semaphore_wait(barrier, E - 1)
    for s in (1, 3):
        for a in range(AXES):
            home = tt[a].at[pl.ds(s * T, T)]
            remote(tok_hbm.at[:, COLS_TOK[a]], home, gt_s.at[a], gt_r.at[a, s], along(a, s))

    expert_row = iota((E, T), 0)
    picked_t = jnp.zeros((E, T), F32)
    for k in range(K):
        picked_t = jnp.where(pick_ref[k : k + 1, :] == expert_row, 1.0, picked_t)
    picked = jnp.transpose(picked_t)
    logits = logit_ref[...]
    top = jnp.max(jnp.where(picked > 0.0, logits, -jnp.inf), axis=1, keepdims=True)
    rwm = jnp.where(picked > 0.0, jnp.exp(jnp.minimum(logits - top, 0.0)), 0.0)
    rwm = rwm / jnp.sum(rwm, axis=1, keepdims=True)
    rwm_ref[...] = rwm
    weight = rwm.astype(BF16)
    earlier = (iota((T, T), 1) < iota((T, T), 0)).astype(BF16)
    code = jnp.where(picked > 0.0, mm(earlier, picked.astype(BF16), NN) + 1.0, 0.0).astype(BF16)
    row, lane = iota((E, E), 0), iota((E, E), 1)
    perm = (expert_at((row & 3, (row >> 2) & 3, (row >> 4) & 3), row >> 6) == lane).astype(BF16)
    perm_ref[...] = perm
    code_rel[...] = mm(perm, code, NT)
    step, core, high, low = row >> 5, (row >> 4) & 1, (row >> 2) & 3, row & 3
    for a in range(AXES):
        place = ((step, low, high), (low, step, high), (low, high, step))[a]
        perm = (expert_at(place, core) == lane).astype(BF16)
        code_a, weight_a = mm(perm, code, NT).astype(BF16), mm(perm, weight, NT).astype(BF16)
        for s in range(LINE):
            home = cw if s else cwg
            home[a, s * 64 : s * 64 + 32, :] = code_a[s * 32 : s * 32 + 32, :]
            home[a, s * 64 + 32 : s * 64 + 64, :] = weight_a[s * 32 : s * 32 + 32, :]
    mb_hot = (mb_ref[...] == iota((8, T), 0)).astype(BF16)
    cnt[0:8, :] = mm(mb_hot, picked.astype(BF16), NN)
    for s in (1, 3, 2):
        for a in range(AXES):
            piece = pl.ds(s * 64, 64)
            remote(cw.at[a, piece], cwg.at[a, piece], gw_s.at[a], gw_r.at[a], along(a, s))
    for s in (1, 3):
        for a in range(AXES):
            home = tc[a].at[pl.ds(s * T, T)]
            remote(cot_hbm.at[:, COLS_COT[a]], home, gc_s.at[a], gc_r.at[a, s], along(a, s))

    def pass_on(held, send_sem, recv_sem, chunks):
        for s, begin in ((1, 0), (3, 1)):
            for a in range(AXES):
                await_bytes(held[a].at[pl.ds(s * T, T)], recv_sem.at[a, s])
                lanes = pl.ds(begin * chunks[a] * 64, chunks[a] * 64)
                block, home = held[a].at[pl.ds(s * T, T), lanes], held[a].at[pl.ds(2 * T, T), lanes]
                remote(block, home, send_sem.at[a], recv_sem.at[a, 2], along(a, s))

    for load in loads:
        load.start()

    def count_round(base, others, stage):
        copies = []
        for n in range(others):
            to = (
                ((x + n + 1) % 4, ex, y),
                (x, ex, (y + n + 1) % 4),
                (x, (ex + n + 1) % 8, y),
            )[stage]
            copies.append(
                pltpu.make_async_remote_copy(
                    src_ref=cnt.at[pl.ds(stage * 8, 8)],
                    dst_ref=cnt_in.at[pl.ds((base + n) * 8, 8)],
                    send_sem=cs_sem.at[base + n],
                    recv_sem=cr_sem.at[base + n],
                    device_id=to,
                    device_id_type=MESH,
                )
            )
        for copy in copies:
            copy.start()
        return copies

    def count_sum(copies, base, stage):
        total = cnt[stage * 8 : stage * 8 + 8, :]
        for n, copy in enumerate(copies):
            copy.wait()
            total = total + cnt_in[(base + n) * 8 : (base + n) * 8 + 8, :]
        cnt[stage * 8 + 8 : stage * 8 + 16, :] = total

    copies = count_round(0, 3, 0)


    def order_block(n, carry):
        pair = iota((64, 1), 0) + n * 64
        s_, x_, y_, z_ = pair % CAP, pair // 9 % 4, pair // 36 % 4, pair // 144
        perm_z[rows_of(n, 64), :] = (((y_ * 4 + x_) * 4 + z_) * CAP + s_ == iota((64, ROWS), 1)).astype(BF16)
        return carry

    lax.fori_loop(0, ROWS // 64, order_block, 0)
    pair = iota((SHEET, 1), 0)
    perm_y[...] = ((pair // 9 % 4 * 4 + pair // 36) * CAP + pair % CAP == iota((SHEET, SHEET), 1)).astype(BF16)
    for load in own:
        load.wait()

    def pack(out, g, q):
        def block(n, carry):
            tile = pg[rows_of(n, BLK), 0 : q * 128].reshape(BLK, q, 128)
            out[rows_of(g * (ROWS // BLK) + n, BLK * q), :] = tile.reshape(BLK * q, 128)
            return carry

        lax.fori_loop(0, ROWS // BLK, block, 0)

    def unpack(src, g, q, out, out_g):
        def block(n, carry):
            tile = src[rows_of(g * (ROWS // BLK) + n, BLK * q), :].reshape(BLK, q, 128)
            out[rows_of(out_g * (ROWS // BLK) + n, BLK), 0 : q * 128] = tile.reshape(BLK, q * 128)
            return carry

        lax.fori_loop(0, ROWS // BLK, block, 0)

    def own_message(g, src, dst, q):
        @pl.when(g == 0)
        def _():
            dst[0 : MSG * q, :] = src[0 : MSG * q, :]

    def send_groups(parts, sign):
        def send(n, carry):
            for g, a, src, dst, s_sem, r_sem, q in parts:
                j = g * PER + turn(n)
                piece = rows_of(j, MSG * q)
                remote(src.at[piece], dst.at[piece], s_sem.at[g, a], r_sem.at[g, a], in_plane(a, j, sign))
            return carry

        lax.fori_loop(1, PER, send, 0)
        for g, a, src, dst, s_sem, r_sem, q in parts:
            if g:
                piece = pl.ds(g * ROWS * q, MSG * q)
                to = in_plane(a, g * PER, sign)
                remote(src.at[piece], dst.at[piece], s_sem.at[g, a], r_sem.at[g, a], to)

    def await_group(g, buf, sem, a, q):
        @pl.when(g == 0)
        def _():
            await_bytes(buf.at[pl.ds(MSG * q, (PER - 1) * MSG * q)], sem.at[0, a])

        @pl.when(g > 0)
        def _():
            await_bytes(buf.at[rows_of(g, ROWS * q)], sem.at[g, a])

    slot = (iota((ROWS, T), 0) % CAP + 1).astype(F32)

    def pick_rows(a, g, s):
        pair, j = iota((ROWS, PER), 0), iota((ROWS, PER), 1)
        return jnp.logical_and(pair // MSG == j, pair // CAP % LINE == s).astype(BF16)

    def fill(one_hot, table, q):
        def half(n, carry):
            for c in range(0, q, 4):
                lanes = slice(c * 128, (c + 4) * 128)
                pg[rows_of(n, HALF), lanes] = mm(one_hot(n), table[:, lanes], NN).astype(BF16)
            return carry

        lax.fori_loop(0, 2, half, 0)

    def find_rows(g):
        for a in range(AXES):
            if g == 0:
                await_bytes(cwg.at[a, pl.ds(64, 192)], gw_r.at[a])
            for s in range(LINE):
                found = mm(pick_rows(a, g, s), cwg[a, pl.ds(s * 64 + g * PER, PER), :], NN)
                hot[a][g * ROWS : (g + 1) * ROWS, s * T : (s + 1) * T] = (found == slot).astype(BF16)

    def token_rows(g):
        for a in range(AXES):
            if g == 0:
                await_bytes(tt[a].at[pl.ds(2 * T, T)], gt_r.at[a, 2])
            fill(lambda n: hot[a][rows_of(2 * g + n, HALF), :], tt[a], Q_TOK[a])
            pack(st[a], g, Q_TOK[a])
            own_message(g, st[a], rt[a], Q_TOK[a])
        return [(g, a, st[a], rt[a], st_sem, rt_sem, Q_TOK[a]) for a in range(AXES)]

    def cotangent_rows(g):
        for a in range(AXES):
            for s in range(LINE):
                lanes = slice(s * T, (s + 1) * T)
                scale = mm(pick_rows(a, g, s), cwg[a, pl.ds(s * 64 + 32 + g * PER, PER), :], NN)
                one_hot = hot[a][g * ROWS : (g + 1) * ROWS, lanes].astype(F32)
                xs[0:ROWS, lanes] = (one_hot * scale).astype(BF16)
            if g == 0:
                await_bytes(tc[a].at[pl.ds(2 * T, T)], gc_r.at[a, 2])
            fill(lambda n: xs[rows_of(n, HALF), 0 : LINE * T], tc[a], Q_COT[a])
            pack(sc[a], g, Q_COT[a])
            own_message(g, sc[a], rc[a], Q_COT[a])
        return [(g, a, sc[a], rc[a], sc_sem, rc_sem, Q_COT[a]) for a in range(AXES)]

    pass_on(tt, gt_s, gt_r, Q_TOK)
    find_rows(0)
    parts = token_rows(0)
    pass_on(tc, gc_s, gc_r, Q_COT)
    send_groups(parts, 1)
    send_groups(cotangent_rows(0), 1)
    find_rows(1)
    send_groups(token_rows(1), 1)
    send_groups(cotangent_rows(1), 1)
    count_sum(copies, 0, 0)
    copies = count_round(3, 3, 1)
    for load in loads:
        load.wait()

    def reorder(a, src, src_col, dst, dst_rows, dst_col, q, dims):
        for c in range(0, q * 128, 256):
            rows, lanes = src(slice(src_col + c, src_col + c + 256)), slice(dst_col + c, dst_col + c + 256)
            if a == 1:
                sheets = [rows[n * SHEET : (n + 1) * SHEET, :] for n in range(ROWS // SHEET)]
                rows = jnp.concatenate([mm(perm_y[...], sheet, dims).astype(BF16) for sheet in sheets], axis=0)
            elif a == 2:
                rows = mm(perm_z[...], rows, dims).astype(BF16)
            dst[dst_rows, lanes] = rows

    collect = (iota((2 * PER, HALF), 1) // CAP == iota((2 * PER, HALF), 0)).astype(BF16)
    slot_lane = (iota((HALF, 128), 0) % CAP == iota((HALF, 128), 1)).astype(F32)

    def arrive(g, out, src, sem, chunks, cols):
        for a in range(AXES):
            await_group(g, src[a], sem, a, chunks[a])
            unpack(src[a], g, chunks[a], pg, 0)
            reorder(a, lambda lanes: pg[:, lanes], 0, out, rows_of(g, ROWS), cols[a].start, chunks[a], NN)

    def send_score(i, carry):
        remote(qs.at[pl.ds(i, 1)], qr.at[pl.ds(i, 1)], qs_sem, qr_sem, any_offset(i, -1))
        return carry

    def expert(g, carry):
        arrive(g, xs, rt, rt_sem, Q_TOK, COLS_TOK)

        def forward(n, carry):
            part = rows_of(2 * g + n, HALF)
            for h in range(H // 256):
                cols = slice(h * 256, (h + 1) * 256)
                pre_gate = mm(xs[part, :], wg[:, cols], NN)
                pre_up = mm(xs[part, :], wu[:, cols], NN)
                logistic = jax.nn.sigmoid(pre_gate)
                act = pre_gate * logistic
                deriv = logistic * (1.0 + pre_gate * (1.0 - logistic))
                hid[part, cols] = (act * pre_up).astype(BF16)
                gu[part, cols] = (pre_up * deriv).astype(BF16)
                gu[part, h * 256 + H : (h + 1) * 256 + H] = act.astype(BF16)
            return carry

        lax.fori_loop(0, 2, forward, 0)
        arrive(g, cs, rc, rc_sem, Q_COT, COLS_COT)
        def backward(n, carry):
            part = rows_of(2 * g + n, HALF)
            score = jnp.zeros((HALF, 1), F32)
            for h in range(H // 256):
                cols, more = slice(h * 256, (h + 1) * 256), slice(h * 256 + H, (h + 1) * 256 + H)
                back = mm(cs[part, :], wd[cols, :], NT)
                score = score + jnp.sum(hid[part, cols].astype(F32) * back, axis=1, keepdims=True)
                gu[part, cols] = (back * gu[part, cols].astype(F32)).astype(BF16)
                gu[part, more] = (back * gu[part, more].astype(F32)).astype(BF16)
            score_rows = mm(collect, (score * slot_lane).astype(BF16), NN)
            for i in range(2 * PER):
                qs[(2 * g + n) * 2 * PER + i] = score_rows[i : i + 1, :]
            return carry

        lax.fori_loop(0, 2, backward, 0)
        part = rows_of(g, ROWS)
        for a in (1, 2, 0):
            q, first = Q_PAIR[a], COLS_PAIR[a].start

            def pair_cols(lanes):
                rows = mm(gu[part, 0:H], wg[lanes, :], NT) + mm(gu[part, H : 2 * H], wu[lanes, :], NT)
                return rows.astype(BF16)

            reorder(a, pair_cols, first, pg, slice(0, ROWS), 0, q, TN)
            await_group(g, st[PAIR_HOME[a]], st_sem, PAIR_HOME[a], q)
            pack(ps[a], g, q)
            own_message(g, ps[a], pr[a], q)

            def send(n, carry):
                j = g * PER + turn(n)
                piece = rows_of(j, MSG * q)
                remote(ps[a].at[piece], pr[a].at[piece], ps_sem.at[g, a], pr_sem.at[g, a], in_plane(a, j, -1))
                return carry

            lax.fori_loop(jnp.where(g == 0, 1, 0), PER, send, 0)

        @pl.when(g == 0)
        def _():
            qr[0] = qs[0]

        lax.fori_loop(jnp.where(g == 0, 1, g * 4 * PER), (g + 1) * 4 * PER, send_score, 0)
        return carry

    lax.fori_loop(0, GROUPS, expert, 0)
    count_sum(copies, 3, 1)
    copies = count_round(6, 7, 2)

    def in_copies(n, buf):
        rows = rows_of(n, 256)
        return (
            pltpu.make_async_copy(out_buf.at[buf, :, pl.ds(0, H)], gg_hbm.at[rows], oa_sem.at[buf, 0]),
            pltpu.make_async_copy(out_buf.at[buf, :, pl.ds(H, H)], gu_hbm.at[rows], oa_sem.at[buf, 1]),
        )

    def grad_in(n, carry):
        buf = n % 2

        @pl.when(n >= 2)
        def _():
            for copy in in_copies(n - 2, buf):
                copy.wait()

        turned = jnp.transpose(xs[:, rows_of(n, 256)])
        for part in (slice(0, H), slice(H, 2 * H)):
            out_buf[buf, :, part] = mm(turned, gu[:, part], NN).astype(BF16)
        for copy in in_copies(n, buf):
            copy.start()
        return carry

    lax.fori_loop(0, D // 256, grad_in, 0)
    for n in (D // 256 - 2, D // 256 - 1):
        for copy in in_copies(n, n % 2):
            copy.wait()

    for a in range(AXES):
        q = Q_PAIR[a]
        for g in range(GROUPS):
            await_group(g, pr[a], pr_sem, a, q)
            unpack(pr[a], g, q, xs, g)
        home = PAIR_HOME[a]
        await_bytes(tt[home].at[pl.ds(T, 3 * T)], gt_s.at[home])
        for c in range(0, q, 4):
            lanes = slice(c * 128, (c + 4) * 128)
            fs[a][:, lanes] = mm(hot[a][...], xs[:, lanes], TN).astype(BF16)
        for s in (1, 3, 2):
            piece = fr[a].at[pl.ds((s - 1) * T, T)]
            remote(fs[a].at[pl.ds(s * T, T)], piece, fs_sem.at[a], fr_sem.at[a], along(a, s, -1))

    def down_copy(n, buf):
        place = gd_hbm.at[rows_of(n // 2, 256), rows_of(n % 2, D // 2)]
        return pltpu.make_async_copy(out_buf.at[buf, :, pl.ds(0, D // 2)], place, od_sem.at[buf])

    def grad_out(n, carry):
        buf = n % 2

        @pl.when(n >= 2)
        def _():
            down_copy(n - 2, buf).wait()

        rows = mm(hid[:, rows_of(n // 2, 256)], cs[:, rows_of(n % 2, D // 2)], TN)
        out_buf[buf, :, 0 : D // 2] = rows.astype(BF16)
        down_copy(n, buf).start()
        return carry

    lax.fori_loop(0, H // 128, grad_out, 0)

    prob = jnp.exp(logit_ref[...] - jnp.max(logit_ref[...], axis=1, keepdims=True))
    prob = prob / jnp.sum(prob, axis=1, keepdims=True)
    count_sum(copies, 6, 2)
    load = cnt[24:32, :] * (E * MICRO / (K * T * E))
    batch_col = jnp.transpose((mb_ref[...] == iota((T, T), 0)).astype(F32))[:, 1:2]
    token_load = jnp.where(batch_col > 0.0, load[1:2, :], load[0:1, :])
    gb_ref[...] = prob * (token_load - jnp.sum(prob * token_load, axis=1, keepdims=True))

    await_bytes(qr.at[pl.ds(1, E - 1)], qr_sem)
    q_all = jnp.concatenate([qr[i] for i in range(E)], axis=0)
    q_rel = jnp.zeros((E, T), F32)
    for s in range(CAP):
        q_rel = jnp.where(code_rel[...] == float(s + 1), q_all[:, s : s + 1], q_rel)
    q_own = mm(q_rel.astype(BF16), perm_ref[...], TN)
    gl_ref[...] = q_own - rwm_ref[...] * jnp.sum(q_own, axis=1, keepdims=True)

    for a in range(AXES):
        await_bytes(fr[a], fr_sem.at[a])
        total = fs[a][0:T, :].astype(F32)
        for s in range(LINE - 1):
            total = total + fr[a][s * T : (s + 1) * T, :].astype(F32)
        gt_ref[:, COLS_PAIR[a]] = total.astype(BF16)

    for n in (H // 128 - 2, H // 128 - 1):
        down_copy(n, n % 2).wait()
    for a in range(AXES):
        await_bytes(tc[a].at[pl.ds(T, 3 * T)], gc_s.at[a])
        await_bytes(cw.at[a, pl.ds(64, 192)], gw_s.at[a])
        await_bytes(fr[a], fs_sem.at[a])
        for g in range(GROUPS):
            await_group(g, sc[a], sc_sem, a, Q_COT[a])
            await_group(g, ps[a], ps_sem, a, Q_PAIR[a])
    await_bytes(qs.at[pl.ds(1, E - 1)], qs_sem)


def settle_kernel(*refs):
    sources, targets, sem, held = refs[:6], refs[6:12], refs[12], refs[13:]
    copies = []
    for src, dst, buf in zip(sources, targets, held):
        pieces = 8 if src.shape[0] > T else 1
        size = src.shape[0] // pieces
        for n in range(pieces):
            rows = pl.ds(n * size, size)
            m = len(copies)
            copies.append(
                (
                    pltpu.make_async_copy(src.at[rows], buf.at[rows], sem.at[0, m]),
                    pltpu.make_async_copy(buf.at[rows], dst.at[rows], sem.at[1, m]),
                )
            )
    for fetch, _ in copies:
        fetch.start()
    for fetch, store in copies:
        fetch.wait()
        store.start()
    for _, store in copies:
        store.wait()


def settle(outs):
    hbm = pl.BlockSpec(memory_space=pl.ANY)
    return pl.pallas_call(
        settle_kernel,
        out_shape=tuple(jax.ShapeDtypeStruct(o.shape, o.dtype) for o in outs),
        in_specs=[hbm] * 6,
        out_specs=(hbm,) * 6,
        scratch_shapes=[pltpu.SemaphoreType.DMA((2, 27))] + [pltpu.VMEM(o.shape, o.dtype) for o in outs],
        compiler_params=pltpu.CompilerParams(vmem_limit_bytes=60 * 2**20),
        name="settle",
    )(*outs)


def per_device(tokens, out_grad, router_logits, expert_picks, micro_batch, w_gate, w_up, w_down):
    vmem, hbm = pl.BlockSpec(memory_space=pltpu.VMEM), pl.BlockSpec(memory_space=pl.ANY)
    dma = pltpu.SemaphoreType.DMA

    def sliced(rows, chunks):
        return [pltpu.VMEM((rows * q, 128), BF16) for q in chunks]

    outs = pl.pallas_call(
        kernel,
        out_shape=(
            jax.ShapeDtypeStruct((T, D), BF16),
            jax.ShapeDtypeStruct((T, E), F32),
            jax.ShapeDtypeStruct((T, E), F32),
            jax.ShapeDtypeStruct((D, H), BF16),
            jax.ShapeDtypeStruct((D, H), BF16),
            jax.ShapeDtypeStruct((H, D), BF16),
        ),
        in_specs=[hbm] * 2 + [vmem] * 3 + [hbm] * 3,
        out_specs=(vmem,) * 3 + (hbm,) * 3,
        scratch_shapes=[
            *sliced(PAIRS, Q_TOK), *sliced(PAIRS, Q_COT),
            *sliced(PAIRS, Q_TOK), *sliced(PAIRS, Q_COT), *sliced(PAIRS, Q_PAIR),
            *[pltpu.VMEM((LINE * T, q * 128), BF16) for q in Q_TOK],
            *[pltpu.VMEM((LINE * T, q * 128), BF16) for q in Q_COT],
            *[pltpu.VMEM((PAIRS, LINE * T), BF16)] * AXES,
            *[pltpu.VMEM((3 * T, q * 128), BF16) for q in Q_PAIR],
            pltpu.VMEM((SHEET, SHEET), BF16), pltpu.VMEM((ROWS, ROWS), BF16),
            *[pltpu.VMEM((PAIRS, D), BF16)] * 2,
            pltpu.VMEM((PAIRS, H), BF16),
            pltpu.VMEM((PAIRS, 2 * H), BF16),
            pltpu.VMEM((D, H), BF16),
            pltpu.VMEM((D, H), BF16),
            pltpu.VMEM((H, D), BF16),
            pltpu.VMEM((ROWS, 1024), BF16),
            pltpu.VMEM((2, 256, 2 * H), BF16),
            pltpu.VMEM((AXES, 256, T), BF16),
            pltpu.VMEM((AXES, 256, T), BF16),
            pltpu.VMEM((E, T), F32),
            pltpu.VMEM((E, E), BF16),
            pltpu.VMEM((T, E), F32),
            pltpu.VMEM((E, 1, 128), F32),
            pltpu.VMEM((E, 1, 128), F32),
            pltpu.VMEM((32, E), F32),
            pltpu.VMEM((13 * 8, E), F32),
            dma((3,)),
            dma((2, AXES)),
            dma((AXES,)), dma((AXES, LINE)), dma((AXES,)), dma((AXES, LINE)), dma((AXES,)), dma((AXES,)),
            *[dma((GROUPS, AXES))] * 6,
            *[dma((AXES,))] * 2,
            dma, dma, dma((13,)), dma((13,)), dma((2, 2)), dma((2,)),
        ],
        compiler_params=pltpu.CompilerParams(
            collective_id=0, has_side_effects=True, vmem_limit_bytes=64 * 2**20
        ),
        name="expert_backward",
    )(tokens, out_grad, router_logits, expert_picks.T, micro_batch.reshape(1, T), w_gate[0], w_up[0], w_down[0])
    grad_tokens, grad_logits, balance_grad, grad_gate, grad_up, grad_down = settle(outs)
    return grad_tokens, grad_logits, balance_grad, grad_gate[None], grad_up[None], grad_down[None]


def solution(mesh):
    rows, cube = P(("dp", "ex", "ey"), None), P(("dp", "ex", "ey"), None, None)
    return jax.shard_map(
        per_device,
        mesh=mesh,
        in_specs=(rows, rows, rows, rows, P(("dp", "ex", "ey")), cube, cube, cube),
        out_specs=(rows, rows, rows, cube, cube, cube),
        check_vma=False,
    )
```

```python
import jax
import jax.numpy as jnp
from jax import lax
from jax.experimental import pallas as pl
from jax.experimental.pallas import tpu as pltpu
from jax.sharding import PartitionSpec as P

MESH = pl.DeviceIdType.MESH
F32, BF16, I32 = jnp.float32, jnp.bfloat16, jnp.int32
NN = (((1,), (0,)), ((), ()))
NT = (((1,), (1,)), ((), ()))
TN = (((0,), (0,)), ((), ()))

D, H, K, T, E, CAP, MICRO = 2048, 768, 8, 128, 128, 9, 2
AXES = 3
LINE = 4
PLANE = E // LINE
GROUPS = 2
PER = PLANE // GROUPS
MSG = LINE * CAP
ROWS = PER * MSG
PAIRS = E * CAP
HALF = ROWS // 2
SHEET = LINE * MSG
BLK = 32
Q_TOK, Q_COT, Q_PAIR = (4, 4, 8), (4, 8, 4), (8, 4, 4)


def slices(chunks):
    starts = [sum(chunks[:a]) * 128 for a in range(AXES)]
    return [slice(s, s + q * 128) for s, q in zip(starts, chunks)]


COLS_TOK, COLS_COT, COLS_PAIR = slices(Q_TOK), slices(Q_COT), slices(Q_PAIR)
PAIR_HOME = (2, 1, 0)


def mm(a, b, dims):
    return lax.dot_general(a, b, dims, preferred_element_type=F32)


def rows_of(g, size):
    return pl.ds(pl.multiple_of(g * size, size), size)


def iota(shape, dim):
    return lax.broadcasted_iota(I32, shape, dim)


def rem(value, size):
    return lax.rem(value, jnp.int32(size)) if isinstance(value, jax.Array) else value % size


def quot(value, size):
    return lax.div(value, jnp.int32(size)) if isinstance(value, jax.Array) else value // size


def moved(steps, dc, sign=1):
    x, ex, y = lax.axis_index("dp"), lax.axis_index("ex"), lax.axis_index("ey")
    z, core = quot(ex, 2), rem(ex, 2)
    side = core if sign == 1 else rem(core + dc, 2)
    dx, dy, dz = axes_of(steps, side)
    if sign == -1:
        dx, dy, dz = 4 - dx, 4 - dy, 4 - dz
    return rem(x + dx, 4), rem(z + dz, 4) * 2 + rem(core + dc, 2), rem(y + dy, 4)


def axes_of(steps, side):
    a, b, c = steps
    return a + side * (c - a), b + side * (a - b), c + side * (b - c)


def along(axis, step, sign=1):
    return moved([step if axis == n else 0 for n in range(AXES)], 0, sign)


def in_plane(axis, j, sign=1):
    core, high, low = quot(j, 16), rem(quot(j, 4), 4), rem(j, 4)
    return moved(((0, low, high), (low, 0, high), (low, high, 0))[axis], core, sign)


def any_offset(i, sign=1):
    return moved((rem(i, 4), rem(quot(i, 4), 4), rem(quot(i, 16), 4)), quot(i, 64), sign)


def turn(n):
    return rem(rem(n, 4) + quot(n, 4), 4) * 4 + rem(n, 4)


def expert_at(steps, dc):
    x, ex, y = lax.axis_index("dp"), lax.axis_index("ex"), lax.axis_index("ey")
    dx, dy, dz = axes_of(steps, ex % 2)
    return ((x + dx) & 3) * 32 + ((((ex // 2) + dz) & 3) * 2 + (((ex % 2) + dc) & 1)) * 4 + ((y + dy) & 3)


def kernel(
    tok_hbm, cot_hbm, logit_ref, pick_ref, mb_ref, wg_hbm, wu_hbm, wd_hbm,
    gt_ref, gl_ref, gb_ref, gg_hbm, gu_hbm, gd_hbm,
    st0, st1, st2, sc0, sc1, sc2, rt0, rt1, rt2, rc0, rc1, rc2, pr0, pr1, pr2,
    tt0, tt1, tt2, tc0, tc1, tc2, hot0, hot1, hot2, fr0, fr1, fr2, perm_y, perm_z,
    xs, cs, hid, gu, wg, wu, wd, pg, out_buf, cw, cwg, code_rel, perm_ref, rwm_ref, qs, qr, cnt, cnt_in,
    w_sem, own_sem, gt_s, gt_r, gc_s, gc_r, gw_s, gw_r, st_sem, sc_sem, rt_sem, rc_sem, ps_sem, pr_sem, fs_sem, fr_sem,
    qs_sem, qr_sem, cs_sem, cr_sem, oa_sem, od_sem,
):
    x, ex, y = lax.axis_index("dp"), lax.axis_index("ex"), lax.axis_index("ey")
    st, sc, rt, rc, pr = (st0, st1, st2), (sc0, sc1, sc2), (rt0, rt1, rt2), (rc0, rc1, rc2), (pr0, pr1, pr2)
    tt, tc, hot, fr = (tt0, tt1, tt2), (tc0, tc1, tc2), (hot0, hot1, hot2), (fr0, fr1, fr2)
    ps = tuple(st[n] for n in PAIR_HOME)
    fs = tuple(tt[n] for n in PAIR_HOME)
    barrier = pltpu.get_barrier_semaphore()

    ys = [rem(y + n, 4) for n in range(4)]
    exs = [rem(quot(ex, 2) + n, 4) * 2 + c for n in range(4) for c in (rem(ex, 2), rem(ex + 1, 2))]

    def greet(n, carry):
        to_x = rem(x + n, 4)
        for m in range(1, 32):
            to = (to_x, exs[m // 4], ys[m % 4])
            pl.semaphore_signal(barrier, inc=1, device_id=to, device_id_type=MESH)
        return carry

    lax.fori_loop(0, 4, greet, 0)
    for n in range(1, 4):
        pl.semaphore_signal(barrier, inc=1, device_id=(rem(x + n, 4), ex, y), device_id_type=MESH)
    loads = [
        pltpu.make_async_copy(src, dst, w_sem.at[n])
        for n, (src, dst) in enumerate(((wg_hbm, wg), (wu_hbm, wu), (wd_hbm, wd)))
    ]
    own = []
    for a in range(AXES):
        own.append(pltpu.make_async_copy(tok_hbm.at[:, COLS_TOK[a]], tt[a].at[pl.ds(0, T)], own_sem.at[0, a]))
        own.append(pltpu.make_async_copy(cot_hbm.at[:, COLS_COT[a]], tc[a].at[pl.ds(0, T)], own_sem.at[1, a]))
    for load in own:
        load.start()

    def remote(src, dst, send_sem, recv_sem, to):
        pltpu.make_async_remote_copy(
            src_ref=src, dst_ref=dst, send_sem=send_sem, recv_sem=recv_sem, device_id=to, device_id_type=MESH
        ).start()

    def await_bytes(piece, sem):
        pltpu.make_async_copy(piece, piece, sem).wait()

    pl.semaphore_wait(barrier, E - 1)
    for s in (1, 3):
        for a in range(AXES):
            home = tt[a].at[pl.ds(s * T, T)]
            remote(tok_hbm.at[:, COLS_TOK[a]], home, gt_s.at[a], gt_r.at[a, s], along(a, s))

    expert_row = iota((E, T), 0)
    picked_t = jnp.zeros((E, T), F32)
    for k in range(K):
        picked_t = jnp.where(pick_ref[k : k + 1, :] == expert_row, 1.0, picked_t)
    picked = jnp.transpose(picked_t)
    logits = logit_ref[...]
    top = jnp.max(jnp.where(picked > 0.0, logits, -jnp.inf), axis=1, keepdims=True)
    rwm = jnp.where(picked > 0.0, jnp.exp(jnp.minimum(logits - top, 0.0)), 0.0)
    rwm = rwm / jnp.sum(rwm, axis=1, keepdims=True)
    rwm_ref[...] = rwm
    weight = rwm.astype(BF16)
    earlier = (iota((T, T), 1) < iota((T, T), 0)).astype(BF16)
    code = jnp.where(picked > 0.0, mm(earlier, picked.astype(BF16), NN) + 1.0, 0.0).astype(BF16)
    row, lane = iota((E, E), 0), iota((E, E), 1)
    perm = (expert_at((row & 3, (row >> 2) & 3, (row >> 4) & 3), row >> 6) == lane).astype(BF16)
    perm_ref[...] = perm
    code_rel[...] = mm(perm, code, NT)
    step, core, high, low = row >> 5, (row >> 4) & 1, (row >> 2) & 3, row & 3
    for a in range(AXES):
        place = ((step, low, high), (low, step, high), (low, high, step))[a]
        perm = (expert_at(place, core) == lane).astype(BF16)
        code_a, weight_a = mm(perm, code, NT).astype(BF16), mm(perm, weight, NT).astype(BF16)
        for s in range(LINE):
            home = cw if s else cwg
            home[a, s * 64 : s * 64 + 32, :] = code_a[s * 32 : s * 32 + 32, :]
            home[a, s * 64 + 32 : s * 64 + 64, :] = weight_a[s * 32 : s * 32 + 32, :]
    mb_hot = (mb_ref[...] == iota((8, T), 0)).astype(BF16)
    cnt[0:8, :] = mm(mb_hot, picked.astype(BF16), NN)
    for s in (1, 3, 2):
        for a in range(AXES):
            piece = pl.ds(s * 64, 64)
            remote(cw.at[a, piece], cwg.at[a, piece], gw_s.at[a], gw_r.at[a], along(a, s))
    for s in (1, 3):
        for a in range(AXES):
            home = tc[a].at[pl.ds(s * T, T)]
            remote(cot_hbm.at[:, COLS_COT[a]], home, gc_s.at[a], gc_r.at[a, s], along(a, s))

    def pass_on(held, send_sem, recv_sem, chunks):
        for s, begin in ((1, 0), (3, 1)):
            for a in range(AXES):
                await_bytes(held[a].at[pl.ds(s * T, T)], recv_sem.at[a, s])
                lanes = pl.ds(begin * chunks[a] * 64, chunks[a] * 64)
                block, home = held[a].at[pl.ds(s * T, T), lanes], held[a].at[pl.ds(2 * T, T), lanes]
                remote(block, home, send_sem.at[a], recv_sem.at[a, 2], along(a, s))

    for load in loads:
        load.start()

    def count_round(base, others, stage):
        copies = []
        for n in range(others):
            to = (
                ((x + n + 1) % 4, ex, y),
                (x, ex, (y + n + 1) % 4),
                (x, (ex + n + 1) % 8, y),
            )[stage]
            copies.append(
                pltpu.make_async_remote_copy(
                    src_ref=cnt.at[pl.ds(stage * 8, 8)],
                    dst_ref=cnt_in.at[pl.ds((base + n) * 8, 8)],
                    send_sem=cs_sem.at[base + n],
                    recv_sem=cr_sem.at[base + n],
                    device_id=to,
                    device_id_type=MESH,
                )
            )
        for copy in copies:
            copy.start()
        return copies

    def count_sum(copies, base, stage):
        total = cnt[stage * 8 : stage * 8 + 8, :]
        for n, copy in enumerate(copies):
            copy.wait()
            total = total + cnt_in[(base + n) * 8 : (base + n) * 8 + 8, :]
        cnt[stage * 8 + 8 : stage * 8 + 16, :] = total

    copies = count_round(0, 3, 0)

    for load in own:
        load.wait()

    def pack(out, g, q, begin=0, end=ROWS // BLK):
        def block(n, carry):
            tile = pg[rows_of(n, BLK), 0 : q * 128].reshape(BLK, q, 128)
            out[rows_of(g * (ROWS // BLK) + n, BLK * q), :] = tile.reshape(BLK * q, 128)
            return carry

        lax.fori_loop(begin, end, block, 0)

    def unpack(src, g, q, out, out_g, first=0):
        def block(n, carry):
            tile = src[rows_of(g * (ROWS // BLK) + n, BLK * q), :].reshape(BLK, q, 128)
            out[rows_of(out_g * (ROWS // BLK) + n, BLK), first : first + q * 128] = tile.reshape(BLK, q * 128)
            return carry

        lax.fori_loop(0, ROWS // BLK, block, 0)

    def own_message(g, src, dst, q):
        @pl.when(g == 0)
        def _():
            dst[0 : MSG * q, :] = src[0 : MSG * q, :]

    def send_groups(parts, sign):
        def send(n, carry):
            for g, a, src, dst, s_sem, r_sem, q in parts:
                j = g * PER + turn(n)
                piece = rows_of(j, MSG * q)
                remote(src.at[piece], dst.at[piece], s_sem.at[g, a], r_sem.at[g, a], in_plane(a, j, sign))
            return carry

        lax.fori_loop(1, PER, send, 0)
        for g, a, src, dst, s_sem, r_sem, q in parts:
            if g:
                piece = pl.ds(g * ROWS * q, MSG * q)
                to = in_plane(a, g * PER, sign)
                remote(src.at[piece], dst.at[piece], s_sem.at[g, a], r_sem.at[g, a], to)

    def await_group(g, buf, sem, a, q):
        @pl.when(g == 0)
        def _():
            await_bytes(buf.at[pl.ds(MSG * q, (PER - 1) * MSG * q)], sem.at[0, a])

        @pl.when(g > 0)
        def _():
            await_bytes(buf.at[rows_of(g, ROWS * q)], sem.at[g, a])

    slot = (iota((ROWS, T), 0) % CAP + 1).astype(F32)

    def pick_rows(a, g, s):
        pair, j = iota((ROWS, PER), 0), iota((ROWS, PER), 1)
        return jnp.logical_and(pair // MSG == j, pair // CAP % LINE == s).astype(BF16)

    def fill(one_hot, table, q):
        def half(n, carry):
            for c in range(0, q, 4):
                lanes = slice(c * 128, (c + 4) * 128)
                pg[rows_of(n, HALF), lanes] = mm(one_hot(n), table[:, lanes], NN).astype(BF16)
            return carry

        lax.fori_loop(0, 2, half, 0)

    def find_rows(g):
        for a in range(AXES):
            if g == 0:
                await_bytes(cwg.at[a, pl.ds(64, 192)], gw_r.at[a])
            for s in range(LINE):
                found = mm(pick_rows(a, g, s), cwg[a, pl.ds(s * 64 + g * PER, PER), :], NN)
                hot[a][g * ROWS : (g + 1) * ROWS, s * T : (s + 1) * T] = (found == slot).astype(BF16)

    def token_rows(g):
        for a in range(AXES):
            if g == 0:
                await_bytes(tt[a].at[pl.ds(2 * T, T)], gt_r.at[a, 2])
            fill(lambda n: hot[a][rows_of(2 * g + n, HALF), :], tt[a], Q_TOK[a])
            pack(st[a], g, Q_TOK[a])
            own_message(g, st[a], rt[a], Q_TOK[a])
            yield g, a, st[a], rt[a], st_sem, rt_sem, Q_TOK[a]

    def cotangent_rows(g):
        for a in range(AXES):
            for s in range(LINE):
                lanes = slice(s * T, (s + 1) * T)
                scale = mm(pick_rows(a, g, s), cwg[a, pl.ds(s * 64 + 32 + g * PER, PER), :], NN)
                one_hot = hot[a][g * ROWS : (g + 1) * ROWS, lanes].astype(F32)
                xs[0:ROWS, lanes] = (one_hot * scale).astype(BF16)
            if g == 0:
                await_bytes(tc[a].at[pl.ds(2 * T, T)], gc_r.at[a, 2])
            fill(lambda n: xs[rows_of(n, HALF), 0 : LINE * T], tc[a], Q_COT[a])
            pack(sc[a], g, Q_COT[a])
            own_message(g, sc[a], rc[a], Q_COT[a])
        return [(g, a, sc[a], rc[a], sc_sem, rc_sem, Q_COT[a]) for a in range(AXES)]

    pass_on(tt, gt_s, gt_r, Q_TOK)
    find_rows(0)
    pass_on(tc, gc_s, gc_r, Q_COT)
    for part in token_rows(0):
        send_groups([part], 1)
    send_groups(cotangent_rows(0), 1)
    find_rows(1)
    send_groups(list(token_rows(1)), 1)
    send_groups(cotangent_rows(1), 1)

    def order_block(n, carry):
        pair = iota((64, 1), 0) + n * 64
        s_, x_, y_, z_ = pair % CAP, pair // 9 % 4, pair // 36 % 4, pair // 144
        perm_z[rows_of(n, 64), :] = (((y_ * 4 + x_) * 4 + z_) * CAP + s_ == iota((64, ROWS), 1)).astype(BF16)
        return carry

    lax.fori_loop(0, ROWS // 64, order_block, 0)
    pair = iota((SHEET, 1), 0)
    perm_y[...] = ((pair // 9 % 4 * 4 + pair // 36) * CAP + pair % CAP == iota((SHEET, SHEET), 1)).astype(BF16)
    count_sum(copies, 0, 0)
    copies = count_round(3, 3, 1)
    for load in loads:
        load.wait()

    def reorder(a, src, src_col, dst, dst_rows, dst_col, q, dims):
        for c in range(0, q * 128, 256):
            rows, lanes = src(slice(src_col + c, src_col + c + 256)), slice(dst_col + c, dst_col + c + 256)
            if a == 1:
                sheets = [rows[n * SHEET : (n + 1) * SHEET, :] for n in range(ROWS // SHEET)]
                rows = jnp.concatenate([mm(perm_y[...], sheet, dims).astype(BF16) for sheet in sheets], axis=0)
            elif a == 2:
                rows = mm(perm_z[...], rows, dims).astype(BF16)
            dst[dst_rows, lanes] = rows

    collect = (iota((2 * PER, HALF), 1) // CAP == iota((2 * PER, HALF), 0)).astype(BF16)
    slot_lane = (iota((HALF, 128), 0) % CAP == iota((HALF, 128), 1)).astype(F32)

    def arrive(g, out, src, sem, chunks, cols):
        for a in range(AXES):
            await_group(g, src[a], sem, a, chunks[a])
            unpack(src[a], g, chunks[a], pg, 0)
            reorder(a, lambda lanes: pg[:, lanes], 0, out, rows_of(g, ROWS), cols[a].start, chunks[a], NN)

    def send_score(i, carry):
        remote(qs.at[pl.ds(i, 1)], qr.at[pl.ds(i, 1)], qs_sem, qr_sem, any_offset(i, -1))
        return carry

    def send_last(g):
        def send(n, carry):
            j = g * PER + turn(n)
            piece = rows_of(j, MSG * Q_PAIR[2])
            remote(ps[2].at[piece], pr[2].at[piece], ps_sem.at[g, 2], pr_sem.at[g, 2], in_plane(2, j, -1))
            return carry

        lax.fori_loop(1, PER, send, 0, unroll=5)
        if g:
            send(0, 0)

    def expert(g, carry):
        arrive(g, xs, rt, rt_sem, Q_TOK, COLS_TOK)

        def forward(n, carry):
            part = rows_of(2 * g + n, HALF)
            for h in range(H // 256):
                cols = slice(h * 256, (h + 1) * 256)
                pre_gate = mm(xs[part, :], wg[:, cols], NN)
                pre_up = mm(xs[part, :], wu[:, cols], NN)
                logistic = jax.nn.sigmoid(pre_gate)
                act = pre_gate * logistic
                deriv = logistic * (1.0 + pre_gate * (1.0 - logistic))
                hid[part, cols] = (act * pre_up).astype(BF16)
                gu[part, cols] = (pre_up * deriv).astype(BF16)
                gu[part, h * 256 + H : (h + 1) * 256 + H] = act.astype(BF16)
            return carry

        lax.fori_loop(0, 2, forward, 0)
        arrive(g, cs, rc, rc_sem, Q_COT, COLS_COT)
        @pl.when(g == 1)
        def _():
            send_last(0)

        for a in range(AXES):
            await_group(g, st[PAIR_HOME[a]], st_sem, PAIR_HOME[a], Q_PAIR[a])

        def pair_rows(part, lanes):
            rows = mm(gu[part, 0:H], wg[lanes, :], NT) + mm(gu[part, H : 2 * H], wu[lanes, :], NT)
            return rows.astype(BF16)

        def send_pair(a, j):
            piece = rows_of(j, MSG * Q_PAIR[a])
            remote(ps[a].at[piece], pr[a].at[piece], ps_sem.at[g, a], pr_sem.at[g, a], in_plane(a, j, -1))

        def backward(n, carry):
            part = rows_of(2 * g + n, HALF)
            score = jnp.zeros((HALF, 1), F32)
            for h in range(H // 256):
                cols, more = slice(h * 256, (h + 1) * 256), slice(h * 256 + H, (h + 1) * 256 + H)
                back = mm(cs[part, :], wd[cols, :], NT)
                score = score + jnp.sum(hid[part, cols].astype(F32) * back, axis=1, keepdims=True)
                gu[part, cols] = (back * gu[part, cols].astype(F32)).astype(BF16)
                gu[part, more] = (back * gu[part, more].astype(F32)).astype(BF16)
            for a in (1, 0):
                q, first = Q_PAIR[a], COLS_PAIR[a].start
                for c in range(0, q * 128, 256):
                    rows = pair_rows(part, slice(first + c, first + c + 256))
                    if a == 1:
                        sheets = [rows[m * SHEET : (m + 1) * SHEET, :] for m in range(HALF // SHEET)]
                        sheets = [mm(perm_y[...], sheet, TN).astype(BF16) for sheet in sheets]
                        rows = jnp.concatenate(sheets, axis=0)
                    pg[rows_of(n, HALF), c : c + 256] = rows
                pack(ps[a], g, q, n * (HALF // BLK), (n + 1) * (HALF // BLK))

                @pl.when(g + n == 0)
                def _():
                    pr[a][0 : MSG * q, :] = ps[a][0 : MSG * q, :]

                def send(m, carry):
                    low = rem(m, 4)
                    send_pair(a, g * PER + (2 * n + rem(low + quot(m, 4), 2)) * 4 + low)
                    return carry

                pl.when(g + n > 0)(lambda: send(0, None))
                lax.fori_loop(1, PER // 2, send, 0, unroll=True)
            score_rows = mm(collect, (score * slot_lane).astype(BF16), NN)
            for i in range(2 * PER):
                qs[(2 * g + n) * 2 * PER + i] = score_rows[i : i + 1, :]
            return carry

        lax.fori_loop(0, 2, backward, 0)
        part = rows_of(g, ROWS)
        first = COLS_PAIR[2].start
        reorder(2, lambda lanes: pair_rows(part, lanes), first, pg, slice(0, ROWS), 0, Q_PAIR[2], TN)
        pack(ps[2], g, Q_PAIR[2])
        own_message(g, ps[2], pr[2], Q_PAIR[2])

        @pl.when(g == 1)
        def _():
            send_last(1)

        @pl.when(g == 0)
        def _():
            qr[0] = qs[0]

        lax.fori_loop(jnp.where(g == 0, 1, g * 4 * PER), (g + 1) * 4 * PER, send_score, 0)
        return carry

    lax.fori_loop(0, GROUPS, expert, 0)
    count_sum(copies, 3, 1)
    copies = count_round(6, 7, 2)

    def in_copies(n, buf):
        rows = rows_of(n, 256)
        return (
            pltpu.make_async_copy(out_buf.at[buf, :, pl.ds(0, H)], gg_hbm.at[rows], oa_sem.at[buf, 0]),
            pltpu.make_async_copy(out_buf.at[buf, :, pl.ds(H, H)], gu_hbm.at[rows], oa_sem.at[buf, 1]),
        )

    def grad_in(n, carry):
        buf = n % 2

        @pl.when(n >= 2)
        def _():
            for copy in in_copies(n - 2, buf):
                copy.wait()

        turned = jnp.transpose(xs[:, rows_of(n, 256)])
        for part in (slice(0, H), slice(H, 2 * H)):
            out_buf[buf, :, part] = mm(turned, gu[:, part], NN).astype(BF16)
        for copy in in_copies(n, buf):
            copy.start()
        return carry

    lax.fori_loop(0, D // 256, grad_in, 0)
    for n in (D // 256 - 2, D // 256 - 1):
        for copy in in_copies(n, n % 2):
            copy.wait()

    for a in range(AXES):
        await_group(0, pr[a], pr_sem, a, Q_PAIR[a])
        unpack(pr[a], 0, Q_PAIR[a], xs, 0, COLS_PAIR[a].start)
    for a in range(AXES):
        q = Q_PAIR[a]
        await_group(1, pr[a], pr_sem, a, q)
        unpack(pr[a], 1, q, xs, 1, COLS_PAIR[a].start)
        home = PAIR_HOME[a]
        await_bytes(tt[home].at[pl.ds(T, 3 * T)], gt_s.at[home])
        for c in range(0, q, 4):
            lanes, cols = slice(c * 128, (c + 4) * 128), pl.ds(COLS_PAIR[a].start + c * 128, 512)
            fs[a][:, lanes] = mm(hot[a][...], xs[:, cols], TN).astype(BF16)
        for s in (1, 3, 2):
            piece = fr[a].at[pl.ds((s - 1) * T, T)]
            remote(fs[a].at[pl.ds(s * T, T)], piece, fs_sem.at[a], fr_sem.at[a], along(a, s, -1))

    def down_copy(n, buf):
        place = gd_hbm.at[rows_of(n // 2, 256), rows_of(n % 2, D // 2)]
        return pltpu.make_async_copy(out_buf.at[buf, :, pl.ds(0, D // 2)], place, od_sem.at[buf])

    def grad_out(n, carry):
        buf = n % 2

        @pl.when(n >= 2)
        def _():
            down_copy(n - 2, buf).wait()

        rows = mm(hid[:, rows_of(n // 2, 256)], cs[:, rows_of(n % 2, D // 2)], TN)
        out_buf[buf, :, 0 : D // 2] = rows.astype(BF16)
        down_copy(n, buf).start()
        return carry

    lax.fori_loop(0, H // 128, grad_out, 0)

    prob = jnp.exp(logit_ref[...] - jnp.max(logit_ref[...], axis=1, keepdims=True))
    prob = prob / jnp.sum(prob, axis=1, keepdims=True)
    count_sum(copies, 6, 2)
    load = cnt[24:32, :] * (E * MICRO / (K * T * E))
    batch_col = jnp.transpose((mb_ref[...] == iota((T, T), 0)).astype(F32))[:, 1:2]
    token_load = jnp.where(batch_col > 0.0, load[1:2, :], load[0:1, :])
    gb_ref[...] = prob * (token_load - jnp.sum(prob * token_load, axis=1, keepdims=True))

    await_bytes(qr.at[pl.ds(1, E - 1)], qr_sem)
    q_all = jnp.concatenate([qr[i] for i in range(E)], axis=0)
    q_rel = jnp.zeros((E, T), F32)
    for s in range(CAP):
        q_rel = jnp.where(code_rel[...] == float(s + 1), q_all[:, s : s + 1], q_rel)
    q_own = mm(q_rel.astype(BF16), perm_ref[...], TN)
    gl_ref[...] = q_own - rwm_ref[...] * jnp.sum(q_own, axis=1, keepdims=True)

    for a in range(AXES):
        await_bytes(fr[a], fr_sem.at[a])
        total = fs[a][0:T, :].astype(F32)
        for s in range(LINE - 1):
            total = total + fr[a][s * T : (s + 1) * T, :].astype(F32)
        gt_ref[:, COLS_PAIR[a]] = total.astype(BF16)

    for n in (H // 128 - 2, H // 128 - 1):
        down_copy(n, n % 2).wait()
    for a in range(AXES):
        await_bytes(tc[a].at[pl.ds(T, 3 * T)], gc_s.at[a])
        await_bytes(cw.at[a, pl.ds(64, 192)], gw_s.at[a])
        await_bytes(fr[a], fs_sem.at[a])
        for g in range(GROUPS):
            await_group(g, sc[a], sc_sem, a, Q_COT[a])
            await_group(g, ps[a], ps_sem, a, Q_PAIR[a])
    await_bytes(qs.at[pl.ds(1, E - 1)], qs_sem)


def settle_kernel(*refs):
    sources, targets, sem, held = refs[:6], refs[6:12], refs[12], refs[13:]
    copies = []
    for src, dst, buf in zip(sources, targets, held):
        pieces = 8 if src.shape[0] > T else 1
        size = src.shape[0] // pieces
        for n in range(pieces):
            rows = pl.ds(n * size, size)
            m = len(copies)
            copies.append(
                (
                    pltpu.make_async_copy(src.at[rows], buf.at[rows], sem.at[0, m]),
                    pltpu.make_async_copy(buf.at[rows], dst.at[rows], sem.at[1, m]),
                )
            )
    for fetch, _ in copies:
        fetch.start()
    for fetch, store in copies:
        fetch.wait()
        store.start()
    for _, store in copies:
        store.wait()


def settle(outs):
    hbm = pl.BlockSpec(memory_space=pl.ANY)
    return pl.pallas_call(
        settle_kernel,
        out_shape=tuple(jax.ShapeDtypeStruct(o.shape, o.dtype) for o in outs),
        in_specs=[hbm] * 6,
        out_specs=(hbm,) * 6,
        scratch_shapes=[pltpu.SemaphoreType.DMA((2, 27))] + [pltpu.VMEM(o.shape, o.dtype) for o in outs],
        compiler_params=pltpu.CompilerParams(vmem_limit_bytes=60 * 2**20),
        name="settle",
    )(*outs)


def per_device(tokens, out_grad, router_logits, expert_picks, micro_batch, w_gate, w_up, w_down):
    vmem, hbm = pl.BlockSpec(memory_space=pltpu.VMEM), pl.BlockSpec(memory_space=pl.ANY)
    dma = pltpu.SemaphoreType.DMA

    def sliced(rows, chunks):
        return [pltpu.VMEM((rows * q, 128), BF16) for q in chunks]

    outs = pl.pallas_call(
        kernel,
        out_shape=(
            jax.ShapeDtypeStruct((T, D), BF16),
            jax.ShapeDtypeStruct((T, E), F32),
            jax.ShapeDtypeStruct((T, E), F32),
            jax.ShapeDtypeStruct((D, H), BF16),
            jax.ShapeDtypeStruct((D, H), BF16),
            jax.ShapeDtypeStruct((H, D), BF16),
        ),
        in_specs=[hbm] * 2 + [vmem] * 3 + [hbm] * 3,
        out_specs=(vmem,) * 3 + (hbm,) * 3,
        scratch_shapes=[
            *sliced(PAIRS, Q_TOK), *sliced(PAIRS, Q_COT),
            *sliced(PAIRS, Q_TOK), *sliced(PAIRS, Q_COT), *sliced(PAIRS, Q_PAIR),
            *[pltpu.VMEM((LINE * T, q * 128), BF16) for q in Q_TOK],
            *[pltpu.VMEM((LINE * T, q * 128), BF16) for q in Q_COT],
            *[pltpu.VMEM((PAIRS, LINE * T), BF16)] * AXES,
            *[pltpu.VMEM((3 * T, q * 128), BF16) for q in Q_PAIR],
            pltpu.VMEM((SHEET, SHEET), BF16), pltpu.VMEM((ROWS, ROWS), BF16),
            *[pltpu.VMEM((PAIRS, D), BF16)] * 2,
            pltpu.VMEM((PAIRS, H), BF16),
            pltpu.VMEM((PAIRS, 2 * H), BF16),
            pltpu.VMEM((D, H), BF16),
            pltpu.VMEM((D, H), BF16),
            pltpu.VMEM((H, D), BF16),
            pltpu.VMEM((ROWS, 1024), BF16),
            pltpu.VMEM((2, 256, 2 * H), BF16),
            pltpu.VMEM((AXES, 256, T), BF16),
            pltpu.VMEM((AXES, 256, T), BF16),
            pltpu.VMEM((E, T), F32),
            pltpu.VMEM((E, E), BF16),
            pltpu.VMEM((T, E), F32),
            pltpu.VMEM((E, 1, 128), F32),
            pltpu.VMEM((E, 1, 128), F32),
            pltpu.VMEM((32, E), F32),
            pltpu.VMEM((13 * 8, E), F32),
            dma((3,)),
            dma((2, AXES)),
            dma((AXES,)), dma((AXES, LINE)), dma((AXES,)), dma((AXES, LINE)), dma((AXES,)), dma((AXES,)),
            *[dma((GROUPS, AXES))] * 6,
            *[dma((AXES,))] * 2,
            dma, dma, dma((13,)), dma((13,)), dma((2, 2)), dma((2,)),
        ],
        compiler_params=pltpu.CompilerParams(
            collective_id=0, has_side_effects=True, vmem_limit_bytes=64 * 2**20
        ),
        name="expert_backward",
    )(tokens, out_grad, router_logits, expert_picks.T, micro_batch.reshape(1, T), w_gate[0], w_up[0], w_down[0])
    grad_tokens, grad_logits, balance_grad, grad_gate, grad_up, grad_down = settle(outs)
    return grad_tokens, grad_logits, balance_grad, grad_gate[None], grad_up[None], grad_down[None]


def solution(mesh):
    rows, cube = P(("dp", "ex", "ey"), None), P(("dp", "ex", "ey"), None, None)
    return jax.shard_map(
        per_device,
        mesh=mesh,
        in_specs=(rows, rows, rows, rows, P(("dp", "ex", "ey")), cube, cube, cube),
        out_specs=(rows, rows, rows, cube, cube, cube),
        check_vma=False,
    )
```

```python
import jax
import jax.numpy as jnp
from jax import lax
from jax.experimental import pallas as pl
from jax.experimental.pallas import tpu as pltpu
from jax.sharding import PartitionSpec as P

MESH = pl.DeviceIdType.MESH
F32, BF16, I32 = jnp.float32, jnp.bfloat16, jnp.int32
NN = (((1,), (0,)), ((), ()))
NT = (((1,), (1,)), ((), ()))
TN = (((0,), (0,)), ((), ()))

D, H, K, T, E, CAP, MICRO = 2048, 768, 8, 128, 128, 9, 2
AXES = 3
LINE = 4
PLANE = E // LINE
GROUPS = 2
PER = PLANE // GROUPS
MSG = LINE * CAP
ROWS = PER * MSG
PAIRS = E * CAP
HALF = ROWS // 2
SHEET = LINE * MSG
BLK = 32
Q_TOK, Q_COT, Q_PAIR = (4, 4, 8), (4, 8, 4), (8, 4, 4)


def slices(chunks):
    starts = [sum(chunks[:a]) * 128 for a in range(AXES)]
    return [slice(s, s + q * 128) for s, q in zip(starts, chunks)]


COLS_TOK, COLS_COT, COLS_PAIR = slices(Q_TOK), slices(Q_COT), slices(Q_PAIR)
PAIR_HOME = (2, 1, 0)


def mm(a, b, dims):
    return lax.dot_general(a, b, dims, preferred_element_type=F32)


def rows_of(g, size):
    return pl.ds(pl.multiple_of(g * size, size), size)


def iota(shape, dim):
    return lax.broadcasted_iota(I32, shape, dim)


def rem(value, size):
    return lax.rem(value, jnp.int32(size)) if isinstance(value, jax.Array) else value % size


def quot(value, size):
    return lax.div(value, jnp.int32(size)) if isinstance(value, jax.Array) else value // size


def moved(steps, dc, sign=1):
    x, ex, y = lax.axis_index("dp"), lax.axis_index("ex"), lax.axis_index("ey")
    z, core = quot(ex, 2), rem(ex, 2)
    side = core if sign == 1 else rem(core + dc, 2)
    dx, dy, dz = axes_of(steps, side)
    if sign == -1:
        dx, dy, dz = 4 - dx, 4 - dy, 4 - dz
    return rem(x + dx, 4), rem(z + dz, 4) * 2 + rem(core + dc, 2), rem(y + dy, 4)


def axes_of(steps, side):
    a, b, c = steps
    return a + side * (c - a), b + side * (a - b), c + side * (b - c)


def along(axis, step, sign=1):
    return moved([step if axis == n else 0 for n in range(AXES)], 0, sign)


def in_plane(axis, j, sign=1):
    core, high, low = quot(j, 16), rem(quot(j, 4), 4), rem(j, 4)
    return moved(((0, low, high), (low, 0, high), (low, high, 0))[axis], core, sign)


def any_offset(i, sign=1):
    return moved((rem(i, 4), rem(quot(i, 4), 4), rem(quot(i, 16), 4)), quot(i, 64), sign)


def turn(n):
    return rem(rem(n, 4) + quot(n, 4), 4) * 4 + rem(n, 4)


def expert_at(steps, dc):
    x, ex, y = lax.axis_index("dp"), lax.axis_index("ex"), lax.axis_index("ey")
    dx, dy, dz = axes_of(steps, ex % 2)
    return ((x + dx) & 3) * 32 + ((((ex // 2) + dz) & 3) * 2 + (((ex % 2) + dc) & 1)) * 4 + ((y + dy) & 3)


def kernel(
    tok_hbm, cot_hbm, logit_ref, pick_ref, mb_ref, wg_hbm, wu_hbm, wd_hbm,
    gt_ref, gl_ref, gb_ref, gg_hbm, gu_hbm, gd_hbm,
    st0, st1, st2, sc0, sc1, sc2, rt0, rt1, rt2, rc0, rc1, rc2, pr0, pr1, pr2,
    tt0, tt1, tt2, tc0, tc1, tc2, hot0, hot1, hot2, fr0, fr1, fr2, perm_y, perm_z,
    xs, cs, hid, gu, wg, wu, wd, pg, out_buf, cw, cwg, code_rel, perm_ref, rwm_ref, qs, qr, cnt, cnt_in,
    w_sem, own_sem, gt_s, gt_r, gc_s, gc_r, gw_s, gw_r, st_sem, sc_sem, rt_sem, rc_sem, ps_sem, pr_sem, fs_sem, fr_sem,
    qs_sem, qr_sem, cs_sem, cr_sem, oa_sem, od_sem,
):
    x, ex, y = lax.axis_index("dp"), lax.axis_index("ex"), lax.axis_index("ey")
    st, sc, rt, rc, pr = (st0, st1, st2), (sc0, sc1, sc2), (rt0, rt1, rt2), (rc0, rc1, rc2), (pr0, pr1, pr2)
    tt, tc, hot, fr = (tt0, tt1, tt2), (tc0, tc1, tc2), (hot0, hot1, hot2), (fr0, fr1, fr2)
    ps = tuple(st[n] for n in PAIR_HOME)
    fs = tuple(tt[n] for n in PAIR_HOME)
    barrier = pltpu.get_barrier_semaphore()

    ys = [rem(y + n, 4) for n in range(4)]
    exs = [rem(quot(ex, 2) + n, 4) * 2 + c for n in range(4) for c in (rem(ex, 2), rem(ex + 1, 2))]

    def greet(n, carry):
        to_x = rem(x + n, 4)
        for m in range(1, 32):
            to = (to_x, exs[m // 4], ys[m % 4])
            pl.semaphore_signal(barrier, inc=1, device_id=to, device_id_type=MESH)
        return carry

    lax.fori_loop(0, 4, greet, 0)
    for n in range(1, 4):
        pl.semaphore_signal(barrier, inc=1, device_id=(rem(x + n, 4), ex, y), device_id_type=MESH)
    loads = [
        pltpu.make_async_copy(src, dst, w_sem.at[n])
        for n, (src, dst) in enumerate(((wg_hbm, wg), (wu_hbm, wu), (wd_hbm, wd)))
    ]
    own = []
    for a in range(AXES):
        own.append(pltpu.make_async_copy(tok_hbm.at[:, COLS_TOK[a]], tt[a].at[pl.ds(0, T)], own_sem.at[0, a]))
        own.append(pltpu.make_async_copy(cot_hbm.at[:, COLS_COT[a]], tc[a].at[pl.ds(0, T)], own_sem.at[1, a]))
    for load in own:
        load.start()

    def remote(src, dst, send_sem, recv_sem, to):
        pltpu.make_async_remote_copy(
            src_ref=src, dst_ref=dst, send_sem=send_sem, recv_sem=recv_sem, device_id=to, device_id_type=MESH
        ).start()

    def await_bytes(piece, sem):
        pltpu.make_async_copy(piece, piece, sem).wait()

    pl.semaphore_wait(barrier, E - 1)
    for s in (1, 3):
        for a in range(AXES):
            home = tt[a].at[pl.ds(s * T, T)]
            remote(tok_hbm.at[:, COLS_TOK[a]], home, gt_s.at[a], gt_r.at[a, s], along(a, s))

    expert_row = iota((E, T), 0)
    picked_t = jnp.zeros((E, T), F32)
    for k in range(K):
        picked_t = jnp.where(pick_ref[k : k + 1, :] == expert_row, 1.0, picked_t)
    picked = jnp.transpose(picked_t)
    logits = logit_ref[...]
    top = jnp.max(jnp.where(picked > 0.0, logits, -jnp.inf), axis=1, keepdims=True)
    rwm = jnp.where(picked > 0.0, jnp.exp(jnp.minimum(logits - top, 0.0)), 0.0)
    rwm = rwm / jnp.sum(rwm, axis=1, keepdims=True)
    rwm_ref[...] = rwm
    weight = rwm.astype(BF16)
    earlier = (iota((T, T), 1) < iota((T, T), 0)).astype(BF16)
    code = jnp.where(picked > 0.0, mm(earlier, picked.astype(BF16), NN) + 1.0, 0.0).astype(BF16)
    row, lane = iota((E, E), 0), iota((E, E), 1)
    perm = (expert_at((row & 3, (row >> 2) & 3, (row >> 4) & 3), row >> 6) == lane).astype(BF16)
    perm_ref[...] = perm
    code_rel[...] = mm(perm, code, NT)
    step, core, high, low = row >> 5, (row >> 4) & 1, (row >> 2) & 3, row & 3
    for a in range(AXES):
        place = ((step, low, high), (low, step, high), (low, high, step))[a]
        perm = (expert_at(place, core) == lane).astype(BF16)
        code_a, weight_a = mm(perm, code, NT).astype(BF16), mm(perm, weight, NT).astype(BF16)
        for s in range(LINE):
            home = cw if s else cwg
            home[a, s * 64 : s * 64 + 32, :] = code_a[s * 32 : s * 32 + 32, :]
            home[a, s * 64 + 32 : s * 64 + 64, :] = weight_a[s * 32 : s * 32 + 32, :]
    mb_hot = (mb_ref[...] == iota((8, T), 0)).astype(BF16)
    cnt[0:8, :] = mm(mb_hot, picked.astype(BF16), NN)
    for s in (1, 3, 2):
        for a in range(AXES):
            piece = pl.ds(s * 64, 64)
            remote(cw.at[a, piece], cwg.at[a, piece], gw_s.at[a], gw_r.at[a], along(a, s))
    for s in (1, 3):
        for a in range(AXES):
            home = tc[a].at[pl.ds(s * T, T)]
            remote(cot_hbm.at[:, COLS_COT[a]], home, gc_s.at[a], gc_r.at[a, s], along(a, s))

    def pass_on(held, send_sem, recv_sem, chunks):
        for s, begin in ((1, 0), (3, 1)):
            for a in range(AXES):
                await_bytes(held[a].at[pl.ds(s * T, T)], recv_sem.at[a, s])
                lanes = pl.ds(begin * chunks[a] * 64, chunks[a] * 64)
                block, home = held[a].at[pl.ds(s * T, T), lanes], held[a].at[pl.ds(2 * T, T), lanes]
                remote(block, home, send_sem.at[a], recv_sem.at[a, 2], along(a, s))

    for load in loads:
        load.start()

    def count_round(base, others, stage):
        copies = []
        for n in range(others):
            to = (
                ((x + n + 1) % 4, ex, y),
                (x, ex, (y + n + 1) % 4),
                (x, (ex + n + 1) % 8, y),
            )[stage]
            copies.append(
                pltpu.make_async_remote_copy(
                    src_ref=cnt.at[pl.ds(stage * 8, 8)],
                    dst_ref=cnt_in.at[pl.ds((base + n) * 8, 8)],
                    send_sem=cs_sem.at[base + n],
                    recv_sem=cr_sem.at[base + n],
                    device_id=to,
                    device_id_type=MESH,
                )
            )
        for copy in copies:
            copy.start()
        return copies

    def count_sum(copies, base, stage):
        total = cnt[stage * 8 : stage * 8 + 8, :]
        for n, copy in enumerate(copies):
            copy.wait()
            total = total + cnt_in[(base + n) * 8 : (base + n) * 8 + 8, :]
        cnt[stage * 8 + 8 : stage * 8 + 16, :] = total

    copies = count_round(0, 3, 0)

    for load in own:
        load.wait()

    def pack(out, g, q, begin=0, end=ROWS // BLK):
        def block(n, carry):
            tile = pg[rows_of(n, BLK), 0 : q * 128].reshape(BLK, q, 128)
            out[rows_of(g * (ROWS // BLK) + n, BLK * q), :] = tile.reshape(BLK * q, 128)
            return carry

        lax.fori_loop(begin, end, block, 0)

    def unpack(src, g, q, out, out_g, first=0):
        def block(n, carry):
            tile = src[rows_of(g * (ROWS // BLK) + n, BLK * q), :].reshape(BLK, q, 128)
            out[rows_of(out_g * (ROWS // BLK) + n, BLK), first : first + q * 128] = tile.reshape(BLK, q * 128)
            return carry

        lax.fori_loop(0, ROWS // BLK, block, 0)

    def own_message(g, src, dst, q):
        @pl.when(g == 0)
        def _():
            dst[0 : MSG * q, :] = src[0 : MSG * q, :]

    def send_groups(parts, sign):
        def send(n, carry):
            for g, a, src, dst, s_sem, r_sem, q in parts:
                j = g * PER + turn(n)
                piece = rows_of(j, MSG * q)
                remote(src.at[piece], dst.at[piece], s_sem.at[g, a], r_sem.at[g, a], in_plane(a, j, sign))
            return carry

        lax.fori_loop(1, PER, send, 0)
        for g, a, src, dst, s_sem, r_sem, q in parts:
            if g:
                piece = pl.ds(g * ROWS * q, MSG * q)
                to = in_plane(a, g * PER, sign)
                remote(src.at[piece], dst.at[piece], s_sem.at[g, a], r_sem.at[g, a], to)

    def await_group(g, buf, sem, a, q):
        @pl.when(g == 0)
        def _():
            await_bytes(buf.at[pl.ds(MSG * q, (PER - 1) * MSG * q)], sem.at[0, a])

        @pl.when(g > 0)
        def _():
            await_bytes(buf.at[rows_of(g, ROWS * q)], sem.at[g, a])

    slot = (iota((ROWS, T), 0) % CAP + 1).astype(F32)

    def pick_rows(a, g, s):
        pair, j = iota((ROWS, PER), 0), iota((ROWS, PER), 1)
        return jnp.logical_and(pair // MSG == j, pair // CAP % LINE == s).astype(BF16)

    def fill(one_hot, table, q):
        def half(n, carry):
            for c in range(0, q, 4):
                lanes = slice(c * 128, (c + 4) * 128)
                pg[rows_of(n, HALF), lanes] = mm(one_hot(n), table[:, lanes], NN).astype(BF16)
            return carry

        lax.fori_loop(0, 2, half, 0)

    def find_rows(g):
        for a in range(AXES):
            if g == 0:
                await_bytes(cwg.at[a, pl.ds(64, 192)], gw_r.at[a])
            for s in range(LINE):
                found = mm(pick_rows(a, g, s), cwg[a, pl.ds(s * 64 + g * PER, PER), :], NN)
                hot[a][g * ROWS : (g + 1) * ROWS, s * T : (s + 1) * T] = (found == slot).astype(BF16)

    def token_rows(g):
        for a in range(AXES):
            if g == 0:
                await_bytes(tt[a].at[pl.ds(2 * T, T)], gt_r.at[a, 2])
            fill(lambda n: hot[a][rows_of(2 * g + n, HALF), :], tt[a], Q_TOK[a])
            pack(st[a], g, Q_TOK[a])
            own_message(g, st[a], rt[a], Q_TOK[a])
            yield g, a, st[a], rt[a], st_sem, rt_sem, Q_TOK[a]

    def cotangent_rows(g):
        for a in range(AXES):
            for s in range(LINE):
                lanes = slice(s * T, (s + 1) * T)
                scale = mm(pick_rows(a, g, s), cwg[a, pl.ds(s * 64 + 32 + g * PER, PER), :], NN)
                one_hot = hot[a][g * ROWS : (g + 1) * ROWS, lanes].astype(F32)
                xs[0:ROWS, lanes] = (one_hot * scale).astype(BF16)
            if g == 0:
                await_bytes(tc[a].at[pl.ds(2 * T, T)], gc_r.at[a, 2])
            fill(lambda n: xs[rows_of(n, HALF), 0 : LINE * T], tc[a], Q_COT[a])
            pack(sc[a], g, Q_COT[a])
            own_message(g, sc[a], rc[a], Q_COT[a])
        return [(g, a, sc[a], rc[a], sc_sem, rc_sem, Q_COT[a]) for a in range(AXES)]

    pass_on(tt, gt_s, gt_r, Q_TOK)
    find_rows(0)
    pass_on(tc, gc_s, gc_r, Q_COT)
    for part in token_rows(0):
        send_groups([part], 1)
    send_groups(cotangent_rows(0), 1)
    find_rows(1)
    send_groups(list(token_rows(1)), 1)
    send_groups(cotangent_rows(1), 1)

    def order_block(n, carry):
        pair = iota((64, 1), 0) + n * 64
        s_, x_, y_, z_ = pair % CAP, pair // 9 % 4, pair // 36 % 4, pair // 144
        perm_z[rows_of(n, 64), :] = (((y_ * 4 + x_) * 4 + z_) * CAP + s_ == iota((64, ROWS), 1)).astype(BF16)
        return carry

    lax.fori_loop(0, ROWS // 64, order_block, 0)
    pair = iota((SHEET, 1), 0)
    perm_y[...] = ((pair // 9 % 4 * 4 + pair // 36) * CAP + pair % CAP == iota((SHEET, SHEET), 1)).astype(BF16)
    count_sum(copies, 0, 0)
    copies = count_round(3, 3, 1)
    for load in loads:
        load.wait()

    def reorder(a, src, src_col, dst, dst_rows, dst_col, q, dims):
        for c in range(0, q * 128, 256):
            rows, lanes = src(slice(src_col + c, src_col + c + 256)), slice(dst_col + c, dst_col + c + 256)
            if a == 1:
                sheets = [rows[n * SHEET : (n + 1) * SHEET, :] for n in range(ROWS // SHEET)]
                rows = jnp.concatenate([mm(perm_y[...], sheet, dims).astype(BF16) for sheet in sheets], axis=0)
            elif a == 2:
                rows = mm(perm_z[...], rows, dims).astype(BF16)
            dst[dst_rows, lanes] = rows

    collect = (iota((2 * PER, HALF), 1) // CAP == iota((2 * PER, HALF), 0)).astype(BF16)
    slot_lane = (iota((HALF, 128), 0) % CAP == iota((HALF, 128), 1)).astype(F32)

    def arrive(g, out, src, sem, chunks, cols):
        for a in range(AXES):
            await_group(g, src[a], sem, a, chunks[a])
            unpack(src[a], g, chunks[a], pg, 0)
            reorder(a, lambda lanes: pg[:, lanes], 0, out, rows_of(g, ROWS), cols[a].start, chunks[a], NN)

    def send_score(i, carry):
        remote(qs.at[pl.ds(i, 1)], qr.at[pl.ds(i, 1)], qs_sem, qr_sem, any_offset(i, -1))
        return carry

    def send_last(g):
        def send(n, carry):
            j = g * PER + turn(n)
            piece = rows_of(j, MSG * Q_PAIR[2])
            remote(ps[2].at[piece], pr[2].at[piece], ps_sem.at[g, 2], pr_sem.at[g, 2], in_plane(2, j, -1))
            return carry

        lax.fori_loop(1, PER, send, 0, unroll=5)
        if g:
            send(0, 0)

    def expert(g, carry):
        arrive(g, xs, rt, rt_sem, Q_TOK, COLS_TOK)

        def forward(n, carry):
            part = rows_of(2 * g + n, HALF)
            for h in range(H // 256):
                cols = slice(h * 256, (h + 1) * 256)
                pre_gate = mm(xs[part, :], wg[:, cols], NN)
                pre_up = mm(xs[part, :], wu[:, cols], NN)
                logistic = jax.nn.sigmoid(pre_gate)
                act = pre_gate * logistic
                deriv = logistic * (1.0 + pre_gate * (1.0 - logistic))
                hid[part, cols] = (act * pre_up).astype(BF16)
                gu[part, cols] = (pre_up * deriv).astype(BF16)
                gu[part, h * 256 + H : (h + 1) * 256 + H] = act.astype(BF16)
            return carry

        lax.fori_loop(0, 2, forward, 0)

        @pl.when(g == 1)
        def _():
            send_last(0)

        arrive(g, cs, rc, rc_sem, Q_COT, COLS_COT)
        for a in range(AXES):
            await_group(g, st[PAIR_HOME[a]], st_sem, PAIR_HOME[a], Q_PAIR[a])

        def pair_rows(part, lanes):
            rows = mm(gu[part, 0:H], wg[lanes, :], NT) + mm(gu[part, H : 2 * H], wu[lanes, :], NT)
            return rows.astype(BF16)

        def send_pair(a, j):
            piece = rows_of(j, MSG * Q_PAIR[a])
            remote(ps[a].at[piece], pr[a].at[piece], ps_sem.at[g, a], pr_sem.at[g, a], in_plane(a, j, -1))

        def backward(n, carry):
            part = rows_of(2 * g + n, HALF)
            score = jnp.zeros((HALF, 1), F32)
            for h in range(H // 256):
                cols, more = slice(h * 256, (h + 1) * 256), slice(h * 256 + H, (h + 1) * 256 + H)
                back = mm(cs[part, :], wd[cols, :], NT)
                score = score + jnp.sum(hid[part, cols].astype(F32) * back, axis=1, keepdims=True)
                gu[part, cols] = (back * gu[part, cols].astype(F32)).astype(BF16)
                gu[part, more] = (back * gu[part, more].astype(F32)).astype(BF16)
            for a in (1, 0):
                q, first = Q_PAIR[a], COLS_PAIR[a].start
                for c in range(0, q * 128, 256):
                    rows = pair_rows(part, slice(first + c, first + c + 256))
                    if a == 1:
                        sheets = [rows[m * SHEET : (m + 1) * SHEET, :] for m in range(HALF // SHEET)]
                        sheets = [mm(perm_y[...], sheet, TN).astype(BF16) for sheet in sheets]
                        rows = jnp.concatenate(sheets, axis=0)
                    pg[rows_of(n, HALF), c : c + 256] = rows
                pack(ps[a], g, q, n * (HALF // BLK), (n + 1) * (HALF // BLK))

                @pl.when(g + n == 0)
                def _():
                    pr[a][0 : MSG * q, :] = ps[a][0 : MSG * q, :]

                def send(m, carry):
                    low = rem(m, 4)
                    send_pair(a, g * PER + (2 * n + rem(low + quot(m, 4), 2)) * 4 + low)
                    return carry

                pl.when(g + n > 0)(lambda: send(0, None))
                lax.fori_loop(1, PER // 2, send, 0, unroll=True)
            score_rows = mm(collect, (score * slot_lane).astype(BF16), NN)
            for i in range(2 * PER):
                qs[(2 * g + n) * 2 * PER + i] = score_rows[i : i + 1, :]
            return carry

        lax.fori_loop(0, 2, backward, 0)
        part = rows_of(g, ROWS)
        first = COLS_PAIR[2].start
        reorder(2, lambda lanes: pair_rows(part, lanes), first, pg, slice(0, ROWS), 0, Q_PAIR[2], TN)
        pack(ps[2], g, Q_PAIR[2])
        own_message(g, ps[2], pr[2], Q_PAIR[2])

        @pl.when(g == 1)
        def _():
            send_last(1)

        @pl.when(g == 0)
        def _():
            qr[0] = qs[0]

        lax.fori_loop(jnp.where(g == 0, 1, g * 4 * PER), (g + 1) * 4 * PER, send_score, 0)
        return carry

    lax.fori_loop(0, GROUPS, expert, 0)
    count_sum(copies, 3, 1)
    copies = count_round(6, 7, 2)

    def in_copies(n, buf):
        rows = rows_of(n, 256)
        return (
            pltpu.make_async_copy(out_buf.at[buf, :, pl.ds(0, H)], gg_hbm.at[rows], oa_sem.at[buf, 0]),
            pltpu.make_async_copy(out_buf.at[buf, :, pl.ds(H, H)], gu_hbm.at[rows], oa_sem.at[buf, 1]),
        )

    def grad_in(n, carry):
        buf = n % 2

        @pl.when(n >= 2)
        def _():
            for copy in in_copies(n - 2, buf):
                copy.wait()

        turned = jnp.transpose(xs[:, rows_of(n, 256)])
        for part in (slice(0, H), slice(H, 2 * H)):
            out_buf[buf, :, part] = mm(turned, gu[:, part], NN).astype(BF16)
        for copy in in_copies(n, buf):
            copy.start()
        return carry

    lax.fori_loop(0, D // 256, grad_in, 0)
    for n in (D // 256 - 2, D // 256 - 1):
        for copy in in_copies(n, n % 2):
            copy.wait()

    for a in range(AXES):
        await_group(0, pr[a], pr_sem, a, Q_PAIR[a])
        unpack(pr[a], 0, Q_PAIR[a], xs, 0, COLS_PAIR[a].start)
    for a in range(AXES):
        q = Q_PAIR[a]
        await_group(1, pr[a], pr_sem, a, q)
        unpack(pr[a], 1, q, xs, 1, COLS_PAIR[a].start)
        home = PAIR_HOME[a]
        await_bytes(tt[home].at[pl.ds(T, 3 * T)], gt_s.at[home])
        for c in range(0, q, 4):
            lanes, cols = slice(c * 128, (c + 4) * 128), pl.ds(COLS_PAIR[a].start + c * 128, 512)
            fs[a][:, lanes] = mm(hot[a][...], xs[:, cols], TN).astype(BF16)
            for s in (2, 1, 3):
                home = fr[a].at[pl.ds((s - 1) * T, T), lanes]
                remote(fs[a].at[pl.ds(s * T, T), lanes], home, fs_sem.at[a], fr_sem.at[a], along(a, s, -1))

    def down_copy(n, buf):
        place = gd_hbm.at[rows_of(n // 2, 256), rows_of(n % 2, D // 2)]
        return pltpu.make_async_copy(out_buf.at[buf, :, pl.ds(0, D // 2)], place, od_sem.at[buf])

    def grad_out(n, carry):
        buf = n % 2

        @pl.when(n >= 2)
        def _():
            down_copy(n - 2, buf).wait()

        rows = mm(hid[:, rows_of(n // 2, 256)], cs[:, rows_of(n % 2, D // 2)], TN)
        out_buf[buf, :, 0 : D // 2] = rows.astype(BF16)
        down_copy(n, buf).start()
        return carry

    lax.fori_loop(0, H // 128, grad_out, 0)

    prob = jnp.exp(logit_ref[...] - jnp.max(logit_ref[...], axis=1, keepdims=True))
    prob = prob / jnp.sum(prob, axis=1, keepdims=True)
    count_sum(copies, 6, 2)
    load = cnt[24:32, :] * (E * MICRO / (K * T * E))
    batch_col = jnp.transpose((mb_ref[...] == iota((T, T), 0)).astype(F32))[:, 1:2]
    token_load = jnp.where(batch_col > 0.0, load[1:2, :], load[0:1, :])
    gb_ref[...] = prob * (token_load - jnp.sum(prob * token_load, axis=1, keepdims=True))

    await_bytes(qr.at[pl.ds(1, E - 1)], qr_sem)
    q_all = jnp.concatenate([qr[i] for i in range(E)], axis=0)
    q_rel = jnp.zeros((E, T), F32)
    for s in range(CAP):
        q_rel = jnp.where(code_rel[...] == float(s + 1), q_all[:, s : s + 1], q_rel)
    q_own = mm(q_rel.astype(BF16), perm_ref[...], TN)
    gl_ref[...] = q_own - rwm_ref[...] * jnp.sum(q_own, axis=1, keepdims=True)

    for a in range(AXES):
        await_bytes(fr[a], fr_sem.at[a])
        total = fs[a][0:T, :].astype(F32)
        for s in range(LINE - 1):
            total = total + fr[a][s * T : (s + 1) * T, :].astype(F32)
        gt_ref[:, COLS_PAIR[a]] = total.astype(BF16)

    for n in (H // 128 - 2, H // 128 - 1):
        down_copy(n, n % 2).wait()
    for a in range(AXES):
        await_bytes(tc[a].at[pl.ds(T, 3 * T)], gc_s.at[a])
        await_bytes(cw.at[a, pl.ds(64, 192)], gw_s.at[a])
        await_bytes(fr[a], fs_sem.at[a])
        for g in range(GROUPS):
            await_group(g, sc[a], sc_sem, a, Q_COT[a])
            await_group(g, ps[a], ps_sem, a, Q_PAIR[a])
    await_bytes(qs.at[pl.ds(1, E - 1)], qs_sem)


def settle_kernel(*refs):
    sources, targets, sem, held = refs[:6], refs[6:12], refs[12], refs[13:]
    copies = []
    for src, dst, buf in zip(sources, targets, held):
        pieces = 8 if src.shape[0] > T else 1
        size = src.shape[0] // pieces
        for n in range(pieces):
            rows = pl.ds(n * size, size)
            m = len(copies)
            copies.append(
                (
                    pltpu.make_async_copy(src.at[rows], buf.at[rows], sem.at[0, m]),
                    pltpu.make_async_copy(buf.at[rows], dst.at[rows], sem.at[1, m]),
                )
            )
    for fetch, _ in copies:
        fetch.start()
    for fetch, store in copies:
        fetch.wait()
        store.start()
    for _, store in copies:
        store.wait()


def settle(outs):
    hbm = pl.BlockSpec(memory_space=pl.ANY)
    return pl.pallas_call(
        settle_kernel,
        out_shape=tuple(jax.ShapeDtypeStruct(o.shape, o.dtype) for o in outs),
        in_specs=[hbm] * 6,
        out_specs=(hbm,) * 6,
        scratch_shapes=[pltpu.SemaphoreType.DMA((2, 27))] + [pltpu.VMEM(o.shape, o.dtype) for o in outs],
        compiler_params=pltpu.CompilerParams(vmem_limit_bytes=60 * 2**20),
        name="settle",
    )(*outs)


def per_device(tokens, out_grad, router_logits, expert_picks, micro_batch, w_gate, w_up, w_down):
    vmem, hbm = pl.BlockSpec(memory_space=pltpu.VMEM), pl.BlockSpec(memory_space=pl.ANY)
    dma = pltpu.SemaphoreType.DMA

    def sliced(rows, chunks):
        return [pltpu.VMEM((rows * q, 128), BF16) for q in chunks]

    outs = pl.pallas_call(
        kernel,
        out_shape=(
            jax.ShapeDtypeStruct((T, D), BF16),
            jax.ShapeDtypeStruct((T, E), F32),
            jax.ShapeDtypeStruct((T, E), F32),
            jax.ShapeDtypeStruct((D, H), BF16),
            jax.ShapeDtypeStruct((D, H), BF16),
            jax.ShapeDtypeStruct((H, D), BF16),
        ),
        in_specs=[hbm] * 2 + [vmem] * 3 + [hbm] * 3,
        out_specs=(vmem,) * 3 + (hbm,) * 3,
        scratch_shapes=[
            *sliced(PAIRS, Q_TOK), *sliced(PAIRS, Q_COT),
            *sliced(PAIRS, Q_TOK), *sliced(PAIRS, Q_COT), *sliced(PAIRS, Q_PAIR),
            *[pltpu.VMEM((LINE * T, q * 128), BF16) for q in Q_TOK],
            *[pltpu.VMEM((LINE * T, q * 128), BF16) for q in Q_COT],
            *[pltpu.VMEM((PAIRS, LINE * T), BF16)] * AXES,
            *[pltpu.VMEM((3 * T, q * 128), BF16) for q in Q_PAIR],
            pltpu.VMEM((SHEET, SHEET), BF16), pltpu.VMEM((ROWS, ROWS), BF16),
            *[pltpu.VMEM((PAIRS, D), BF16)] * 2,
            pltpu.VMEM((PAIRS, H), BF16),
            pltpu.VMEM((PAIRS, 2 * H), BF16),
            pltpu.VMEM((D, H), BF16),
            pltpu.VMEM((D, H), BF16),
            pltpu.VMEM((H, D), BF16),
            pltpu.VMEM((ROWS, 1024), BF16),
            pltpu.VMEM((2, 256, 2 * H), BF16),
            pltpu.VMEM((AXES, 256, T), BF16),
            pltpu.VMEM((AXES, 256, T), BF16),
            pltpu.VMEM((E, T), F32),
            pltpu.VMEM((E, E), BF16),
            pltpu.VMEM((T, E), F32),
            pltpu.VMEM((E, 1, 128), F32),
            pltpu.VMEM((E, 1, 128), F32),
            pltpu.VMEM((32, E), F32),
            pltpu.VMEM((13 * 8, E), F32),
            dma((3,)),
            dma((2, AXES)),
            dma((AXES,)), dma((AXES, LINE)), dma((AXES,)), dma((AXES, LINE)), dma((AXES,)), dma((AXES,)),
            *[dma((GROUPS, AXES))] * 6,
            *[dma((AXES,))] * 2,
            dma, dma, dma((13,)), dma((13,)), dma((2, 2)), dma((2,)),
        ],
        compiler_params=pltpu.CompilerParams(
            collective_id=0, has_side_effects=True, vmem_limit_bytes=64 * 2**20
        ),
        name="expert_backward",
    )(tokens, out_grad, router_logits, expert_picks.T, micro_batch.reshape(1, T), w_gate[0], w_up[0], w_down[0])
    grad_tokens, grad_logits, balance_grad, grad_gate, grad_up, grad_down = settle(outs)
    return grad_tokens, grad_logits, balance_grad, grad_gate[None], grad_up[None], grad_down[None]


def solution(mesh):
    rows, cube = P(("dp", "ex", "ey"), None), P(("dp", "ex", "ey"), None, None)
    return jax.shard_map(
        per_device,
        mesh=mesh,
        in_specs=(rows, rows, rows, rows, P(("dp", "ex", "ey")), cube, cube, cube),
        out_specs=(rows, rows, rows, cube, cube, cube),
        check_vma=False,
    )
```

```python
import jax
import jax.numpy as jnp
from jax import lax
from jax.experimental import pallas as pl
from jax.experimental.pallas import tpu as pltpu
from jax.sharding import PartitionSpec as P

MESH = pl.DeviceIdType.MESH
F32, BF16, I32 = jnp.float32, jnp.bfloat16, jnp.int32
NN = (((1,), (0,)), ((), ()))
NT = (((1,), (1,)), ((), ()))
TN = (((0,), (0,)), ((), ()))

D, H, K, T, E, CAP, MICRO = 2048, 768, 8, 128, 128, 9, 2
AXES = 3
LINE = 4
PLANE = E // LINE
GROUPS = 2
PER = PLANE // GROUPS
MSG = LINE * CAP
ROWS = PER * MSG
PAIRS = E * CAP
HALF = ROWS // 2
SHEET = LINE * MSG
BLK = 32
Q_TOK, Q_COT, Q_PAIR = (4, 4, 8), (4, 8, 4), (8, 4, 4)


def slices(chunks):
    starts = [sum(chunks[:a]) * 128 for a in range(AXES)]
    return [slice(s, s + q * 128) for s, q in zip(starts, chunks)]


COLS_TOK, COLS_COT, COLS_PAIR = slices(Q_TOK), slices(Q_COT), slices(Q_PAIR)
PAIR_HOME = (2, 1, 0)


def mm(a, b, dims):
    return lax.dot_general(a, b, dims, preferred_element_type=F32)


def rows_of(g, size):
    return pl.ds(pl.multiple_of(g * size, size), size)


def iota(shape, dim):
    return lax.broadcasted_iota(I32, shape, dim)


def rem(value, size):
    return lax.rem(value, jnp.int32(size)) if isinstance(value, jax.Array) else value % size


def quot(value, size):
    return lax.div(value, jnp.int32(size)) if isinstance(value, jax.Array) else value // size


def moved(steps, dc, sign=1):
    x, ex, y = lax.axis_index("dp"), lax.axis_index("ex"), lax.axis_index("ey")
    z, core = quot(ex, 2), rem(ex, 2)
    side = core if sign == 1 else rem(core + dc, 2)
    dx, dy, dz = axes_of(steps, side)
    if sign == -1:
        dx, dy, dz = 4 - dx, 4 - dy, 4 - dz
    return rem(x + dx, 4), rem(z + dz, 4) * 2 + rem(core + dc, 2), rem(y + dy, 4)


def axes_of(steps, side):
    a, b, c = steps
    return a + side * (c - a), b + side * (a - b), c + side * (b - c)


def along(axis, step, sign=1):
    return moved([step if axis == n else 0 for n in range(AXES)], 0, sign)


def in_plane(axis, j, sign=1):
    core, high, low = quot(j, 16), rem(quot(j, 4), 4), rem(j, 4)
    return moved(((0, low, high), (low, 0, high), (low, high, 0))[axis], core, sign)


def any_offset(i, sign=1):
    return moved((rem(i, 4), rem(quot(i, 4), 4), rem(quot(i, 16), 4)), quot(i, 64), sign)


def turn(n):
    return rem(rem(n, 4) + quot(n, 4), 4) * 4 + rem(n, 4)


def expert_at(steps, dc):
    x, ex, y = lax.axis_index("dp"), lax.axis_index("ex"), lax.axis_index("ey")
    dx, dy, dz = axes_of(steps, ex % 2)
    return ((x + dx) & 3) * 32 + ((((ex // 2) + dz) & 3) * 2 + (((ex % 2) + dc) & 1)) * 4 + ((y + dy) & 3)


def kernel(
    tok_hbm, cot_hbm, logit_ref, pick_ref, mb_ref, wg_hbm, wu_hbm, wd_hbm,
    gt_ref, gl_ref, gb_ref, gg_hbm, gu_hbm, gd_hbm,
    st0, st1, st2, sc0, sc1, sc2, rt0, rt1, rt2, rc0, rc1, rc2, pr0, pr1, pr2,
    tt0, tt1, tt2, tc0, tc1, tc2, hot0, hot1, hot2, fr0, fr1, fr2, perm_y, perm_z,
    xs, cs, hid, gu, wg, wu, wd, pg, out_buf, cw, cwg, code_rel, perm_ref, rwm_ref, qs, qr, cnt, cnt_in,
    w_sem, own_sem, gt_s, gt_r, gh_r, gc_s, gc_r, gw_s, gw_r, st_sem, sc_sem, rt_sem, rc_sem, ps_sem, pr_sem, fs_sem, fr_sem,
    qs_sem, qr_sem, cs_sem, cr_sem, oa_sem, od_sem,
):
    x, ex, y = lax.axis_index("dp"), lax.axis_index("ex"), lax.axis_index("ey")
    st, sc, rt, rc, pr = (st0, st1, st2), (sc0, sc1, sc2), (rt0, rt1, rt2), (rc0, rc1, rc2), (pr0, pr1, pr2)
    tt, tc, hot, fr = (tt0, tt1, tt2), (tc0, tc1, tc2), (hot0, hot1, hot2), (fr0, fr1, fr2)
    ps = tuple(st[n] for n in PAIR_HOME)
    fs = tuple(tt[n] for n in PAIR_HOME)
    barrier = pltpu.get_barrier_semaphore()

    ys = [rem(y + n, 4) for n in range(4)]
    exs = [rem(quot(ex, 2) + n, 4) * 2 + c for n in range(4) for c in (rem(ex, 2), rem(ex + 1, 2))]

    def greet(n, carry):
        to_x = rem(x + n, 4)
        for m in range(1, 32):
            to = (to_x, exs[m // 4], ys[m % 4])
            pl.semaphore_signal(barrier, inc=1, device_id=to, device_id_type=MESH)
        return carry

    lax.fori_loop(0, 4, greet, 0)
    for n in range(1, 4):
        pl.semaphore_signal(barrier, inc=1, device_id=(rem(x + n, 4), ex, y), device_id_type=MESH)
    loads = [
        pltpu.make_async_copy(src, dst, w_sem.at[n])
        for n, (src, dst) in enumerate(((wg_hbm, wg), (wu_hbm, wu), (wd_hbm, wd)))
    ]
    own = []
    for a in range(AXES):
        own.append(pltpu.make_async_copy(tok_hbm.at[:, COLS_TOK[a]], tt[a].at[pl.ds(0, T)], own_sem.at[0, a]))
        own.append(pltpu.make_async_copy(cot_hbm.at[:, COLS_COT[a]], tc[a].at[pl.ds(0, T)], own_sem.at[1, a]))
    for load in own:
        load.start()

    def remote(src, dst, send_sem, recv_sem, to):
        pltpu.make_async_remote_copy(
            src_ref=src, dst_ref=dst, send_sem=send_sem, recv_sem=recv_sem, device_id=to, device_id_type=MESH
        ).start()

    def await_bytes(piece, sem):
        pltpu.make_async_copy(piece, piece, sem).wait()

    pl.semaphore_wait(barrier, E - 1)
    for first in (True, False):
        for s in (1, 3):
            for a in range(AXES):
                width = Q_TOK[a] * 64
                begin = width if (s == 3) == first else 0
                block = tok_hbm.at[:, pl.ds(COLS_TOK[a].start + begin, width)]
                home = tt[a].at[pl.ds(s * T, T), pl.ds(begin, width)]
                remote(block, home, gt_s.at[a], (gt_r if first else gh_r).at[a, s], along(a, s))

    expert_row = iota((E, T), 0)
    picked_t = jnp.zeros((E, T), F32)
    for k in range(K):
        picked_t = jnp.where(pick_ref[k : k + 1, :] == expert_row, 1.0, picked_t)
    picked = jnp.transpose(picked_t)
    logits = logit_ref[...]
    top = jnp.max(jnp.where(picked > 0.0, logits, -jnp.inf), axis=1, keepdims=True)
    rwm = jnp.where(picked > 0.0, jnp.exp(jnp.minimum(logits - top, 0.0)), 0.0)
    rwm = rwm / jnp.sum(rwm, axis=1, keepdims=True)
    rwm_ref[...] = rwm
    weight = rwm.astype(BF16)
    earlier = (iota((T, T), 1) < iota((T, T), 0)).astype(BF16)
    code = jnp.where(picked > 0.0, mm(earlier, picked.astype(BF16), NN) + 1.0, 0.0).astype(BF16)
    row, lane = iota((E, E), 0), iota((E, E), 1)
    perm = (expert_at((row & 3, (row >> 2) & 3, (row >> 4) & 3), row >> 6) == lane).astype(BF16)
    perm_ref[...] = perm
    code_rel[...] = mm(perm, code, NT)
    step, core, high, low = row >> 5, (row >> 4) & 1, (row >> 2) & 3, row & 3
    for a in range(AXES):
        place = ((step, low, high), (low, step, high), (low, high, step))[a]
        perm = (expert_at(place, core) == lane).astype(BF16)
        code_a, weight_a = mm(perm, code, NT).astype(BF16), mm(perm, weight, NT).astype(BF16)
        for s in range(LINE):
            home = cw if s else cwg
            home[a, s * 64 : s * 64 + 32, :] = code_a[s * 32 : s * 32 + 32, :]
            home[a, s * 64 + 32 : s * 64 + 64, :] = weight_a[s * 32 : s * 32 + 32, :]
    mb_hot = (mb_ref[...] == iota((8, T), 0)).astype(BF16)
    cnt[0:8, :] = mm(mb_hot, picked.astype(BF16), NN)
    for s in (1, 3, 2):
        for a in range(AXES):
            piece = pl.ds(s * 64, 64)
            remote(cw.at[a, piece], cwg.at[a, piece], gw_s.at[a], gw_r.at[a], along(a, s))
    for s in (1, 3):
        for a in range(AXES):
            home = tc[a].at[pl.ds(s * T, T)]
            remote(cot_hbm.at[:, COLS_COT[a]], home, gc_s.at[a], gc_r.at[a, s], along(a, s))

    def pass_on(held, send_sem, recv_sem, chunks, halves=False):
        for s, begin in ((1, 0), (3, 1)):
            for a in range(AXES):
                lanes = pl.ds(begin * chunks[a] * 64, chunks[a] * 64)
                whole = held[a].at[pl.ds(s * T, T)]
                await_bytes(held[a].at[pl.ds(s * T, T), lanes] if halves else whole, recv_sem.at[a, s])
                block, home = held[a].at[pl.ds(s * T, T), lanes], held[a].at[pl.ds(2 * T, T), lanes]
                remote(block, home, send_sem.at[a], recv_sem.at[a, 2], along(a, s))

    for load in loads:
        load.start()

    def count_round(base, others, stage):
        copies = []
        for n in range(others):
            to = (
                ((x + n + 1) % 4, ex, y),
                (x, ex, (y + n + 1) % 4),
                (x, (ex + n + 1) % 8, y),
            )[stage]
            copies.append(
                pltpu.make_async_remote_copy(
                    src_ref=cnt.at[pl.ds(stage * 8, 8)],
                    dst_ref=cnt_in.at[pl.ds((base + n) * 8, 8)],
                    send_sem=cs_sem.at[base + n],
                    recv_sem=cr_sem.at[base + n],
                    device_id=to,
                    device_id_type=MESH,
                )
            )
        for copy in copies:
            copy.start()
        return copies

    def count_sum(copies, base, stage):
        total = cnt[stage * 8 : stage * 8 + 8, :]
        for n, copy in enumerate(copies):
            copy.wait()
            total = total + cnt_in[(base + n) * 8 : (base + n) * 8 + 8, :]
        cnt[stage * 8 + 8 : stage * 8 + 16, :] = total

    copies = count_round(0, 3, 0)

    for load in own:
        load.wait()

    def pack(out, g, q, begin=0, end=ROWS // BLK):
        def block(n, carry):
            tile = pg[rows_of(n, BLK), 0 : q * 128].reshape(BLK, q, 128)
            out[rows_of(g * (ROWS // BLK) + n, BLK * q), :] = tile.reshape(BLK * q, 128)
            return carry

        lax.fori_loop(begin, end, block, 0)

    def unpack(src, g, q, out, out_g, first=0):
        def block(n, carry):
            tile = src[rows_of(g * (ROWS // BLK) + n, BLK * q), :].reshape(BLK, q, 128)
            out[rows_of(out_g * (ROWS // BLK) + n, BLK), first : first + q * 128] = tile.reshape(BLK, q * 128)
            return carry

        lax.fori_loop(0, ROWS // BLK, block, 0)

    def own_message(g, src, dst, q):
        @pl.when(g == 0)
        def _():
            dst[0 : MSG * q, :] = src[0 : MSG * q, :]

    def send_groups(parts, sign):
        def send(n, carry):
            for g, a, src, dst, s_sem, r_sem, q in parts:
                j = g * PER + turn(n)
                piece = rows_of(j, MSG * q)
                remote(src.at[piece], dst.at[piece], s_sem.at[g, a], r_sem.at[g, a], in_plane(a, j, sign))
            return carry

        lax.fori_loop(1, PER, send, 0, unroll=5)
        for g, a, src, dst, s_sem, r_sem, q in parts:
            if g:
                piece = pl.ds(g * ROWS * q, MSG * q)
                to = in_plane(a, g * PER, sign)
                remote(src.at[piece], dst.at[piece], s_sem.at[g, a], r_sem.at[g, a], to)

    def await_group(g, buf, sem, a, q):
        @pl.when(g == 0)
        def _():
            await_bytes(buf.at[pl.ds(MSG * q, (PER - 1) * MSG * q)], sem.at[0, a])

        @pl.when(g > 0)
        def _():
            await_bytes(buf.at[rows_of(g, ROWS * q)], sem.at[g, a])

    slot = (iota((ROWS, T), 0) % CAP + 1).astype(F32)

    def pick_rows(a, g, s):
        pair, j = iota((ROWS, PER), 0), iota((ROWS, PER), 1)
        return jnp.logical_and(pair // MSG == j, pair // CAP % LINE == s).astype(BF16)

    def fill(one_hot, table, q):
        def half(n, carry):
            for c in range(0, q, 4):
                lanes = slice(c * 128, (c + 4) * 128)
                pg[rows_of(n, HALF), lanes] = mm(one_hot(n), table[:, lanes], NN).astype(BF16)
            return carry

        lax.fori_loop(0, 2, half, 0)

    def find_rows(g):
        for a in range(AXES):
            if g == 0:
                await_bytes(cwg.at[a, pl.ds(64, 192)], gw_r.at[a])
            for s in range(LINE):
                found = mm(pick_rows(a, g, s), cwg[a, pl.ds(s * 64 + g * PER, PER), :], NN)
                hot[a][g * ROWS : (g + 1) * ROWS, s * T : (s + 1) * T] = (found == slot).astype(BF16)

    def token_rows(g):
        for a in range(AXES):
            if g == 0:
                await_bytes(tt[a].at[pl.ds(2 * T, T)], gt_r.at[a, 2])
                for s, begin in ((1, Q_TOK[a] * 64), (3, 0)):
                    await_bytes(tt[a].at[pl.ds(s * T, T), pl.ds(begin, Q_TOK[a] * 64)], gh_r.at[a, s])
            fill(lambda n: hot[a][rows_of(2 * g + n, HALF), :], tt[a], Q_TOK[a])
            pack(st[a], g, Q_TOK[a])
            own_message(g, st[a], rt[a], Q_TOK[a])
            yield g, a, st[a], rt[a], st_sem, rt_sem, Q_TOK[a]

    def cotangent_rows(g):
        for a in range(AXES):
            for s in range(LINE):
                lanes = slice(s * T, (s + 1) * T)
                scale = mm(pick_rows(a, g, s), cwg[a, pl.ds(s * 64 + 32 + g * PER, PER), :], NN)
                one_hot = hot[a][g * ROWS : (g + 1) * ROWS, lanes].astype(F32)
                xs[0:ROWS, lanes] = (one_hot * scale).astype(BF16)
            if g == 0:
                await_bytes(tc[a].at[pl.ds(2 * T, T)], gc_r.at[a, 2])
            fill(lambda n: xs[rows_of(n, HALF), 0 : LINE * T], tc[a], Q_COT[a])
            pack(sc[a], g, Q_COT[a])
            own_message(g, sc[a], rc[a], Q_COT[a])
        return [(g, a, sc[a], rc[a], sc_sem, rc_sem, Q_COT[a]) for a in range(AXES)]

    pass_on(tt, gt_s, gt_r, Q_TOK, True)
    find_rows(0)
    pass_on(tc, gc_s, gc_r, Q_COT)
    for part in token_rows(0):
        send_groups([part], 1)
    send_groups(cotangent_rows(0), 1)
    find_rows(1)
    send_groups(list(token_rows(1)), 1)
    send_groups(cotangent_rows(1), 1)

    def order_block(n, carry):
        pair = iota((64, 1), 0) + n * 64
        s_, x_, y_, z_ = pair % CAP, pair // 9 % 4, pair // 36 % 4, pair // 144
        perm_z[rows_of(n, 64), :] = (((y_ * 4 + x_) * 4 + z_) * CAP + s_ == iota((64, ROWS), 1)).astype(BF16)
        return carry

    lax.fori_loop(0, ROWS // 64, order_block, 0)
    pair = iota((SHEET, 1), 0)
    perm_y[...] = ((pair // 9 % 4 * 4 + pair // 36) * CAP + pair % CAP == iota((SHEET, SHEET), 1)).astype(BF16)
    count_sum(copies, 0, 0)
    copies = count_round(3, 3, 1)
    for load in loads:
        load.wait()

    def reorder(a, src, src_col, dst, dst_rows, dst_col, q, dims):
        for c in range(0, q * 128, 256):
            rows, lanes = src(slice(src_col + c, src_col + c + 256)), slice(dst_col + c, dst_col + c + 256)
            if a == 1:
                sheets = [rows[n * SHEET : (n + 1) * SHEET, :] for n in range(ROWS // SHEET)]
                rows = jnp.concatenate([mm(perm_y[...], sheet, dims).astype(BF16) for sheet in sheets], axis=0)
            elif a == 2:
                rows = mm(perm_z[...], rows, dims).astype(BF16)
            dst[dst_rows, lanes] = rows

    collect = (iota((2 * PER, HALF), 1) // CAP == iota((2 * PER, HALF), 0)).astype(BF16)
    slot_lane = (iota((HALF, 128), 0) % CAP == iota((HALF, 128), 1)).astype(F32)

    def arrive(g, out, src, sem, chunks, cols):
        for a in range(AXES):
            await_group(g, src[a], sem, a, chunks[a])
            unpack(src[a], g, chunks[a], pg, 0)
            reorder(a, lambda lanes: pg[:, lanes], 0, out, rows_of(g, ROWS), cols[a].start, chunks[a], NN)

    def send_score(i, carry):
        remote(qs.at[pl.ds(i, 1)], qr.at[pl.ds(i, 1)], qs_sem, qr_sem, any_offset(i, -1))
        return carry

    def send_last(g):
        def send(n, carry):
            j = g * PER + turn(n)
            piece = rows_of(j, MSG * Q_PAIR[2])
            remote(ps[2].at[piece], pr[2].at[piece], ps_sem.at[g, 2], pr_sem.at[g, 2], in_plane(2, j, -1))
            return carry

        lax.fori_loop(1, PER, send, 0, unroll=5)
        if g:
            send(0, 0)

    def expert(g, carry):
        arrive(g, xs, rt, rt_sem, Q_TOK, COLS_TOK)

        def forward(n, carry):
            part = rows_of(2 * g + n, HALF)
            for h in range(H // 256):
                cols = slice(h * 256, (h + 1) * 256)
                pre_gate = mm(xs[part, :], wg[:, cols], NN)
                pre_up = mm(xs[part, :], wu[:, cols], NN)
                logistic = jax.nn.sigmoid(pre_gate)
                act = pre_gate * logistic
                deriv = logistic * (1.0 + pre_gate * (1.0 - logistic))
                hid[part, cols] = (act * pre_up).astype(BF16)
                gu[part, cols] = (pre_up * deriv).astype(BF16)
                gu[part, h * 256 + H : (h + 1) * 256 + H] = act.astype(BF16)
            return carry

        lax.fori_loop(0, 2, forward, 0)

        @pl.when(g == 1)
        def _():
            send_last(0)

        arrive(g, cs, rc, rc_sem, Q_COT, COLS_COT)
        for a in range(AXES):
            await_group(g, st[PAIR_HOME[a]], st_sem, PAIR_HOME[a], Q_PAIR[a])

        def pair_rows(part, lanes):
            rows = mm(gu[part, 0:H], wg[lanes, :], NT) + mm(gu[part, H : 2 * H], wu[lanes, :], NT)
            return rows.astype(BF16)

        def send_pair(a, j):
            piece = rows_of(j, MSG * Q_PAIR[a])
            remote(ps[a].at[piece], pr[a].at[piece], ps_sem.at[g, a], pr_sem.at[g, a], in_plane(a, j, -1))

        def backward(n, carry):
            part = rows_of(2 * g + n, HALF)
            score = jnp.zeros((HALF, 1), F32)
            for h in range(H // 256):
                cols, more = slice(h * 256, (h + 1) * 256), slice(h * 256 + H, (h + 1) * 256 + H)
                back = mm(cs[part, :], wd[cols, :], NT)
                score = score + jnp.sum(hid[part, cols].astype(F32) * back, axis=1, keepdims=True)
                gu[part, cols] = (back * gu[part, cols].astype(F32)).astype(BF16)
                gu[part, more] = (back * gu[part, more].astype(F32)).astype(BF16)
            for a in (1, 0):
                q, first = Q_PAIR[a], COLS_PAIR[a].start
                for c in range(0, q * 128, 256):
                    rows = pair_rows(part, slice(first + c, first + c + 256))
                    if a == 1:
                        sheets = [rows[m * SHEET : (m + 1) * SHEET, :] for m in range(HALF // SHEET)]
                        sheets = [mm(perm_y[...], sheet, TN).astype(BF16) for sheet in sheets]
                        rows = jnp.concatenate(sheets, axis=0)
                    pg[rows_of(n, HALF), c : c + 256] = rows
                pack(ps[a], g, q, n * (HALF // BLK), (n + 1) * (HALF // BLK))

                @pl.when(g + n == 0)
                def _():
                    pr[a][0 : MSG * q, :] = ps[a][0 : MSG * q, :]

                def send(m, carry):
                    low = rem(m, 4)
                    send_pair(a, g * PER + (2 * n + rem(low + quot(m, 4), 2)) * 4 + low)
                    return carry

                pl.when(g + n > 0)(lambda: send(0, None))
                lax.fori_loop(1, PER // 2, send, 0, unroll=True)
            score_rows = mm(collect, (score * slot_lane).astype(BF16), NN)
            for i in range(2 * PER):
                qs[(2 * g + n) * 2 * PER + i] = score_rows[i : i + 1, :]
            return carry

        lax.fori_loop(0, 2, backward, 0)
        part = rows_of(g, ROWS)
        first = COLS_PAIR[2].start
        reorder(2, lambda lanes: pair_rows(part, lanes), first, pg, slice(0, ROWS), 0, Q_PAIR[2], TN)
        pack(ps[2], g, Q_PAIR[2])
        own_message(g, ps[2], pr[2], Q_PAIR[2])

        @pl.when(g == 1)
        def _():
            send_last(1)

        @pl.when(g == 0)
        def _():
            qr[0] = qs[0]

        lax.fori_loop(jnp.where(g == 0, 1, g * 4 * PER), (g + 1) * 4 * PER, send_score, 0)
        return carry

    lax.fori_loop(0, GROUPS, expert, 0)
    count_sum(copies, 3, 1)
    copies = count_round(6, 7, 2)

    def in_copies(n, buf):
        rows = rows_of(n, 256)
        return (
            pltpu.make_async_copy(out_buf.at[buf, :, pl.ds(0, H)], gg_hbm.at[rows], oa_sem.at[buf, 0]),
            pltpu.make_async_copy(out_buf.at[buf, :, pl.ds(H, H)], gu_hbm.at[rows], oa_sem.at[buf, 1]),
        )

    def grad_in(n, carry):
        buf = n % 2

        @pl.when(n >= 2)
        def _():
            for copy in in_copies(n - 2, buf):
                copy.wait()

        turned = jnp.transpose(xs[:, rows_of(n, 256)])
        for part in (slice(0, H), slice(H, 2 * H)):
            out_buf[buf, :, part] = mm(turned, gu[:, part], NN).astype(BF16)
        for copy in in_copies(n, buf):
            copy.start()
        return carry

    lax.fori_loop(0, D // 256, grad_in, 0)
    for n in (D // 256 - 2, D // 256 - 1):
        for copy in in_copies(n, n % 2):
            copy.wait()

    for a in range(AXES):
        await_group(0, pr[a], pr_sem, a, Q_PAIR[a])
        unpack(pr[a], 0, Q_PAIR[a], xs, 0, COLS_PAIR[a].start)
    for a in range(AXES):
        q = Q_PAIR[a]
        await_group(1, pr[a], pr_sem, a, q)
        unpack(pr[a], 1, q, xs, 1, COLS_PAIR[a].start)
        home = PAIR_HOME[a]
        await_bytes(tt[home].at[pl.ds(T, 3 * T)], gt_s.at[home])
        for c in range(0, q, 4):
            lanes, cols = slice(c * 128, (c + 4) * 128), pl.ds(COLS_PAIR[a].start + c * 128, 512)
            fs[a][:, lanes] = mm(hot[a][...], xs[:, cols], TN).astype(BF16)
            for s in (2, 1, 3):
                home = fr[a].at[pl.ds((s - 1) * T, T), lanes]
                remote(fs[a].at[pl.ds(s * T, T), lanes], home, fs_sem.at[a], fr_sem.at[a], along(a, s, -1))

    def down_copy(n, buf):
        place = gd_hbm.at[rows_of(n // 2, 256), rows_of(n % 2, D // 2)]
        return pltpu.make_async_copy(out_buf.at[buf, :, pl.ds(0, D // 2)], place, od_sem.at[buf])

    def grad_out(n, carry):
        buf = n % 2

        @pl.when(n >= 2)
        def _():
            down_copy(n - 2, buf).wait()

        rows = mm(hid[:, rows_of(n // 2, 256)], cs[:, rows_of(n % 2, D // 2)], TN)
        out_buf[buf, :, 0 : D // 2] = rows.astype(BF16)
        down_copy(n, buf).start()
        return carry

    lax.fori_loop(0, H // 128, grad_out, 0)

    prob = jnp.exp(logit_ref[...] - jnp.max(logit_ref[...], axis=1, keepdims=True))
    prob = prob / jnp.sum(prob, axis=1, keepdims=True)
    count_sum(copies, 6, 2)
    load = cnt[24:32, :] * (E * MICRO / (K * T * E))
    batch_col = jnp.transpose((mb_ref[...] == iota((T, T), 0)).astype(F32))[:, 1:2]
    token_load = jnp.where(batch_col > 0.0, load[1:2, :], load[0:1, :])
    gb_ref[...] = prob * (token_load - jnp.sum(prob * token_load, axis=1, keepdims=True))

    await_bytes(qr.at[pl.ds(1, E - 1)], qr_sem)
    q_all = jnp.concatenate([qr[i] for i in range(E)], axis=0)
    q_rel = jnp.zeros((E, T), F32)
    for s in range(CAP):
        q_rel = jnp.where(code_rel[...] == float(s + 1), q_all[:, s : s + 1], q_rel)
    q_own = mm(q_rel.astype(BF16), perm_ref[...], TN)
    gl_ref[...] = q_own - rwm_ref[...] * jnp.sum(q_own, axis=1, keepdims=True)

    for a in range(AXES):
        await_bytes(fr[a], fr_sem.at[a])
        total = fs[a][0:T, :].astype(F32)
        for s in range(LINE - 1):
            total = total + fr[a][s * T : (s + 1) * T, :].astype(F32)
        gt_ref[:, COLS_PAIR[a]] = total.astype(BF16)

    for n in (H // 128 - 2, H // 128 - 1):
        down_copy(n, n % 2).wait()
    for a in range(AXES):
        await_bytes(tc[a].at[pl.ds(T, 3 * T)], gc_s.at[a])
        await_bytes(cw.at[a, pl.ds(64, 192)], gw_s.at[a])
        await_bytes(fr[a], fs_sem.at[a])
        for g in range(GROUPS):
            await_group(g, sc[a], sc_sem, a, Q_COT[a])
            await_group(g, ps[a], ps_sem, a, Q_PAIR[a])
    await_bytes(qs.at[pl.ds(1, E - 1)], qs_sem)


def settle_kernel(*refs):
    sources, targets, sem, held = refs[:6], refs[6:12], refs[12], refs[13:]
    copies = []
    for src, dst, buf in zip(sources, targets, held):
        pieces = 8 if src.shape[0] > T else 1
        size = src.shape[0] // pieces
        for n in range(pieces):
            rows = pl.ds(n * size, size)
            m = len(copies)
            copies.append(
                (
                    pltpu.make_async_copy(src.at[rows], buf.at[rows], sem.at[0, m]),
                    pltpu.make_async_copy(buf.at[rows], dst.at[rows], sem.at[1, m]),
                )
            )
    for fetch, _ in copies:
        fetch.start()
    for fetch, store in copies:
        fetch.wait()
        store.start()
    for _, store in copies:
        store.wait()


def settle(outs):
    hbm = pl.BlockSpec(memory_space=pl.ANY)
    return pl.pallas_call(
        settle_kernel,
        out_shape=tuple(jax.ShapeDtypeStruct(o.shape, o.dtype) for o in outs),
        in_specs=[hbm] * 6,
        out_specs=(hbm,) * 6,
        scratch_shapes=[pltpu.SemaphoreType.DMA((2, 27))] + [pltpu.VMEM(o.shape, o.dtype) for o in outs],
        compiler_params=pltpu.CompilerParams(vmem_limit_bytes=60 * 2**20),
        name="settle",
    )(*outs)


def per_device(tokens, out_grad, router_logits, expert_picks, micro_batch, w_gate, w_up, w_down):
    vmem, hbm = pl.BlockSpec(memory_space=pltpu.VMEM), pl.BlockSpec(memory_space=pl.ANY)
    dma = pltpu.SemaphoreType.DMA

    def sliced(rows, chunks):
        return [pltpu.VMEM((rows * q, 128), BF16) for q in chunks]

    outs = pl.pallas_call(
        kernel,
        out_shape=(
            jax.ShapeDtypeStruct((T, D), BF16),
            jax.ShapeDtypeStruct((T, E), F32),
            jax.ShapeDtypeStruct((T, E), F32),
            jax.ShapeDtypeStruct((D, H), BF16),
            jax.ShapeDtypeStruct((D, H), BF16),
            jax.ShapeDtypeStruct((H, D), BF16),
        ),
        in_specs=[hbm] * 2 + [vmem] * 3 + [hbm] * 3,
        out_specs=(vmem,) * 3 + (hbm,) * 3,
        scratch_shapes=[
            *sliced(PAIRS, Q_TOK), *sliced(PAIRS, Q_COT),
            *sliced(PAIRS, Q_TOK), *sliced(PAIRS, Q_COT), *sliced(PAIRS, Q_PAIR),
            *[pltpu.VMEM((LINE * T, q * 128), BF16) for q in Q_TOK],
            *[pltpu.VMEM((LINE * T, q * 128), BF16) for q in Q_COT],
            *[pltpu.VMEM((PAIRS, LINE * T), BF16)] * AXES,
            *[pltpu.VMEM((3 * T, q * 128), BF16) for q in Q_PAIR],
            pltpu.VMEM((SHEET, SHEET), BF16), pltpu.VMEM((ROWS, ROWS), BF16),
            *[pltpu.VMEM((PAIRS, D), BF16)] * 2,
            pltpu.VMEM((PAIRS, H), BF16),
            pltpu.VMEM((PAIRS, 2 * H), BF16),
            pltpu.VMEM((D, H), BF16),
            pltpu.VMEM((D, H), BF16),
            pltpu.VMEM((H, D), BF16),
            pltpu.VMEM((ROWS, 1024), BF16),
            pltpu.VMEM((2, 256, 2 * H), BF16),
            pltpu.VMEM((AXES, 256, T), BF16),
            pltpu.VMEM((AXES, 256, T), BF16),
            pltpu.VMEM((E, T), F32),
            pltpu.VMEM((E, E), BF16),
            pltpu.VMEM((T, E), F32),
            pltpu.VMEM((E, 1, 128), F32),
            pltpu.VMEM((E, 1, 128), F32),
            pltpu.VMEM((32, E), F32),
            pltpu.VMEM((13 * 8, E), F32),
            dma((3,)),
            dma((2, AXES)),
            dma((AXES,)), dma((AXES, LINE)), dma((AXES, LINE)), dma((AXES,)), dma((AXES, LINE)), dma((AXES,)), dma((AXES,)),
            *[dma((GROUPS, AXES))] * 6,
            *[dma((AXES,))] * 2,
            dma, dma, dma((13,)), dma((13,)), dma((2, 2)), dma((2,)),
        ],
        compiler_params=pltpu.CompilerParams(
            collective_id=0, has_side_effects=True, vmem_limit_bytes=64 * 2**20
        ),
        name="expert_backward",
    )(tokens, out_grad, router_logits, expert_picks.T, micro_batch.reshape(1, T), w_gate[0], w_up[0], w_down[0])
    grad_tokens, grad_logits, balance_grad, grad_gate, grad_up, grad_down = settle(outs)
    return grad_tokens, grad_logits, balance_grad, grad_gate[None], grad_up[None], grad_down[None]


def solution(mesh):
    rows, cube = P(("dp", "ex", "ey"), None), P(("dp", "ex", "ey"), None, None)
    return jax.shard_map(
        per_device,
        mesh=mesh,
        in_specs=(rows, rows, rows, rows, P(("dp", "ex", "ey")), cube, cube, cube),
        out_specs=(rows, rows, rows, cube, cube, cube),
        check_vma=False,
    )
```
